32 devices in a mesh: seq: 4 (over y, x), dp: 8 (over z, core).
Axes of the slice: x: 2, y: 2, z: 4, core: 2. Of those that a mesh axis runs over, the one named last changes fastest.
Arguments:
- frames: bfloat16 [8, 1024, 1024], P('dp', 'seq'), may hold values from -6 to 6
- segment_ids: int32 [8, 1024], P('dp'), may hold values from 0 to 1, never falling along the last dimension, each value on 1 to 1000 neighbouring positions
- span_starts: int32 [8, 40], P('dp'), may hold values from 0 to 1014
- cotangent: bfloat16 [8, 1024, 1024], P('dp', 'seq'), may hold values from -6 to 6
- attn_master: float32 [1024, 4096], P('seq', 'dp')
- attn_first: float32 [1024, 4096], P('seq', 'dp'), may hold values from -0.00048828125 to 0.00048828125
- attn_second: float32 [1024, 4096], P('seq', 'dp'), may hold values from 3.973643e-11 to 6.3578287e-10
- ffn_master: float32 [4096, 2048], P('seq', 'dp')
- ffn_first: float32 [4096, 2048], P('seq', 'dp'), may hold values from -0.00048828125 to 0.00048828125
- ffn_second: float32 [4096, 2048], P('seq', 'dp'), may hold values from 3.973643e-11 to 6.3578287e-10
- vec_master: float32 [13, 1024], replicated
- vec_first: float32 [13, 1024], replicated, may hold values from -0.00048828125 to 0.00048828125
- vec_second: float32 [13, 1024], replicated, may hold values from 3.973643e-11 to 6.3578287e-10
Outputs:
- output: bfloat16 [8, 1024, 1024], P('dp', 'seq')
- frames_grad: float32 [8, 1024, 1024], P('dp', 'seq')
- grad_norm: float32 [], replicated
- attn_master_new: float32 [1024, 4096], P('seq', 'dp')
- attn_first_new: float32 [1024, 4096], P('seq', 'dp')
- attn_second_new: float32 [1024, 4096], P('seq', 'dp')
- attn_copy: bfloat16 [1024, 4096], P('seq', 'dp')
- ffn_master_new: float32 [4096, 2048], P('seq', 'dp')
- ffn_first_new: float32 [4096, 2048], P('seq', 'dp')
- ffn_second_new: float32 [4096, 2048], P('seq', 'dp')
- ffn_copy: bfloat16 [4096, 2048], P('seq', 'dp')
- vec_master_new: float32 [13, 1024], replicated
- vec_first_new: float32 [13, 1024], replicated
- vec_second_new: float32 [13, 1024], replicated
The draws below stay inside these ranges and needn't reach their ends.
Inputs may be any that keep to these rules, and one draw needn't show every extreme that they name: `segment_ids`: each group holds 2 utterances one after another, each of 1 to 1000 frames.
All inputs are finite; a program needn't handle non-finite values.
Results may differ from the reference program's by a relative error of at most 0.012.
The reference program's roundings to bfloat16 on the way count: a program that leaves them out, or rounds other values in their place, can miss the bound.
Values may be sent and summed in bfloat16 or wider, within the bound.
A program may use at most 128 MiB of HBM per device.

```python
import math
import jax
import jax.numpy as jnp
import numpy as np
from jax import lax

D = 1024
H = 16
HD = 64
FF = 4096
GTOK = 1024
GROUPS = 8
MAXLEN = 1000
UTT = 2
SPAN = 10
SPANS = 40
STEP = 10
VROWS = 13


def draw_attn_master(key, part):
    noise = jax.random.truncated_normal(jax.random.fold_in(key, 11), -4.0, 4.0, (D, 4 * D), jnp.float32)
    column = lax.broadcasted_iota(jnp.int32, (D, 4 * D), 1)
    base = D ** (-0.5)
    wide = base * (MAXLEN // 4) ** 0.25
    return jnp.where(column < 2 * D, noise * (1.4 * base), noise * wide)


def draw_ffn_master(key, part):
    noise = jax.random.truncated_normal(jax.random.fold_in(key, 21), -4.0, 4.0, (FF, 2 * D), jnp.float32)
    column = lax.broadcasted_iota(jnp.int32, (FF, 2 * D), 1)
    return jnp.where(column < D, noise * D ** (-0.5), noise * FF ** (-0.5))


def draw_vec_master(key, part):
    noise = jax.random.truncated_normal(jax.random.fold_in(key, 31), -4.0, 4.0, (VROWS, D), jnp.float32)
    row_index = lax.broadcasted_iota(jnp.int32, (VROWS, D), 0)
    gain_rows = (row_index == 0) | (row_index == 5)
    return jnp.where(gain_rows, 1.0 + 0.1 * noise, jnp.where(row_index == 8, noise, 0.3 * noise))


def place_ends(values, stream_key, smallest, top_value):
    longest = values.shape.index(max(values.shape))
    spots = []
    for shift in (0, 1):
        where = [jax.random.randint(jax.random.fold_in(stream_key, axis), (), 0, length) for axis, length in enumerate(values.shape)]
        where[longest] = (where[longest] + shift) % values.shape[longest]
        spots.append(tuple(where))
    return values.at[spots[0]].set(smallest).at[spots[1]].set(top_value)


def level_of(key, shape, cuts, smallest, high):
    def one(position, blocks):
        steps = jax.random.uniform(jax.random.fold_in(jax.random.fold_in(key, 6), position), (blocks,), jnp.float32, smallest / len(cuts), high / len(cuts))
        return jnp.repeat(jnp.exp(steps), shape[position] // blocks).reshape((-1,) + (1,) * (len(shape) - position - 1))

    loudness = one(*cuts[0])
    for cut in cuts[1:]:
        loudness = loudness * one(*cut)
    return loudness


def length_profile(number_of, total, most, slope):
    loads = [(1 << 20) // math.isqrt(standing ** slope) + 1 for standing in range(2, number_of + 1)]
    spare, given = total - most - (number_of - 1), [1] * (number_of - 1)
    while spare > 0:
        movable = [i for i in range(number_of - 1) if given[i] < most]
        pool, remaining = sum([loads[i] for i in movable]), spare
        for i in movable:
            more = min(most - given[i], max(1, remaining * loads[i] // pool), spare)
            given[i] = given[i] + more
            spare = spare - more
    return np.array([most] + given)


def uneven_parts(stream_key, amount, total, reach, skew):
    if amount == 2:
        one = jax.random.randint(stream_key, (), max(1, total - reach), min(reach, total - 1) + 1)
        return jnp.stack([one, total - one])
    lengths = jnp.asarray(length_profile(amount, total, reach, skew), jnp.int32)
    pairs = (amount - 1) // 2
    donor, receiver = lengths[1:1 + 2 * pairs:2], lengths[2:2 + 2 * pairs:2]
    slack = jnp.minimum(donor - 1, reach - receiver)
    passed = jax.random.randint(jax.random.fold_in(stream_key, 1), (pairs,), 0, 1 << 20) % (slack + 1)
    lengths = lengths.at[1:1 + 2 * pairs:2].set(donor - passed).at[2:2 + 2 * pairs:2].set(receiver + passed)
    return lengths[jax.random.permutation(jax.random.fold_in(stream_key, 2), amount)]


def normal_values(key, shape, scale, reach, cuts=(), dtype=jnp.bfloat16):
    entries = scale * jax.random.normal(key, shape, jnp.float32)
    if cuts:
        entries = entries * level_of(key, shape, cuts, -0.22, 0.18)
    return jnp.clip(entries, -reach, reach).astype(dtype)


def setup_inputs(seed: int = 0) -> dict:
    key_list = jax.random.split(jax.random.key(seed), 14)
    return {
        "frames": normal_values(key_list[0], (GROUPS, GTOK, D), 1.0, 6.0, ((0, 8), (1, 4))),
        "segment_ids": jax.vmap(lambda own: jnp.searchsorted(jnp.cumsum(uneven_parts(own, UTT, GTOK, MAXLEN, 2)), jnp.arange(GTOK), side="right"))(jax.random.split(key_list[1], GROUPS)).reshape((GROUPS, GTOK)).astype(jnp.int32),
        "span_starts": place_ends(jax.random.randint(key_list[2], (GROUPS, SPANS), 0, GTOK - SPAN + 1), jax.random.fold_in(key_list[2], 1), 0, GTOK - SPAN).astype(jnp.int32),
        "cotangent": normal_values(key_list[3], (GROUPS, GTOK, D), 1.0, 6.0, ((0, 8), (1, 4))),
        "attn_master": draw_attn_master(jax.random.fold_in(key_list[13], 71), 0),
        "attn_first": normal_values(key_list[5], (D, 4 * D), (0.11 / (4 * D * D + 2 * D * FF) ** 0.5), 0.00048828125, ((0, 4), (1, 8)), jnp.float32),
        "attn_second": jnp.clip(jnp.exp(math.log(6.357828707947988e-10) - 2.7725887 * jax.random.uniform(key_list[6], (D, 4 * D), jnp.float32) ** level_of(key_list[6], (D, 4 * D), ((0, 4), (1, 8)), -0.2, 0.2)), 3.9736429424674924e-11, 6.357828707947988e-10),
        "ffn_master": draw_ffn_master(jax.random.fold_in(key_list[13], 71), 0),
        "ffn_first": normal_values(key_list[8], (FF, 2 * D), (0.11 / (4 * D * D + 2 * D * FF) ** 0.5), 0.00048828125, ((0, 4), (1, 8)), jnp.float32),
        "ffn_second": jnp.clip(jnp.exp(math.log(6.357828707947988e-10) - 2.7725887 * jax.random.uniform(key_list[9], (FF, 2 * D), jnp.float32) ** level_of(key_list[9], (FF, 2 * D), ((0, 4), (1, 8)), -0.2, 0.2)), 3.9736429424674924e-11, 6.357828707947988e-10),
        "vec_master": draw_vec_master(jax.random.fold_in(key_list[13], 71), 0),
        "vec_first": normal_values(key_list[11], (VROWS, D), (0.11 / (4 * D * D + 2 * D * FF) ** 0.5), 0.00048828125, (), jnp.float32),
        "vec_second": jnp.clip(jnp.exp(jax.random.uniform(key_list[12], (VROWS, D), jnp.float32, math.log(3.9736429424674924e-11), math.log(6.357828707947988e-10))), 3.9736429424674924e-11, 6.357828707947988e-10),
    }


EPS_NORM = 1e-05
BETA_ONE = 0.9
BETA_TWO = 0.999
EPS_ADAM = 1e-08
RATE_ATTN = 0.12
RATE_FFN = 0.03
RATE_VEC = 0.5
DECAY_RATE = 0.01
MAX_NORM = 1.0
NEG_FILL = -1e+30

@jax.custom_vjp
def low(v):
    return lax.optimization_barrier(v.astype(jnp.bfloat16)).astype(jnp.float32)

@jax.custom_vjp
def low_back(v):
    return v

def low_keep(v):
    return (low(v), None)

def low_pass(kept, grad):
    return (grad,)

def back_keep(v):
    return (v, None)

def back_low(kept, grad):
    return (low(grad),)
low.defvjp(low_keep, low_pass)
low_back.defvjp(back_keep, back_low)

def matmul(left, right):
    return jnp.dot(left, right, precision=lax.Precision.HIGHEST, preferred_element_type=jnp.float32)

def layer_norm(source, gain_row, shift_row):
    mean_val = lax.optimization_barrier(jnp.mean(source, axis=-1, keepdims=True))
    centred = source - mean_val
    inv_std = lax.rsqrt(lax.optimization_barrier(jnp.mean(centred * centred, axis=-1, keepdims=True)) + EPS_NORM)
    return centred * inv_std * gain_row + shift_row

def attend(query_all, key_all, value_all, segment_row):
    head_size = query_all.shape[-1]
    block_rows = min(512, GTOK)
    block_count = GTOK // block_rows

    def one_block(pieces):
        query_block, query_seg = pieces
        raw = jnp.einsum('qhd,khd->hqk', query_block, key_all, precision=lax.Precision.HIGHEST) * head_size ** (-0.5)
        raw = low_back(raw)
        same_utt = query_seg[None, :, None] == segment_row[None, None, :]
        masked_scores = jnp.where(same_utt, raw, NEG_FILL)
        probabilities = low(jax.nn.softmax(masked_scores, axis=-1))
        return jnp.einsum('hqk,khd->qhd', probabilities, value_all, precision=lax.Precision.HIGHEST)
    blocks = lax.map(jax.checkpoint(one_block), (query_all.reshape(block_count, block_rows, H, head_size), segment_row.reshape(block_count, block_rows)))
    return blocks.reshape(GTOK, D)

def layer(frame_rows, segment_row, masked, attn_w, ffn_w, vectors):
    w_qkv = attn_w[:, :3 * D].reshape(D, 3, D).transpose(2, 1, 0).reshape(D, 3 * D)
    w_proj = attn_w[:, 3 * D:]
    w_inner = ffn_w[:, :D].T
    w_outer = ffn_w[:, D:]
    x_in = jnp.where(masked[:, None], vectors[8][None, :], frame_rows)
    normed_a = low(layer_norm(x_in, vectors[0], vectors[1]))
    qkv = matmul(normed_a, w_qkv)
    query_all = low_back(low(qkv[:, :D] + vectors[2])).reshape(GTOK, H, HD)
    key_all = low_back(low(qkv[:, D:2 * D])).reshape(GTOK, H, HD)
    value_all = low_back(low(qkv[:, 2 * D:] + vectors[3])).reshape(GTOK, H, HD)
    attended = low_back(low(attend(query_all, key_all, value_all, segment_row)))
    resid = x_in + low_back(matmul(attended, w_proj) + vectors[4])
    normed_b = low(layer_norm(resid, vectors[5], vectors[6]))
    pre_act = low_back(matmul(normed_b, w_inner) + vectors[9:].reshape(FF))
    act_low = low(jax.nn.gelu(pre_act, approximate=False))
    return resid + low_back(matmul(act_low, w_outer) + vectors[7])

def adam_step(master, first, second, grad, rate, decay):
    first_new = BETA_ONE * first + (1.0 - BETA_ONE) * grad
    second_new = BETA_TWO * second + (1.0 - BETA_TWO) * grad * grad
    first_hat = first_new / (1.0 - BETA_ONE ** STEP)
    second_hat = second_new / (1.0 - BETA_TWO ** STEP)
    master_new = master - rate * (first_hat / (jnp.sqrt(second_hat) + EPS_ADAM) + decay * master)
    return (master_new, first_new, second_new)

def reference(frames, segment_ids, span_starts, cotangent, attn_master, attn_first, attn_second, ffn_master, ffn_first, ffn_second, vec_master, vec_first, vec_second):
    attn_low = attn_master.astype(jnp.bfloat16).astype(jnp.float32)
    ffn_low = ffn_master.astype(jnp.bfloat16).astype(jnp.float32)
    positions = lax.iota(jnp.int32, GTOK)

    def one_group(carry, inputs):
        frame_rows, segment_row, start_row, cot_rows = inputs
        inside = (positions[:, None] >= start_row[None, :]) & (positions[:, None] < start_row[None, :] + SPAN)
        masked = jnp.any(inside, axis=1)

        def forward(frame_in, attn_w, ffn_w, vectors):
            return layer(frame_in, segment_row, masked, attn_w, ffn_w, vectors)
        result, pull_back = jax.vjp(forward, frame_rows.astype(jnp.float32), attn_low, ffn_low, vec_master)
        grads = pull_back(cot_rows.astype(jnp.float32))
        summed = tuple((left + right for left, right in zip(carry, grads[1:])))
        return (summed, (result.astype(jnp.bfloat16), grads[0]))
    start = (jnp.zeros_like(attn_low), jnp.zeros_like(ffn_low), jnp.zeros_like(vec_master))
    summed, (output, frames_grad) = lax.scan(one_group, start, (frames, segment_ids, span_starts, cotangent))
    attn_grad, ffn_grad, vec_grad = summed
    grad_norm = jnp.sqrt(jnp.sum(attn_grad * attn_grad) + jnp.sum(ffn_grad * ffn_grad) + jnp.sum(vec_grad * vec_grad))
    clip = jnp.minimum(1.0, MAX_NORM / (grad_norm + 1e-06))
    attn_new, attn_first_new, attn_second_new = adam_step(attn_master, attn_first, attn_second, attn_grad * clip, RATE_ATTN, DECAY_RATE)
    ffn_new, ffn_first_new, ffn_second_new = adam_step(ffn_master, ffn_first, ffn_second, ffn_grad * clip, RATE_FFN, DECAY_RATE)
    vec_new, vec_first_new, vec_second_new = adam_step(vec_master, vec_first, vec_second, vec_grad * clip, RATE_VEC, 0.0)
    return (output, frames_grad, grad_norm, attn_new, attn_first_new, attn_second_new, attn_new.astype(jnp.bfloat16), ffn_new, ffn_first_new, ffn_second_new, ffn_new.astype(jnp.bfloat16), vec_new, vec_first_new, vec_second_new)
```

```python
import functools

import jax
import jax.numpy as jnp
from jax import lax
from jax.experimental import pallas as pl
from jax.experimental.pallas import tpu as pltpu
from jax.sharding import PartitionSpec as P

H = 16
SPAN = 10
STEP = 10

EPS_NORM = 1e-05
BETA_ONE = 0.9
BETA_TWO = 0.999
EPS_ADAM = 1e-08
RATE_ATTN = 0.12
RATE_FFN = 0.03
RATE_VEC = 0.5
DECAY_RATE = 0.01
MAX_NORM = 1.0
NEG_FILL = -1e30

SLABS = 8
LANES = 128
F32 = jnp.float32
BF16 = jnp.bfloat16
MESH = pl.DeviceIdType.MESH


def adam_step(master, first, second, grad, rate, decay):
    first_new = BETA_ONE * first + (1.0 - BETA_ONE) * grad
    second_new = BETA_TWO * second + (1.0 - BETA_TWO) * grad * grad
    first_hat = first_new / (1.0 - BETA_ONE**STEP)
    second_hat = second_new / (1.0 - BETA_TWO**STEP)
    master_new = master - rate * (first_hat / (jnp.sqrt(second_hat) + EPS_ADAM) + decay * master)
    return (master_new, first_new, second_new)


def nn(left, right):
    return lax.dot_general(left, right, (((1,), (0,)), ((), ())), preferred_element_type=F32)


def nt(left, right):
    return lax.dot_general(left, right, (((1,), (1,)), ((), ())), preferred_element_type=F32)


def tn(left, right):
    return lax.dot_general(left, right, (((0,), (0,)), ((), ())), preferred_element_type=F32)


def normalise(source):
    mean_val = jnp.mean(source, axis=-1, keepdims=True)
    centred = source - mean_val
    inv_std = lax.rsqrt(jnp.mean(centred * centred, axis=-1, keepdims=True) + EPS_NORM)
    return centred * inv_std, inv_std


def norm_back(grad_out, normed, inv_std, gain_row):
    scaled = grad_out * gain_row
    inner = (
        scaled
        - jnp.mean(scaled, axis=-1, keepdims=True)
        - normed * jnp.mean(scaled * normed, axis=-1, keepdims=True)
    )
    return inner * inv_std


def col_sum(value):
    return jnp.sum(value, axis=0, keepdims=True)


class Gather:
    def __init__(self, cp, buf, base, place, off, rows):
        self.cp, self.buf, self.b = cp, buf, base
        self.s, self.px, self.py, self.pd = place
        self.off, self.h = off, rows // 2

    def top(self, slot):
        return self.buf.at[slot, pl.ds(self.off, self.h)]

    def bot(self, slot):
        return self.buf.at[slot, pl.ds(self.off + self.h, self.h)]

    def c(self, part, slot, i, to):
        ref = part(slot)
        return self.cp(ref, ref, self.b + i, to)

    def start(self):
        self.c(self.top, self.s, 0, self.px).start()
        self.c(self.bot, self.s, 2, self.py).start()
        self.c(self.bot, self.s, 1, self.px).start()
        self.c(self.top, self.s, 3, self.py).start()

    def relay(self):
        self.c(self.top, self.px, 0, self.px).wait_recv()
        self.c(self.top, self.px, 4, self.py).start()
        self.c(self.bot, self.py, 2, self.py).wait_recv()
        self.c(self.bot, self.py, 5, self.px).start()

    def wait_x(self):
        self.c(self.bot, self.px, 1, self.px).wait_recv()

    def wait_y(self):
        self.c(self.top, self.py, 3, self.py).wait_recv()

    def wait_d(self):
        self.c(self.top, self.pd, 4, self.py).wait_recv()
        self.c(self.bot, self.pd, 5, self.px).wait_recv()

    def sent(self):
        for part, slot, i, to in (
            (self.top, self.s, 0, self.px),
            (self.bot, self.s, 2, self.py),
            (self.bot, self.s, 1, self.px),
            (self.top, self.s, 3, self.py),
            (self.top, self.px, 4, self.py),
            (self.bot, self.py, 5, self.px),
        ):
            self.c(part, slot, i, to).wait_send()


class Scatter:
    def __init__(self, cp, part, in_x, in_y, via_x, via_y, base, place):
        _, px, py, _ = place
        h = in_x.shape[0] // 2
        top, bot = pl.ds(0, h), pl.ds(h, h)
        self.part, self.via_x, self.via_y, self.h = part, via_x, via_y, h
        self.copies = [
            cp(part.at[2, top], via_x, base, px),
            cp(part.at[2, bot], via_y, base + 1, py),
            cp(part.at[0, top], in_x.at[top], base + 2, px),
            cp(part.at[1, bot], in_y.at[bot], base + 3, py),
            cp(part.at[1, top], in_y.at[top], base + 4, py),
            cp(part.at[0, bot], in_x.at[bot], base + 5, px),
        ]

    def start(self, relation):
        for i in {3: (0, 1), 1: (2,), 2: (3,)}[relation]:
            self.copies[i].start()

    def relay_y(self):
        self.copies[0].wait_recv()
        self.part[1, : self.h, :] = (self.part[1, : self.h, :].astype(F32) + self.via_x[...].astype(F32)).astype(BF16)
        self.copies[4].start()

    def relay_x(self):
        self.copies[1].wait_recv()
        self.part[0, self.h :, :] = (self.part[0, self.h :, :].astype(F32) + self.via_y[...].astype(F32)).astype(BF16)
        self.copies[5].start()

    def wait(self):
        for i in (2, 3, 4, 5):
            self.copies[i].wait_recv()

    def sent(self):
        for copy in self.copies:
            copy.wait_send()


def layer_kernel(
    frames,
    mask_col,
    cot,
    seg_q,
    seg_k,
    vec,
    w_attn,
    w_ffn,
    out,
    frames_grad,
    vec_grad,
    g_attn,
    g_ffn,
    fr_g,
    cot_g,
    a_g,
    wp,
    qa,
    ka,
    va,
    kt,
    att,
    b_g,
    act_g,
    gp_g,
    resid,
    own,
    part,
    part2,
    in_x,
    in_y,
    via_x,
    via_y,
    in_x2,
    in_y2,
    via_x2,
    via_y2,
    gsend,
    gm,
    dom,
    ga_g,
    gres,
    dqkv,
    dk_acc,
    dv_acc,
    send_sem,
    recv_sem,
):
    s = lax.axis_index("seq")
    d = lax.axis_index("dp")
    core = lax.rem(d, 2)
    sib = d + 1 - 2 * core

    def peer(r):
        high = lax.rem(s // 2 + r // 2, 2)
        low = lax.rem(lax.rem(s, 2) + r % 2, 2)
        return 2 * high + low

    px, py, pd = peer(1), peer(2), peer(3)
    place = (s, px, py, pd)

    def cp(src, dst, i, to):
        return pltpu.make_async_remote_copy(
            src_ref=src,
            dst_ref=dst,
            send_sem=send_sem.at[i],
            recv_sem=recv_sem.at[i],
            device_id=(to, d),
            device_id_type=MESH,
        )

    def cp_sib(src, dst, i):
        return pltpu.make_async_remote_copy(
            src_ref=src,
            dst_ref=dst,
            send_sem=send_sem.at[i],
            recv_sem=recv_sem.at[i],
            device_id=(s, sib),
            device_id_type=MESH,
        )

    rows = frames.shape[0]
    width = frames.shape[1]
    local = width // 4
    slab_a = w_attn.shape[2]
    slab_f = w_ffn.shape[2]
    per_a = width // slab_a
    per_f = width // slab_f
    tile = 256
    chunk = 32

    barrier = pltpu.get_barrier_semaphore()
    for to in (px, py, pd):
        pl.semaphore_signal(barrier, inc=1, device_id=(to, d), device_id_type=MESH)
    pl.semaphore_signal(barrier, inc=1, device_id=(s, sib), device_id_type=MESH)
    pl.semaphore_wait(barrier, 4)

    fr_g[s] = frames[...]
    frames_in = Gather(cp, fr_g, 0, place, 0, rows)
    frames_in.start()

    cot_g[s] = cot[...]
    cot_in = Gather(cp, cot_g, 15, place, 0, rows)
    for i in range(per_a):
        wp[s, :, i * slab_a : (i + 1) * slab_a] = w_attn[3 * per_a + i]
    half = rows // 2
    wp_off = pl.multiple_of(core * half, half)
    wp_in = Gather(cp, wp, 6, place, wp_off, half)
    wp_cross = [
        cp_sib(wp.at[p, pl.ds(wp_off, half)], wp.at[p, pl.ds(wp_off, half)], 12 + i) for i, p in enumerate((px, py, pd))
    ]
    vec_grad[...] = jnp.zeros_like(vec_grad)

    lane = lax.broadcasted_iota(jnp.int32, (rows, LANES), 1)
    low_head = lane < LANES // 2
    q_bias = vec[2:3, pl.ds(pl.multiple_of(s * local, local), local)]
    v_bias = vec[3:4, pl.ds(pl.multiple_of(s * local, local), local)]

    def weight_rows(first, count, start, size):
        return jnp.concatenate([w_attn[first + i, start : start + size, :] for i in range(count)], axis=1)

    def enter(blk):
        def norm_rows(i, carry):
            at = pl.ds(pl.multiple_of(i * chunk, chunk), chunk)
            at_all = pl.ds(pl.multiple_of(blk * rows + i * chunk, chunk), chunk)
            x = jnp.where(mask_col[at_all, :] > 0.0, vec[8:9, :], fr_g[blk, at, :].astype(F32))
            normed, _ = normalise(x)
            a_g[blk, at, :] = (normed * vec[0:1, :] + vec[1:2, :]).astype(BF16)
            return carry

        lax.fori_loop(0, rows // chunk, norm_rows, 0)
        a = a_g[blk]
        at_all = pl.ds(pl.multiple_of(blk * rows, rows), rows)
        q = (nt(a, weight_rows(0, per_a, 0, local)) + q_bias).astype(BF16).astype(F32) * 0.125
        for pair in range(2):
            both = q[:, pair * LANES : (pair + 1) * LANES]
            for h in range(2):
                keep = low_head if h == 0 else jnp.logical_not(low_head)
                qa[2 * pair + h, blk, :, :LANES] = jnp.where(keep, both, 0.0).astype(BF16)
                qa[2 * pair + h, blk, :, LANES:] = seg_q[at_all, :]
        k = nt(a, weight_rows(per_a, per_a, 0, local)).astype(BF16)
        for pair in range(2):
            both = k[:, pair * LANES : (pair + 1) * LANES]
            ka[pair, at_all, :LANES] = both
            ka[pair, at_all, LANES:] = seg_k[at_all, :]
            kt[pair, :, at_all] = jnp.transpose(both)
        v = (nt(a, weight_rows(2 * per_a, per_a, 0, local)) + v_bias).astype(BF16)
        for pair in range(2):
            va[pair, at_all, :] = v[:, pair * LANES : (pair + 1) * LANES]

    enter(s)
    frames_in.relay()
    wp_in.start()
    frames_in.wait_x()
    enter(px)
    frames_in.wait_y()
    enter(py)
    frames_in.wait_d()
    enter(pd)
    wp_in.relay()
    cot_in.start()

    def att_x(j, slot):
        return cp(att.at[slot, j], att.at[slot, j], 21 + j, px)

    def att_y(j, slot):
        return cp(att.at[slot, j], att.at[slot, j], 25 + j, py)

    def att_relay(j, start):
        even = lax.rem(j, 2) == 0

        @pl.when(even)
        def _():
            if start:
                att_x(j, px).wait_recv()
                cp(att.at[px, j], att.at[px, j], 29 + j, py).start()
            else:
                cp(att.at[px, j], att.at[px, j], 29 + j, py).wait_send()

        @pl.when(jnp.logical_not(even))
        def _():
            if start:
                att_y(j, py).wait_recv()
                cp(att.at[py, j], att.at[py, j], 29 + j, px).start()
            else:
                cp(att.at[py, j], att.at[py, j], 29 + j, px).wait_send()

    def attend(j, carry):
        for pair in range(2):
            outs = []
            for h in range(2):
                head = 2 * pair + h
                scores = nt(qa[head, j], ka[pair])
                peak = jnp.max(scores, axis=-1, keepdims=True)
                terms = jnp.exp(scores - peak)
                total = jnp.sum(terms, axis=-1, keepdims=True)
                probs = (terms * (1.0 / total)).astype(BF16)
                outs.append(nn(probs, va[pair]))
                log_total = -(peak + jnp.log(total))
                part_one = log_total.astype(BF16).astype(F32)
                rest = log_total - part_one
                part_two = rest.astype(BF16).astype(F32)
                part_three = rest - part_two
                aug = qa[head, j, :, LANES:].astype(F32)
                aug = jnp.where(lane == 2, part_one, aug)
                aug = jnp.where(lane == 3, part_two, aug)
                aug = jnp.where(lane == 4, part_three, aug)
                qa[head, j, :, LANES:] = aug.astype(BF16)
            att[s, j, :, pair * LANES : (pair + 1) * LANES] = jnp.where(low_head, outs[0], outs[1]).astype(BF16)
        att_x(j, s).start()
        att_y(j, s).start()

        @pl.when(j > 0)
        def _():
            att_relay(j - 1, True)

        return carry

    lax.fori_loop(0, 4, attend, 0)
    att_relay(3, True)
    wp_in.wait_x()
    wp_cross[0].start()
    wp_in.wait_y()
    wp_cross[1].start()
    wp_in.wait_d()
    wp_cross[2].start()
    cot_in.relay()
    other_off = pl.multiple_of((1 - core) * half, half)
    for i, p in enumerate((px, py, pd)):
        cp_sib(wp.at[p, pl.ds(other_off, half)], wp.at[p, pl.ds(other_off, half)], 12 + i).wait_recv()

    def project(j, carry):
        even = lax.rem(j, 2) == 0

        @pl.when(even)
        def _():
            att_y(j, py).wait_recv()
            cp(att.at[pd, j], att.at[pd, j], 29 + j, py).wait_recv()

        @pl.when(jnp.logical_not(even))
        def _():
            att_x(j, px).wait_recv()
            cp(att.at[pd, j], att.at[pd, j], 29 + j, px).wait_recv()

        left = jnp.concatenate([att[p, j] for p in range(4)], axis=1)
        for i in range(width // tile):
            right = jnp.concatenate([wp[p, :, i * tile : (i + 1) * tile] for p in range(4)], axis=0)
            own[:, i * tile : (i + 1) * tile] = nn(left, right)

        def norm_rows(i, inner):
            at = pl.ds(pl.multiple_of(i * chunk, chunk), chunk)
            at_all = pl.ds(pl.multiple_of(j * rows + i * chunk, chunk), chunk)
            x = jnp.where(mask_col[at_all, :] > 0.0, vec[8:9, :], fr_g[j, at, :].astype(F32))
            total = x + own[at, :] + vec[4:5, :]

            @pl.when(j == s)
            def _():
                resid[at, :] = total

            normed, _ = normalise(total)
            b_g[j, at, :] = (normed * vec[5:6, :] + vec[6:7, :]).astype(BF16)
            return inner

        lax.fori_loop(0, rows // chunk, norm_rows, 0)
        return carry

    lax.fori_loop(0, 4, project, 0)

    def feed(r):
        blk = peer(r)

        def hidden_tile(i, carry):
            at = pl.ds(pl.multiple_of(i * tile, tile), tile)
            w_in = jnp.concatenate([w_ffn[k, at, :] for k in range(per_f)], axis=1)
            w_out = jnp.concatenate([w_ffn[per_f + k, at, :] for k in range(per_f)], axis=1)
            pre = nt(b_g[blk], w_in) + vec[pl.ds(9 + s, 1), at]
            grad_act = nt(cot_g[blk], w_out)
            cdf = 0.5 * (1.0 + lax.erf(pre * 0.7071067811865476))
            act_g[blk, :, at] = (pre * cdf).astype(BF16)
            density = jnp.exp(-0.5 * pre * pre) * 0.3989422804014327
            grad_pre = ((cdf + pre * density) * grad_act).astype(BF16)
            gp_g[blk, :, at] = grad_pre
            vec_grad[pl.ds(9 + s, 1), at] += col_sum(grad_pre.astype(F32))
            return carry

        lax.fori_loop(0, w_ffn.shape[1] // tile, hidden_tile, 0)
        left = gp_g[blk]
        for k in range(per_f):
            at = slice(k * slab_f, (k + 1) * slab_f)
            value = nn(left, w_ffn[k])
            if r == 0:
                own[:, at] = value
            else:
                part[r - 1, :, at] = value.astype(BF16)

    sum_b = Scatter(cp, part, in_x, in_y, via_x, via_y, 33, place)
    cot_in.wait_x()
    cot_in.wait_y()
    cot_in.wait_d()
    feed(3)
    sum_b.start(3)
    feed(1)
    sum_b.start(1)
    feed(2)
    sum_b.start(2)
    sum_b.relay_y()
    sum_b.relay_x()
    feed(0)
    sum_b.wait()

    def back_two(i, carry):
        at = pl.ds(pl.multiple_of(i * chunk, chunk), chunk)
        grad_b = own[at, :] + in_x[at, :].astype(F32) + in_y[at, :].astype(F32)
        normed, inv_std = normalise(resid[at, :])
        grad_y = cot[at, :].astype(F32)
        grad_resid = grad_y + norm_back(grad_b, normed, inv_std, vec[5:6, :])
        gres[at, :] = grad_resid
        low = grad_resid.astype(BF16)
        ga_g[s, at, :] = low
        vec_grad[4:5, :] += col_sum(low.astype(F32))
        vec_grad[5:6, :] += col_sum(grad_b * normed)
        vec_grad[6:7, :] += col_sum(grad_b)
        vec_grad[7:8, :] += col_sum(grad_y)
        return carry

    lax.fori_loop(0, rows // chunk, back_two, 0)

    for i, r in enumerate((3, 1, 2)):
        gsend[r] = nt(ga_g[s], wp[peer(r)]).astype(BF16)
        cp(gsend.at[r], gm.at[s], 39 + i, peer(r)).start()
    gm[s] = nt(ga_g[s], wp[s]).astype(BF16)
    ga_in = Gather(cp, ga_g, 42, place, 0, rows)
    ga_in.start()
    sum_b.sent()

    sum_o = Scatter(cp, part, in_x2, in_y2, via_x2, via_y2, 48, place)

    def out_part(blk, k):
        return nn(act_g[blk], w_ffn[per_f + k])

    for r in (3, 1, 2):
        for k in range(per_f):
            part[r - 1, :, k * slab_f : (k + 1) * slab_f] = out_part(peer(r), k).astype(BF16)
        sum_o.start(r)

    def ffn_grads(i, carry):
        at = pl.ds(pl.multiple_of(i * tile, tile), tile)
        for left, right, first in ((gp_g, b_g, 0), (act_g, cot_g, per_f)):
            turned = jnp.transpose(jnp.concatenate([left[p, :, at] for p in range(4)], axis=0))
            for k in range(per_f):
                cols = jnp.concatenate([right[p, :, k * slab_f : (k + 1) * slab_f] for p in range(4)], axis=0)
                g_ffn[first + k, at, :] = nn(turned, cols).astype(BF16)
        return carry

    lax.fori_loop(0, w_ffn.shape[1] // tile, ffn_grads, 0)

    for i, r in enumerate((3, 1, 2)):
        cp(gsend.at[r], gm.at[peer(r)], 39 + i, peer(r)).wait_recv()

    def spread(j, carry):
        for pair in range(2):
            both = gm[j, :, pair * LANES : (pair + 1) * LANES].astype(F32)
            dom[2 * pair, j] = jnp.where(low_head, both, 0.0).astype(BF16)
            dom[2 * pair + 1, j] = jnp.where(low_head, 0.0, both).astype(BF16)
        return carry

    lax.fori_loop(0, 4, spread, 0)
    ga_in.relay()
    sum_o.relay_y()
    sum_o.relay_x()

    def back_pair(pair):
        dk_acc[...] = jnp.zeros_like(dk_acc)
        dv_acc[...] = jnp.zeros_like(dv_acc)

        def back_block(j, carry):
            sides = []
            for h in range(2):
                head = 2 * pair + h
                probs = jnp.exp(nt(ka[pair], qa[head, j]))
                grad_probs = nt(va[pair], dom[head, j])
                delta = jnp.sum(probs * grad_probs, axis=0, keepdims=True)
                grad_scores = (probs * (grad_probs - delta)).astype(BF16)
                dv_acc[...] += nn(probs.astype(BF16), dom[head, j])
                dk_acc[...] += nn(grad_scores, qa[head, j, :, :LANES])
                sides.append(nn(kt[pair], grad_scores))
            half_lane = LANES // 2
            turned = jnp.concatenate([sides[0][:half_lane], sides[1][half_lane:]], axis=0)
            dqkv[0, j, :, pair * LANES : (pair + 1) * LANES] = (jnp.transpose(turned) * 0.125).astype(BF16)
            return carry

        lax.fori_loop(0, 4, back_block, 0)
        for j in range(4):
            at = slice(j * rows, (j + 1) * rows)
            dqkv[1, j, :, pair * LANES : (pair + 1) * LANES] = dk_acc[at, :].astype(BF16)
            dqkv[2, j, :, pair * LANES : (pair + 1) * LANES] = dv_acc[at, :].astype(BF16)

    back_pair(0)
    back_pair(1)

    sum_a = Scatter(cp, part2, in_x, in_y, via_x, via_y, 54, place)

    def grad_in(r):
        blk = peer(r)
        left = jnp.concatenate([dqkv[c, blk] for c in range(3)], axis=1)
        for k in range(per_a):
            at = slice(k * slab_a, (k + 1) * slab_a)
            right = jnp.concatenate([w_attn[c * per_a + k] for c in range(3)], axis=0)
            value = nn(left, right)
            if r == 0:
                own[:, at] = value
            else:
                part2[r - 1, :, at] = value.astype(BF16)

    for r in (3, 1, 2):
        grad_in(r)
        sum_a.start(r)
    grad_in(0)

    my_cols = pl.ds(pl.multiple_of(s * local, local), local)
    for j in range(4):
        vec_grad[2:3, my_cols] += col_sum(dqkv[0, j].astype(F32))
        vec_grad[3:4, my_cols] += col_sum(dqkv[2, j].astype(F32))

    def attn_grads(c):
        turned = jnp.transpose(jnp.concatenate([dqkv[c, p] for p in range(4)], axis=0))
        for k in range(per_a):
            cols = jnp.concatenate([a_g[p, :, k * slab_a : (k + 1) * slab_a] for p in range(4)], axis=0)
            g_attn[c * per_a + k] = nn(turned, cols).astype(BF16)

    attn_grads(0)
    attn_grads(1)
    sum_a.relay_y()
    sum_a.relay_x()
    attn_grads(2)
    ga_in.wait_x()
    ga_in.wait_y()
    ga_in.wait_d()
    turned = jnp.transpose(jnp.concatenate([att[s, p] for p in range(4)], axis=0))
    for k in range(per_a):
        cols = jnp.concatenate([ga_g[p, :, k * slab_a : (k + 1) * slab_a] for p in range(4)], axis=0)
        g_attn[3 * per_a + k] = nn(turned, cols).astype(BF16)

    sum_o.wait()
    for k in range(per_f):
        at = slice(k * slab_f, (k + 1) * slab_f)
        total = out_part(s, k) + resid[:, at] + in_x2[:, at].astype(F32) + in_y2[:, at].astype(F32) + vec[7:8, at]
        out[:, at] = total.astype(BF16)

    sum_a.wait()

    def back_one(i, carry):
        at = pl.ds(pl.multiple_of(i * chunk, chunk), chunk)
        at_all = pl.ds(pl.multiple_of(s * rows + i * chunk, chunk), chunk)
        grad_a = own[at, :] + in_x[at, :].astype(F32) + in_y[at, :].astype(F32)
        masked = mask_col[at_all, :] > 0.0
        normed, inv_std = normalise(jnp.where(masked, vec[8:9, :], frames[at, :].astype(F32)))
        grad_x = gres[at, :] + norm_back(grad_a, normed, inv_std, vec[0:1, :])
        frames_grad[at, :] = jnp.where(masked, 0.0, grad_x)
        vec_grad[0:1, :] += col_sum(grad_a * normed)
        vec_grad[1:2, :] += col_sum(grad_a)
        vec_grad[8:9, :] += col_sum(jnp.where(masked, grad_x, 0.0))
        return carry

    lax.fori_loop(0, rows // chunk, back_one, 0)

    frames_in.sent()
    wp_in.sent()
    for copy in wp_cross:
        copy.wait_send()
    cot_in.sent()

    def att_sent(j, carry):
        att_x(j, s).wait_send()
        att_y(j, s).wait_send()
        att_relay(j, False)
        return carry

    lax.fori_loop(0, 4, att_sent, 0)
    for i, r in enumerate((3, 1, 2)):
        cp(gsend.at[r], gm.at[s], 39 + i, peer(r)).wait_send()
    ga_in.sent()
    sum_o.sent()
    sum_a.sent()


def run_layer(frames, mask_col, cot, seg_q, seg_k, vec, w_attn, w_ffn):
    rows, width = frames.shape
    group = 4 * rows
    hidden = w_ffn.shape[1]
    local = width // 4
    vmem = pl.BlockSpec(memory_space=pltpu.VMEM)
    block = (4, rows, width)
    scratch = [
        pltpu.VMEM(block, BF16),
        pltpu.VMEM(block, BF16),
        pltpu.VMEM(block, BF16),
        pltpu.VMEM((4, local, width), BF16),
        pltpu.VMEM((4, 4, rows, 2 * LANES), BF16),
        pltpu.VMEM((2, group, 2 * LANES), BF16),
        pltpu.VMEM((2, group, LANES), BF16),
        pltpu.VMEM((2, LANES, group), BF16),
        pltpu.VMEM((4, 4, rows, local), BF16),
        pltpu.VMEM(block, BF16),
        pltpu.VMEM((4, rows, hidden), BF16),
        pltpu.VMEM((4, rows, hidden), BF16),
        pltpu.VMEM((rows, width), F32),
        pltpu.VMEM((rows, width), F32),
        pltpu.VMEM((3, rows, width), BF16),
        pltpu.VMEM((3, rows, width), BF16),
        pltpu.VMEM((rows, width), BF16),
        pltpu.VMEM((rows, width), BF16),
        pltpu.VMEM((rows // 2, width), BF16),
        pltpu.VMEM((rows // 2, width), BF16),
        pltpu.VMEM((rows, width), BF16),
        pltpu.VMEM((rows, width), BF16),
        pltpu.VMEM((rows // 2, width), BF16),
        pltpu.VMEM((rows // 2, width), BF16),
        pltpu.VMEM((4, rows, local), BF16),
        pltpu.VMEM((4, rows, local), BF16),
        pltpu.VMEM((4, 4, rows, LANES), BF16),
        pltpu.VMEM(block, BF16),
        pltpu.VMEM((rows, width), F32),
        pltpu.VMEM((3, 4, rows, local), BF16),
        pltpu.VMEM((group, LANES), F32),
        pltpu.VMEM((group, LANES), F32),
        pltpu.SemaphoreType.DMA((60,)),
        pltpu.SemaphoreType.DMA((60,)),
    ]
    return pl.pallas_call(
        layer_kernel,
        out_shape=(
            jax.ShapeDtypeStruct((rows, width), BF16),
            jax.ShapeDtypeStruct((rows, width), F32),
            jax.ShapeDtypeStruct(vec.shape, F32),
            jax.ShapeDtypeStruct(w_attn.shape, BF16),
            jax.ShapeDtypeStruct(w_ffn.shape, BF16),
        ),
        in_specs=[vmem] * 8,
        out_specs=(vmem,) * 5,
        scratch_shapes=scratch,
        compiler_params=pltpu.CompilerParams(
            collective_id=0, has_side_effects=True, vmem_limit_bytes=60 * 1024 * 1024
        ),
    )(frames, mask_col, cot, seg_q, seg_k, vec, w_attn, w_ffn)


def per_device(
    frames,
    segment_ids,
    span_starts,
    cotangent,
    attn_master,
    attn_first,
    attn_second,
    ffn_master,
    ffn_first,
    ffn_second,
    vec_master,
    vec_first,
    vec_second,
):
    dp_count = lax.axis_size("dp")
    group = segment_ids.shape[1]

    def gather_slabs(master):
        shard = master.astype(BF16)
        if dp_count == SLABS:
            return lax.all_gather(shard, "dp", axis=0)
        whole = lax.all_gather(shard, "dp", axis=1, tiled=True)
        return whole.reshape(shard.shape[0], SLABS, -1).transpose(1, 0, 2)

    w_attn = gather_slabs(attn_master)
    w_ffn = gather_slabs(ffn_master)

    positions = lax.iota(jnp.int32, group)
    starts = span_starts[0]
    inside = (positions[:, None] >= starts[None, :]) & (positions[:, None] < starts[None, :] + SPAN)
    mask_col = jnp.any(inside, axis=1).astype(F32)[:, None]
    seg = segment_ids[0][:, None]
    lane = lax.broadcasted_iota(jnp.int32, (group, LANES), 1)
    first, second = seg == 0, seg == 1
    zero = jnp.zeros((), F32)
    seg_q = jnp.where(lane == 0, jnp.where(second, NEG_FILL, zero), jnp.where(lane == 1, jnp.where(first, NEG_FILL, zero), zero))
    seg_k = jnp.where(
        lane == 0,
        first.astype(F32),
        jnp.where(lane == 1, second.astype(F32), ((lane >= 2) & (lane <= 4)).astype(F32)),
    )
    output, frames_grad, vec_local, g_attn, g_ffn = run_layer(
        frames[0], mask_col, cotangent[0], seg_q.astype(BF16), seg_k.astype(BF16), vec_master, w_attn, w_ffn
    )

    def scatter_slabs(slabs):
        slabs = slabs.astype(F32)
        if dp_count == SLABS:
            return lax.psum_scatter(slabs, "dp", scatter_dimension=0, tiled=False)
        whole = slabs.transpose(1, 0, 2).reshape(slabs.shape[1], -1)
        return lax.psum_scatter(whole, "dp", scatter_dimension=1, tiled=True)

    attn_owned = scatter_slabs(g_attn)
    ffn_owned = scatter_slabs(g_ffn)
    owned_squares = jnp.sum(attn_owned * attn_owned) + jnp.sum(ffn_owned * ffn_owned)
    vec_grad, total_squares = lax.psum((vec_local, owned_squares), ("seq", "dp"))
    grad_norm = jnp.sqrt(total_squares + jnp.sum(vec_grad * vec_grad))
    clip = jnp.minimum(1.0, MAX_NORM / (grad_norm + 1e-06))
    attn_new, attn_first_new, attn_second_new = adam_step(
        attn_master, attn_first, attn_second, attn_owned * clip, RATE_ATTN, DECAY_RATE
    )
    ffn_new, ffn_first_new, ffn_second_new = adam_step(
        ffn_master, ffn_first, ffn_second, ffn_owned * clip, RATE_FFN, DECAY_RATE
    )
    vec_new, vec_first_new, vec_second_new = adam_step(
        vec_master, vec_first, vec_second, vec_grad * clip, RATE_VEC, 0.0
    )
    return (
        output[None],
        frames_grad[None],
        grad_norm,
        attn_new,
        attn_first_new,
        attn_second_new,
        attn_new.astype(BF16),
        ffn_new,
        ffn_first_new,
        ffn_second_new,
        ffn_new.astype(BF16),
        vec_new,
        vec_first_new,
        vec_second_new,
    )


def solution(mesh):
    return jax.shard_map(
        per_device,
        mesh=mesh,
        in_specs=(
            P("dp", "seq", None),
            P("dp", None),
            P("dp", None),
            P("dp", "seq", None),
            P("seq", "dp"),
            P("seq", "dp"),
            P("seq", "dp"),
            P("seq", "dp"),
            P("seq", "dp"),
            P("seq", "dp"),
            P(),
            P(),
            P(),
        ),
        out_specs=(
            P("dp", "seq", None),
            P("dp", "seq", None),
            P(),
            P("seq", "dp"),
            P("seq", "dp"),
            P("seq", "dp"),
            P("seq", "dp"),
            P("seq", "dp"),
            P("seq", "dp"),
            P("seq", "dp"),
            P("seq", "dp"),
            P(),
            P(),
            P(),
        ),
        check_vma=False,
    )
```

```python
import functools

import jax
import jax.numpy as jnp
from jax import lax
from jax.experimental import pallas as pl
from jax.experimental.pallas import tpu as pltpu
from jax.sharding import PartitionSpec as P

H = 16
SPAN = 10
STEP = 10

EPS_NORM = 1e-05
BETA_ONE = 0.9
BETA_TWO = 0.999
EPS_ADAM = 1e-08
RATE_ATTN = 0.12
RATE_FFN = 0.03
RATE_VEC = 0.5
DECAY_RATE = 0.01
MAX_NORM = 1.0
NEG_FILL = -1e30

SLABS = 8
LANES = 128
VMEM_LIMIT = 62 * 1024 * 1024
F32 = jnp.float32
BF16 = jnp.bfloat16
MESH = pl.DeviceIdType.MESH


def adam_step(master, first, second, grad, rate, decay):
    first_new = BETA_ONE * first + (1.0 - BETA_ONE) * grad
    second_new = BETA_TWO * second + (1.0 - BETA_TWO) * grad * grad
    first_hat = first_new / (1.0 - BETA_ONE**STEP)
    second_hat = second_new / (1.0 - BETA_TWO**STEP)
    master_new = master - rate * (first_hat / (jnp.sqrt(second_hat) + EPS_ADAM) + decay * master)
    return (master_new, first_new, second_new)


def nn(left, right):
    return lax.dot_general(left, right, (((1,), (0,)), ((), ())), preferred_element_type=F32)


def nt(left, right):
    return lax.dot_general(left, right, (((1,), (1,)), ((), ())), preferred_element_type=F32)


def tn(left, right):
    return lax.dot_general(left, right, (((0,), (0,)), ((), ())), preferred_element_type=F32)


def normalise(source):
    mean_val = jnp.mean(source, axis=-1, keepdims=True)
    centred = source - mean_val
    inv_std = lax.rsqrt(jnp.mean(centred * centred, axis=-1, keepdims=True) + EPS_NORM)
    return centred * inv_std, inv_std


def norm_back(grad_out, normed, inv_std, gain_row):
    scaled = grad_out * gain_row
    inner = (
        scaled
        - jnp.mean(scaled, axis=-1, keepdims=True)
        - normed * jnp.mean(scaled * normed, axis=-1, keepdims=True)
    )
    return inner * inv_std


def col_sum(value):
    return jnp.sum(value, axis=0, keepdims=True)


class Gather:
    def __init__(self, cp, buf, base, place, off, rows):
        self.cp, self.buf, self.b = cp, buf, base
        self.s, self.px, self.py, self.pd = place
        self.off, self.h = off, rows // 2

    def top(self, slot):
        return self.buf.at[slot, pl.ds(self.off, self.h)]

    def bot(self, slot):
        return self.buf.at[slot, pl.ds(self.off + self.h, self.h)]

    def c(self, part, slot, i, to):
        ref = part(slot)
        return self.cp(ref, ref, self.b + i, to)

    def start(self):
        self.c(self.top, self.s, 0, self.px).start()
        self.c(self.bot, self.s, 2, self.py).start()
        self.c(self.bot, self.s, 1, self.px).start()
        self.c(self.top, self.s, 3, self.py).start()

    def relay(self):
        self.c(self.top, self.px, 0, self.px).wait_recv()
        self.c(self.top, self.px, 4, self.py).start()
        self.c(self.bot, self.py, 2, self.py).wait_recv()
        self.c(self.bot, self.py, 5, self.px).start()

    def wait_x(self):
        self.c(self.bot, self.px, 1, self.px).wait_recv()

    def wait_y(self):
        self.c(self.top, self.py, 3, self.py).wait_recv()

    def wait_d(self):
        self.c(self.top, self.pd, 4, self.py).wait_recv()
        self.c(self.bot, self.pd, 5, self.px).wait_recv()

    def sent(self):
        for part, slot, i, to in (
            (self.top, self.s, 0, self.px),
            (self.bot, self.s, 2, self.py),
            (self.bot, self.s, 1, self.px),
            (self.top, self.s, 3, self.py),
            (self.top, self.px, 4, self.py),
            (self.bot, self.py, 5, self.px),
        ):
            self.c(part, slot, i, to).wait_send()


class Scatter:
    def __init__(self, cp, part, in_x, in_y, via_x, via_y, base, place):
        _, px, py, _ = place
        h = in_x.shape[0] // 2
        top, bot = pl.ds(0, h), pl.ds(h, h)
        self.part, self.via_x, self.via_y, self.h = part, via_x, via_y, h
        self.copies = [
            cp(part.at[2, top], via_x, base, px),
            cp(part.at[2, bot], via_y, base + 1, py),
            cp(part.at[0, top], in_x.at[top], base + 2, px),
            cp(part.at[1, bot], in_y.at[bot], base + 3, py),
            cp(part.at[1, top], in_y.at[top], base + 4, py),
            cp(part.at[0, bot], in_x.at[bot], base + 5, px),
        ]

    def start(self, relation):
        for i in {3: (0, 1), 1: (2,), 2: (3,)}[relation]:
            self.copies[i].start()

    def relay_y(self):
        self.copies[0].wait_recv()
        self.part[1, : self.h, :] = (self.part[1, : self.h, :].astype(F32) + self.via_x[...].astype(F32)).astype(BF16)
        self.copies[4].start()

    def relay_x(self):
        self.copies[1].wait_recv()
        self.part[0, self.h :, :] = (self.part[0, self.h :, :].astype(F32) + self.via_y[...].astype(F32)).astype(BF16)
        self.copies[5].start()

    def wait(self):
        for i in (2, 3, 4, 5):
            self.copies[i].wait_recv()

    def sent(self):
        for copy in self.copies:
            copy.wait_send()


class Line:
    def __init__(self, cp_dp, buf, base, chip, core, chips):
        self.cp, self.buf, self.b = cp_dp, buf, base
        self.z, self.core, self.n = chip, core, chips

    def c(self, shard, kind, to):
        at = 2 * shard + self.core
        return self.cp(self.buf.at[at], self.buf.at[at], self.b + kind * self.n + shard, to)

    def up(self, shard):
        return self.c(shard, 0, 2 * (self.z + 1) + self.core)

    def down(self, shard):
        return self.c(shard, 1, 2 * (self.z - 1) + self.core)

    def across(self, shard):
        return self.c(shard, 2, 2 * self.z + 1 - self.core)

    def start_up(self):
        @pl.when(self.z < self.n - 1)
        def _():
            self.up(self.z).start()

    def start_down(self):
        @pl.when(self.z > 0)
        def _():
            self.down(self.z).start()

    def start(self):
        self.start_up()
        self.start_down()
        self.across(self.z).start()

    def step(self, k):
        low, high = self.z - k, self.z + k

        @pl.when(low >= 0)
        def _():
            self.c(low, 0, 2 * self.z + 1 - self.core).wait_recv()

            @pl.when(self.z < self.n - 1)
            def _():
                self.up(low).start()

            self.across(low).start()

        @pl.when(high < self.n)
        def _():
            self.c(high, 1, 2 * self.z + 1 - self.core).wait_recv()

            @pl.when(self.z > 0)
            def _():
                self.down(high).start()

            self.across(high).start()

    def crossed(self, shard):
        other = 1 - self.core
        ref = self.buf.at[2 * shard + other]
        self.cp(ref, ref, self.b + 2 * self.n + shard, 2 * self.z + other).wait_recv()

    def sent(self):
        for shard in range(self.n):
            self.across(shard).wait_send()

            @pl.when(jnp.logical_and(shard <= self.z, self.z < self.n - 1))
            def _(shard=shard):
                self.up(shard).wait_send()

            @pl.when(jnp.logical_and(shard >= self.z, self.z > 0))
            def _(shard=shard):
                self.down(shard).wait_send()


class LineSum:
    def __init__(self, cp_dp, part, cross, landed, base, chip, core, chips):
        self.cp, self.part, self.cross, self.landed, self.b = cp_dp, part, cross, landed, base
        self.z, self.core, self.n = chip, core, chips

    def mine(self, shard):
        return 2 * shard + self.core

    def across(self, shard):
        src = self.part.at[2 * shard + 1 - self.core]
        return self.cp(src, self.cross.at[shard], self.b + shard, 2 * self.z + 1 - self.core)

    def up(self, shard):
        src = self.part.at[self.mine(shard)]
        return self.cp(src, self.landed.at[shard + 1], self.b + self.n + shard, 2 * (self.z + 1) + self.core)

    def down(self, shard):
        src = self.part.at[self.mine(shard)]
        return self.cp(src, self.landed.at[shard], self.b + 2 * self.n + shard, 2 * (self.z - 1) + self.core)

    def start(self, shard):
        self.across(shard).start()

    def add(self, shard, ref):
        size = min(256, ref.shape[0])

        def one(i, carry):
            at = pl.ds(pl.multiple_of(i * size, size), size)
            total = self.part[self.mine(shard), at, :].astype(F32) + ref[at, :].astype(F32)
            self.part[self.mine(shard), at, :] = total.astype(BF16)
            return carry

        lax.fori_loop(0, ref.shape[0] // size, one, 0)

    def fold(self, shard):
        self.across(shard).wait_recv()
        self.add(shard, self.cross.at[shard])

    def step(self, k):
        if k > self.n - 2:
            return
        up, down = self.n - 1 - k + self.z, k - (self.n - 1 - self.z)

        @pl.when(k >= self.z)
        def _():
            @pl.when(k > self.z)
            def _():
                self.up(up + 1).wait_send()

            @pl.when(self.z > 0)
            def _():
                self.up(up).wait_recv()
                self.add(up, self.landed.at[up + 1])

            self.up(up).start()

        @pl.when(k >= self.n - 1 - self.z)
        def _():
            @pl.when(k > self.n - 1 - self.z)
            def _():
                self.down(down - 1).wait_send()

            @pl.when(self.z < self.n - 1)
            def _():
                self.down(down).wait_recv()
                self.add(down, self.landed.at[down])

            self.down(down).start()

    def finish(self, owned):
        owned[...] = self.part[self.mine(self.z)].astype(F32)

        @pl.when(self.z > 0)
        def _():
            self.up(self.z).wait_recv()
            owned[...] += self.landed[self.z + 1].astype(F32)

        @pl.when(self.z < self.n - 1)
        def _():
            self.down(self.z).wait_recv()
            owned[...] += self.landed[self.z].astype(F32)

    def sent(self):
        for shard in range(self.n):
            self.across(shard).wait_send()

        @pl.when(self.z < self.n - 1)
        def _():
            self.up(self.z + 1).wait_send()

        @pl.when(self.z > 0)
        def _():
            self.down(self.z - 1).wait_send()


class Everyone:
    def __init__(self, cp_any, plane, line, base, s, chip, core, chips):
        self.cp, self.plane, self.line, self.b = cp_any, plane, line, base
        self.s, self.z, self.core, self.n = s, chip, core, chips
        self.me = 2 * s + core

    def to_plane(self, o):
        p = lax.rem(self.me + o, 8)
        return self.cp(self.plane.at[self.me], self.plane.at[self.me], self.b + o, p // 2, 2 * self.z + lax.rem(p, 2))

    def from_plane(self, o):
        p = lax.rem(self.me - o + 8, 8)
        return self.cp(self.plane.at[p], self.plane.at[p], self.b + o, p // 2, 2 * self.z + lax.rem(p, 2))

    def to_line(self, o):
        p = lax.rem(self.z + o, self.n)
        return self.cp(self.line.at[self.z], self.line.at[self.z], self.b + 7 + o, self.s, 2 * p + self.core)

    def from_line(self, o):
        p = lax.rem(self.z - o + self.n, self.n)
        return self.cp(self.line.at[p], self.line.at[p], self.b + 7 + o, self.s, 2 * p + self.core)

    def start(self, value):
        self.plane[self.me] = value
        for o in range(1, 8):
            self.to_plane(o).start()

    def middle(self):
        for o in range(1, 8):
            self.from_plane(o).wait_recv()
        total = self.plane[0]
        for p in range(1, 8):
            total = total + self.plane[p]
        self.line[self.z] = total
        for o in range(1, self.n):
            self.to_line(o).start()

    def end(self):
        for o in range(1, self.n):
            self.from_line(o).wait_recv()
        total = self.line[0]
        for p in range(1, self.n):
            total = total + self.line[p]
        return total

    def sent(self):
        for o in range(1, 8):
            self.to_plane(o).wait_send()
        for o in range(1, self.n):
            self.to_line(o).wait_send()


def layer_kernel(inside, chips, *refs):
    refs = list(refs)

    def take(count):
        head = refs[:count]
        del refs[:count]
        return head

    frames, mask_col, cot, seg_q, seg_k, vec, attn_src, ffn_src = take(8)
    if inside:
        out, frames_grad, vec_out, norm_out, attn_owned, ffn_owned = take(6)
    else:
        out, frames_grad, early, late, g_attn, g_ffn = take(6)
        w_attn, w_ffn = attn_src, ffn_src
    fr_g, cot_g, a_g, wp, qa, ka, va, kt, att, b_g, gp_g = take(11)
    act_g = fr_g
    resid, own, part, in_x, in_y, via_x, via_y, in_x2, in_y2, via_x2, via_y2 = take(11)
    gsend, gm, dom, ga_g, gres, dqkv, dk_acc, dv_acc, send_sem, recv_sem, local_sem = take(11)
    if inside:
        w_attn, w_ffn, g_attn, g_ffn, cross_a, cross_f, landed_a, landed_f, early, late, planes, lines = take(12)
    s = lax.axis_index("seq")
    d = lax.axis_index("dp")
    core = lax.rem(d, 2)
    sib = d + 1 - 2 * core

    def peer(r):
        high = lax.rem(s // 2 + r // 2, 2)
        low = lax.rem(lax.rem(s, 2) + r % 2, 2)
        return 2 * high + low

    px, py, pd = peer(1), peer(2), peer(3)
    place = (s, px, py, pd)

    def cp(src, dst, i, to):
        return pltpu.make_async_remote_copy(
            src_ref=src,
            dst_ref=dst,
            send_sem=send_sem.at[i],
            recv_sem=recv_sem.at[i],
            device_id=(to, d),
            device_id_type=MESH,
        )

    def cp_any(src, dst, i, to_seq, to_dp):
        return pltpu.make_async_remote_copy(
            src_ref=src,
            dst_ref=dst,
            send_sem=send_sem.at[i],
            recv_sem=recv_sem.at[i],
            device_id=(to_seq, to_dp),
            device_id_type=MESH,
        )

    def cp_dp(src, dst, i, to):
        return cp_any(src, dst, i, s, to)

    def cp_sib(src, dst, i):
        return cp_any(src, dst, i, s, sib)

    def no_step(k):
        return None

    rows = frames.shape[0]
    width = frames.shape[1]
    local = width // 4
    slab_a = w_attn.shape[2]
    slab_f = w_ffn.shape[2]
    per_a = width // slab_a
    per_f = width // slab_f
    tile = 256
    chunk = 32

    cot_load = pltpu.make_async_copy(cot, cot_g.at[s], local_sem.at[0])
    cot_load.start()
    chip = d // 2
    loads = []
    if inside:
        loads = [pltpu.make_async_copy(attn_src, own.at[:, :slab_a], local_sem.at[1])]
        for i, spot in enumerate((dk_acc, dv_acc)):
            at = slice(i * LANES, (i + 1) * LANES)
            loads.append(pltpu.make_async_copy(ffn_src.at[:, at], spot, local_sem.at[2 + i]))
        for load in loads:
            load.start()

    barrier = pltpu.get_barrier_semaphore()
    if inside:
        for o in range(1, 8):
            p = lax.rem(2 * s + core + o, 8)
            to = (p // 2, 2 * chip + lax.rem(p, 2))
            pl.semaphore_signal(barrier, inc=1, device_id=to, device_id_type=MESH)
        for o in range(1, chips):
            to = (s, 2 * lax.rem(chip + o, chips) + core)
            pl.semaphore_signal(barrier, inc=1, device_id=to, device_id_type=MESH)
        pl.semaphore_wait(barrier, 6 + chips)
    else:
        for to in (px, py, pd):
            pl.semaphore_signal(barrier, inc=1, device_id=(to, d), device_id_type=MESH)
        pl.semaphore_signal(barrier, inc=1, device_id=(s, sib), device_id_type=MESH)
        pl.semaphore_wait(barrier, 4)

    fr_g[s] = frames[...]
    frames_in = Gather(cp, fr_g, 0, place, 0, rows)
    frames_in.start()
    cot_in = Gather(cp, cot_g, 15, place, 0, rows)
    attn_step = ffn_step = no_step
    if inside:
        line_a = Line(cp_dp, w_attn, 60, chip, core, chips)
        line_f = Line(cp_dp, w_ffn, 60 + 3 * chips, chip, core, chips)
        loads[0].wait()
        w_attn[d] = own[:, :slab_a].astype(BF16)
        line_a.start()
        attn_step, ffn_step = line_a.step, line_f.step
    half = rows // 2
    wp_off = pl.multiple_of(core * half, half)
    wp_in = Gather(cp, wp, 6, place, wp_off, half)
    wp_cross = [
        cp_sib(wp.at[p, pl.ds(wp_off, half)], wp.at[p, pl.ds(wp_off, half)], 12 + i) for i, p in enumerate((px, py, pd))
    ]
    early[...] = jnp.zeros_like(early)
    late[...] = jnp.zeros_like(late)
    half = rows // 2

    lane = lax.broadcasted_iota(jnp.int32, (rows, LANES), 1)
    low_head = lane < LANES // 2
    q_bias = vec[2:3, pl.ds(pl.multiple_of(s * local, local), local)]
    v_bias = vec[3:4, pl.ds(pl.multiple_of(s * local, local), local)]

    def weight_rows(first, count, start, size):
        return jnp.concatenate([w_attn[first + i, start : start + size, :] for i in range(count)], axis=1)

    def enter(blk):
        def norm_rows(i, carry):
            at = pl.ds(pl.multiple_of(i * chunk, chunk), chunk)
            at_all = pl.ds(pl.multiple_of(blk * rows + i * chunk, chunk), chunk)
            x = jnp.where(mask_col[at_all, :] > 0.0, vec[8:9, :], fr_g[blk, at, :].astype(F32))
            normed, _ = normalise(x)
            a_g[blk, at, :] = (normed * vec[0:1, :] + vec[1:2, :]).astype(BF16)
            return carry

        lax.fori_loop(0, rows // chunk, norm_rows, 0)

    def project_in(blk):
        a = a_g[blk]
        at_all = pl.ds(pl.multiple_of(blk * rows, rows), rows)
        q = (nt(a, weight_rows(0, per_a, 0, local)) + q_bias).astype(BF16).astype(F32) * 0.125
        for pair in range(2):
            both = q[:, pair * LANES : (pair + 1) * LANES]
            for h in range(2):
                keep = low_head if h == 0 else jnp.logical_not(low_head)
                qa[2 * pair + h, blk, :, :LANES] = jnp.where(keep, both, 0.0).astype(BF16)
                qa[2 * pair + h, blk, :, LANES:] = seg_q[at_all, :]
        k = nt(a, weight_rows(per_a, per_a, 0, local)).astype(BF16)
        for pair in range(2):
            both = k[:, pair * LANES : (pair + 1) * LANES]
            ka[pair, at_all, :LANES] = both
            ka[pair, at_all, LANES:] = seg_k[at_all, :]
            kt[pair, :, at_all] = jnp.transpose(both)
        v = (nt(a, weight_rows(2 * per_a, per_a, 0, local)) + v_bias).astype(BF16)
        for pair in range(2):
            va[pair, at_all, :] = v[:, pair * LANES : (pair + 1) * LANES]

    enter(s)
    if inside:
        for i, spot in enumerate((dk_acc, dv_acc)):
            loads[1 + i].wait()
            w_ffn[d, :, i * LANES : (i + 1) * LANES] = spot[...].astype(BF16)
    attn_step(1)
    frames_in.relay()
    attn_step(2)
    frames_in.wait_x()
    enter(px)
    frames_in.wait_y()
    enter(py)
    attn_step(3)
    if inside:
        line_f.start()
    frames_in.wait_d()
    enter(pd)
    if inside:
        for shard in range(chips):
            line_a.crossed(shard)
    for i in range(per_a):
        wp[s, :, i * slab_a : (i + 1) * slab_a] = w_attn[3 * per_a + i]
    wp_in.start()
    lax.fori_loop(0, 4, lambda j, carry: (project_in(j), carry)[1], 0)
    wp_in.relay()
    cot_load.wait()
    cot_in.start()

    def att_x(j, slot):
        return cp(att.at[slot, j], att.at[slot, j], 21 + j, px)

    def att_y(j, slot):
        return cp(att.at[slot, j], att.at[slot, j], 25 + j, py)

    def att_relay(j, start):
        even = lax.rem(j, 2) == 0

        @pl.when(even)
        def _():
            if start:
                att_x(j, px).wait_recv()
                cp(att.at[px, j], att.at[px, j], 29 + j, py).start()
            else:
                cp(att.at[px, j], att.at[px, j], 29 + j, py).wait_send()

        @pl.when(jnp.logical_not(even))
        def _():
            if start:
                att_y(j, py).wait_recv()
                cp(att.at[py, j], att.at[py, j], 29 + j, px).start()
            else:
                cp(att.at[py, j], att.at[py, j], 29 + j, px).wait_send()

    def attend(j, carry):
        for pair in range(2):
            outs = []
            for h in range(2):
                head = 2 * pair + h
                scores = nt(qa[head, j], ka[pair])
                peak = jnp.max(scores, axis=-1, keepdims=True)
                terms = jnp.exp(scores - peak)
                total = jnp.sum(terms, axis=-1, keepdims=True)
                probs = (terms * (1.0 / total)).astype(BF16)
                outs.append(nn(probs, va[pair]))
                log_total = -(peak + jnp.log(total))
                part_one = log_total.astype(BF16).astype(F32)
                rest = log_total - part_one
                part_two = rest.astype(BF16).astype(F32)
                part_three = rest - part_two
                aug = qa[head, j, :, LANES:].astype(F32)
                aug = jnp.where(lane == 2, part_one, aug)
                aug = jnp.where(lane == 3, part_two, aug)
                aug = jnp.where(lane == 4, part_three, aug)
                qa[head, j, :, LANES:] = aug.astype(BF16)
            att[s, j, :, pair * LANES : (pair + 1) * LANES] = jnp.where(low_head, outs[0], outs[1]).astype(BF16)
        att_x(j, s).start()
        att_y(j, s).start()

        @pl.when(j > 0)
        def _():
            att_relay(j - 1, True)

        return carry

    lax.fori_loop(0, 3, attend, 0)
    ffn_step(1)
    lax.fori_loop(3, 4, attend, 0)
    att_relay(3, True)
    wp_in.wait_x()
    wp_cross[0].start()
    wp_in.wait_y()
    wp_cross[1].start()
    wp_in.wait_d()
    wp_cross[2].start()
    cot_in.relay()
    other_off = pl.multiple_of((1 - core) * half, half)
    for i, p in enumerate((px, py, pd)):
        cp_sib(wp.at[p, pl.ds(other_off, half)], wp.at[p, pl.ds(other_off, half)], 12 + i).wait_recv()

    def project(j, carry):
        even = lax.rem(j, 2) == 0

        @pl.when(even)
        def _():
            att_y(j, py).wait_recv()
            cp(att.at[pd, j], att.at[pd, j], 29 + j, py).wait_recv()

        @pl.when(jnp.logical_not(even))
        def _():
            att_x(j, px).wait_recv()
            cp(att.at[pd, j], att.at[pd, j], 29 + j, px).wait_recv()

        left = jnp.concatenate([att[p, j] for p in range(4)], axis=1)
        for i in range(width // tile):
            right = jnp.concatenate([wp[p, :, i * tile : (i + 1) * tile] for p in range(4)], axis=0)
            own[:, i * tile : (i + 1) * tile] = nn(left, right)

        def norm_rows(i, inner):
            at = pl.ds(pl.multiple_of(i * chunk, chunk), chunk)
            at_all = pl.ds(pl.multiple_of(j * rows + i * chunk, chunk), chunk)
            x = jnp.where(mask_col[at_all, :] > 0.0, vec[8:9, :], fr_g[j, at, :].astype(F32))
            total = x + own[at, :] + vec[4:5, :]

            @pl.when(j == s)
            def _():
                resid[at, :] = total

            normed, _ = normalise(total)
            b_g[j, at, :] = (normed * vec[5:6, :] + vec[6:7, :]).astype(BF16)
            return inner

        lax.fori_loop(0, rows // chunk, norm_rows, 0)
        return carry

    lax.fori_loop(0, 3, project, 0)
    ffn_step(2)
    lax.fori_loop(3, 4, project, 0)
    ffn_step(3)
    if inside:
        for shard in range(chips):
            line_f.crossed(shard)

    def feed(r):
        blk = peer(r)

        def hidden_tile(i, carry):
            at = pl.ds(pl.multiple_of(i * tile, tile), tile)
            w_in = jnp.concatenate([w_ffn[k, at, :] for k in range(per_f)], axis=1)
            w_out = jnp.concatenate([w_ffn[per_f + k, at, :] for k in range(per_f)], axis=1)
            pre = nt(b_g[blk], w_in) + vec[pl.ds(9 + s, 1), at]
            grad_act = nt(cot_g[blk], w_out)
            cdf = 0.5 * (1.0 + lax.erf(pre * 0.7071067811865476))
            act_g[blk, :, at] = (pre * cdf).astype(BF16)
            density = jnp.exp(-0.5 * pre * pre) * 0.3989422804014327
            grad_pre = ((cdf + pre * density) * grad_act).astype(BF16)
            gp_g[blk, :, at] = grad_pre
            early[pl.ds(4 + s, 1), at] += col_sum(grad_pre.astype(F32))
            return carry

        lax.fori_loop(0, w_ffn.shape[1] // tile, hidden_tile, 0)
        left = gp_g[blk]
        for k in range(per_f):
            at = slice(k * slab_f, (k + 1) * slab_f)
            value = nn(left, w_ffn[k])
            if r == 0:
                own[:, at] = value
            else:
                part[r - 1, :, at] = value.astype(BF16)

    sum_b = Scatter(cp, part, in_x, in_y, via_x, via_y, 33, place)
    cot_in.wait_x()
    cot_in.wait_y()
    cot_in.wait_d()
    frames_in.sent()
    feed(3)
    sum_b.start(3)
    feed(1)
    sum_b.start(1)
    feed(2)
    sum_b.start(2)
    sum_b.relay_y()
    sum_b.relay_x()
    feed(0)
    sum_b.wait()

    def back_two(i, carry):
        at = pl.ds(pl.multiple_of(i * chunk, chunk), chunk)
        grad_b = own[at, :] + in_x[at, :].astype(F32) + in_y[at, :].astype(F32)
        normed, inv_std = normalise(resid[at, :])
        grad_y = cot_g[s, at, :].astype(F32)
        grad_resid = grad_y + norm_back(grad_b, normed, inv_std, vec[5:6, :])
        gres[at, :] = grad_resid
        low = grad_resid.astype(BF16)
        ga_g[s, at, :] = low
        early[0:1, :] += col_sum(low.astype(F32))
        early[1:2, :] += col_sum(grad_b * normed)
        early[2:3, :] += col_sum(grad_b)
        early[3:4, :] += col_sum(grad_y)
        return carry

    lax.fori_loop(0, rows // chunk, back_two, 0)

    for i, r in enumerate((3, 1, 2)):
        gsend[r] = nt(ga_g[s], wp[peer(r)]).astype(BF16)
        cp(gsend.at[r], gm.at[s], 39 + i, peer(r)).start()
    gm[s] = nt(ga_g[s], wp[s]).astype(BF16)
    ga_in = Gather(cp, ga_g, 42, place, 0, rows)
    ga_in.start()
    sum_b.sent()

    sum_o = Scatter(cp, part, in_x2, in_y2, via_x2, via_y2, 48, place)

    def out_part(blk, k):
        return nn(act_g[blk], w_ffn[per_f + k])

    for r in (3, 1, 2):
        for k in range(per_f):
            part[r - 1, :, k * slab_f : (k + 1) * slab_f] = out_part(peer(r), k).astype(BF16)
        sum_o.start(r)

    def ffn_grads(i, carry):
        at = pl.ds(pl.multiple_of(i * tile, tile), tile)
        for left, right, first in ((gp_g, b_g, 0), (act_g, cot_g, per_f)):
            turned = jnp.transpose(jnp.concatenate([left[p, :, at] for p in range(4)], axis=0))
            for k in range(per_f):
                cols = jnp.concatenate([right[p, :, k * slab_f : (k + 1) * slab_f] for p in range(4)], axis=0)
                g_ffn[first + k, at, :] = nn(turned, cols).astype(BF16)
        return carry

    lax.fori_loop(0, w_ffn.shape[1] // tile, ffn_grads, 0)
    sum_step = no_step
    if inside:
        sum_f = LineSum(cp_dp, g_ffn, cross_f, landed_f, 60 + 6 * chips, chip, core, chips)
        sum_g = LineSum(cp_dp, g_attn, cross_a, landed_a, 60 + 9 * chips, chip, core, chips)
        all_early = Everyone(cp_any, planes.at[0], lines.at[0], 60 + 12 * chips, s, chip, core, chips)
        all_late = Everyone(cp_any, planes.at[1], lines.at[1], 67 + 13 * chips, s, chip, core, chips)
        sum_step = sum_f.step
        for shard in range(chips):
            sum_f.start(shard)
        all_early.start(early[...])

    for i, r in enumerate((3, 1, 2)):
        cp(gsend.at[r], gm.at[peer(r)], 39 + i, peer(r)).wait_recv()

    def spread(j, carry):
        for pair in range(2):
            both = gm[j, :, pair * LANES : (pair + 1) * LANES].astype(F32)
            dom[2 * pair, j] = jnp.where(low_head, both, 0.0).astype(BF16)
            dom[2 * pair + 1, j] = jnp.where(low_head, 0.0, both).astype(BF16)
        return carry

    lax.fori_loop(0, 4, spread, 0)
    if inside:
        for shard in range(chips):
            sum_f.fold(shard)
    sum_step(0)
    ga_in.relay()
    sum_o.relay_y()
    sum_o.relay_x()
    if inside:
        all_early.middle()

    def back_pair(pair):
        dk_acc[...] = jnp.zeros_like(dk_acc)
        dv_acc[...] = jnp.zeros_like(dv_acc)

        def back_block(j, carry):
            sides = []
            for h in range(2):
                head = 2 * pair + h
                probs = jnp.exp(nt(ka[pair], qa[head, j]))
                grad_probs = nt(va[pair], dom[head, j])
                delta = jnp.sum(probs * grad_probs, axis=0, keepdims=True)
                grad_scores = (probs * (grad_probs - delta)).astype(BF16)
                dv_acc[...] += nn(probs.astype(BF16), dom[head, j])
                dk_acc[...] += nn(grad_scores, qa[head, j, :, :LANES])
                sides.append(nn(kt[pair], grad_scores))
            half_lane = LANES // 2
            turned = jnp.concatenate([sides[0][:half_lane], sides[1][half_lane:]], axis=0)
            dqkv[0, j, :, pair * LANES : (pair + 1) * LANES] = (jnp.transpose(turned) * 0.125).astype(BF16)
            return carry

        lax.fori_loop(0, 4, back_block, 0)
        for j in range(4):
            at = slice(j * rows, (j + 1) * rows)
            dqkv[1, j, :, pair * LANES : (pair + 1) * LANES] = dk_acc[at, :].astype(BF16)
            dqkv[2, j, :, pair * LANES : (pair + 1) * LANES] = dv_acc[at, :].astype(BF16)

    back_pair(0)
    sum_step(1)
    back_pair(1)
    sum_step(2)

    sum_o.sent()
    sum_a = Scatter(cp, part, in_x, in_y, via_x, via_y, 54, place)

    def grad_in(r):
        blk = peer(r)
        left = jnp.concatenate([dqkv[c, blk] for c in range(3)], axis=1)
        for k in range(per_a):
            at = slice(k * slab_a, (k + 1) * slab_a)
            right = jnp.concatenate([w_attn[c * per_a + k] for c in range(3)], axis=0)
            value = nn(left, right)
            if r == 0:
                own[:, at] = value
            else:
                part[r - 1, :, at] = value.astype(BF16)

    sum_o.wait()
    for k in range(per_f):
        at = slice(k * slab_f, (k + 1) * slab_f)
        total = out_part(s, k) + resid[:, at] + in_x2[:, at].astype(F32) + in_y2[:, at].astype(F32) + vec[7:8, at]
        out[:, at] = total.astype(BF16)

    for r in (3, 1, 2):
        grad_in(r)
        sum_a.start(r)
    grad_in(0)

    my_cols = pl.ds(pl.multiple_of(s * local, local), local)
    for j in range(4):
        late[2:3, my_cols] += col_sum(dqkv[0, j].astype(F32))
        late[3:4, my_cols] += col_sum(dqkv[2, j].astype(F32))

    def attn_grads(c):
        turned = jnp.transpose(jnp.concatenate([dqkv[c, p] for p in range(4)], axis=0))
        for k in range(per_a):
            cols = jnp.concatenate([a_g[p, :, k * slab_a : (k + 1) * slab_a] for p in range(4)], axis=0)
            g_attn[c * per_a + k] = nn(turned, cols).astype(BF16)

    attn_grads(0)
    attn_grads(1)
    sum_a.relay_y()
    sum_a.relay_x()
    attn_grads(2)
    ga_in.wait_x()
    ga_in.wait_y()
    ga_in.wait_d()
    turned = jnp.transpose(jnp.concatenate([att[s, p] for p in range(4)], axis=0))
    for k in range(per_a):
        cols = jnp.concatenate([ga_g[p, :, k * slab_a : (k + 1) * slab_a] for p in range(4)], axis=0)
        g_attn[3 * per_a + k] = nn(turned, cols).astype(BF16)

    if inside:
        for shard in range(chips):
            sum_g.start(shard)
        sum_f.finish(ffn_owned)
        for shard in range(chips):
            sum_g.fold(shard)
        sum_g.step(0)
    sum_a.wait()

    def back_one(i, carry):
        at = pl.ds(pl.multiple_of(i * chunk, chunk), chunk)
        at_all = pl.ds(pl.multiple_of(s * rows + i * chunk, chunk), chunk)
        grad_a = own[at, :] + in_x[at, :].astype(F32) + in_y[at, :].astype(F32)
        masked = mask_col[at_all, :] > 0.0
        normed, inv_std = normalise(jnp.where(masked, vec[8:9, :], frames[at, :].astype(F32)))
        grad_x = gres[at, :] + norm_back(grad_a, normed, inv_std, vec[0:1, :])
        frames_grad[at, :] = jnp.where(masked, 0.0, grad_x)
        late[0:1, :] += col_sum(grad_a * normed)
        late[1:2, :] += col_sum(grad_a)
        late[4:5, :] += col_sum(jnp.where(masked, grad_x, 0.0))
        return carry

    lax.fori_loop(0, rows // chunk, back_one, 0)
    if inside:
        sum_g.step(1)
        sum_g.step(2)
        sum_g.finish(attn_owned)
        late[5:6, :slab_a] = col_sum(attn_owned[...] * attn_owned[...])
        late[5:6, slab_a : slab_a + slab_f] = col_sum(ffn_owned[...] * ffn_owned[...])
        all_late.start(late[...])
        whole_early = all_early.end()
        all_late.middle()
        whole_late = all_late.end()
        vec_out[0:4, :] = whole_late[0:4]
        vec_out[4:8, :] = whole_early[0:4]
        vec_out[8:9, :] = whole_late[4:5]
        vec_out[9:13, :] = whole_early[4:8]
        vec_square = vec_out[...] * vec_out[...]
        total = jnp.sum(col_sum(vec_square) + whole_late[5:6], axis=1, keepdims=True)
        norm_out[...] = jnp.broadcast_to(jnp.sqrt(total), norm_out.shape)
        line_a.sent()
        line_f.sent()
        sum_f.sent()
        sum_g.sent()
        all_early.sent()
        all_late.sent()

    wp_in.sent()
    for copy in wp_cross:
        copy.wait_send()
    cot_in.sent()

    def att_sent(j, carry):
        att_x(j, s).wait_send()
        att_y(j, s).wait_send()
        att_relay(j, False)
        return carry

    lax.fori_loop(0, 4, att_sent, 0)
    for i, r in enumerate((3, 1, 2)):
        cp(gsend.at[r], gm.at[s], 39 + i, peer(r)).wait_send()
    ga_in.sent()
    sum_a.sent()


def run_layer(frames, mask_col, cot, seg_q, seg_k, vec, attn_src, ffn_src, inside, chips):
    rows, width = frames.shape
    group = 4 * rows
    local = width // 4
    slab_count = 2 * chips if inside else SLABS
    hidden = ffn_src.shape[0] if inside else ffn_src.shape[1]
    attn_shape = (slab_count, local, attn_src.shape[-1])
    ffn_shape = (slab_count, hidden, ffn_src.shape[-1])
    vmem = pl.BlockSpec(memory_space=pltpu.VMEM)
    anywhere = pl.BlockSpec(memory_space=pl.ANY)
    source = anywhere if inside else vmem
    block = (4, rows, width)
    sums = (8, width)
    scratch = [
        pltpu.VMEM(block, BF16),
        pltpu.VMEM(block, BF16),
        pltpu.VMEM(block, BF16),
        pltpu.VMEM((4, local, width), BF16),
        pltpu.VMEM((4, 4, rows, 2 * LANES), BF16),
        pltpu.VMEM((2, group, 2 * LANES), BF16),
        pltpu.VMEM((2, group, LANES), BF16),
        pltpu.VMEM((2, LANES, group), BF16),
        pltpu.VMEM((4, 4, rows, local), BF16),
        pltpu.VMEM(block, BF16),
        pltpu.VMEM((4, rows, hidden), BF16),
        pltpu.VMEM((rows, width), F32),
        pltpu.VMEM((rows, width), F32),
        pltpu.VMEM((3, rows, width), BF16),
        pltpu.VMEM((rows, width), BF16),
        pltpu.VMEM((rows, width), BF16),
        pltpu.VMEM((rows // 2, width), BF16),
        pltpu.VMEM((rows // 2, width), BF16),
        pltpu.VMEM((rows, width), BF16),
        pltpu.VMEM((rows, width), BF16),
        pltpu.VMEM((rows // 2, width), BF16),
        pltpu.VMEM((rows // 2, width), BF16),
        pltpu.VMEM((4, rows, local), BF16),
        pltpu.VMEM((4, rows, local), BF16),
        pltpu.VMEM((4, 4, rows, LANES), BF16),
        pltpu.VMEM(block, BF16),
        pltpu.VMEM((rows, width), F32),
        pltpu.VMEM((3, 4, rows, local), BF16),
        pltpu.VMEM((group, LANES), F32),
        pltpu.VMEM((group, LANES), F32),
    ]
    sem_count = 75 + 14 * chips if inside else 60
    scratch += [pltpu.SemaphoreType.DMA((sem_count,)), pltpu.SemaphoreType.DMA((sem_count,))]
    scratch.append(pltpu.SemaphoreType.DMA((4,)))
    if inside:
        scratch += [
            pltpu.VMEM(attn_shape, BF16),
            pltpu.VMEM(ffn_shape, BF16),
            pltpu.VMEM(attn_shape, BF16),
            pltpu.VMEM(ffn_shape, BF16),
            pltpu.VMEM((chips, *attn_shape[1:]), BF16),
            pltpu.VMEM((chips, *ffn_shape[1:]), BF16),
            pltpu.VMEM((chips + 1, *attn_shape[1:]), BF16),
            pltpu.VMEM((chips + 1, *ffn_shape[1:]), BF16),
            pltpu.VMEM(sums, F32),
            pltpu.VMEM(sums, F32),
            pltpu.VMEM((2, 8, *sums), F32),
            pltpu.VMEM((2, chips, *sums), F32),
        ]
        last = (
            jax.ShapeDtypeStruct(vec.shape, F32),
            jax.ShapeDtypeStruct((8, LANES), F32),
            jax.ShapeDtypeStruct(attn_shape[1:], F32),
            jax.ShapeDtypeStruct(ffn_shape[1:], F32),
        )
    else:
        last = (
            jax.ShapeDtypeStruct(sums, F32),
            jax.ShapeDtypeStruct(sums, F32),
            jax.ShapeDtypeStruct(attn_shape, BF16),
            jax.ShapeDtypeStruct(ffn_shape, BF16),
        )
    return pl.pallas_call(
        functools.partial(layer_kernel, inside, chips),
        out_shape=(jax.ShapeDtypeStruct((rows, width), BF16), jax.ShapeDtypeStruct((rows, width), F32), *last),
        in_specs=[vmem, vmem, anywhere, vmem, vmem, vmem, source, source],
        out_specs=(vmem,) * 6,
        scratch_shapes=scratch,
        compiler_params=pltpu.CompilerParams(
            collective_id=0, has_side_effects=True, vmem_limit_bytes=VMEM_LIMIT
        ),
    )(frames, mask_col, cot, seg_q, seg_k, vec, attn_src, ffn_src)


def per_device(
    frames,
    segment_ids,
    span_starts,
    cotangent,
    attn_master,
    attn_first,
    attn_second,
    ffn_master,
    ffn_first,
    ffn_second,
    vec_master,
    vec_first,
    vec_second,
):
    dp_count = lax.axis_size("dp")
    group = segment_ids.shape[1]

    def gather_slabs(master):
        shard = master.astype(BF16)
        whole = lax.all_gather(shard, "dp", axis=1, tiled=True)
        return whole.reshape(shard.shape[0], SLABS, -1).transpose(1, 0, 2)

    positions = lax.iota(jnp.int32, group)
    starts = span_starts[0]
    inside = (positions[:, None] >= starts[None, :]) & (positions[:, None] < starts[None, :] + SPAN)
    mask_col = jnp.any(inside, axis=1).astype(F32)[:, None]
    seg = segment_ids[0][:, None]
    lane = lax.broadcasted_iota(jnp.int32, (group, LANES), 1)
    first, second = seg == 0, seg == 1
    zero = jnp.zeros((), F32)
    seg_q = jnp.where(lane == 0, jnp.where(second, NEG_FILL, zero), jnp.where(lane == 1, jnp.where(first, NEG_FILL, zero), zero))
    seg_k = jnp.where(
        lane == 0,
        first.astype(F32),
        jnp.where(lane == 1, second.astype(F32), ((lane >= 2) & (lane <= 4)).astype(F32)),
    )
    inside = attn_master.shape[1] % 256 == 0 and ffn_master.shape[1] % 256 == 0 and dp_count in (4, 8)
    head = (frames[0], mask_col, cotangent[0], seg_q.astype(BF16), seg_k.astype(BF16), vec_master)
    if inside:
        output, frames_grad, vec_grad, norm, attn_owned, ffn_owned = run_layer(
            *head, attn_master, ffn_master, True, dp_count // 2
        )
        grad_norm = norm[0, 0]
    else:
        output, frames_grad, early, late, g_attn, g_ffn = run_layer(
            *head, gather_slabs(attn_master), gather_slabs(ffn_master), False, dp_count // 2
        )
        vec_local = jnp.concatenate([late[0:4], early[0:4], late[4:5], early[4:8]], axis=0)

        def scatter_slabs(slabs):
            whole = slabs.astype(F32).transpose(1, 0, 2).reshape(slabs.shape[1], -1)
            return lax.psum_scatter(whole, "dp", scatter_dimension=1, tiled=True)

        attn_owned = scatter_slabs(g_attn)
        ffn_owned = scatter_slabs(g_ffn)
        owned_squares = jnp.sum(attn_owned * attn_owned) + jnp.sum(ffn_owned * ffn_owned)
        vec_grad, total_squares = lax.psum((vec_local, owned_squares), ("seq", "dp"))
        grad_norm = jnp.sqrt(total_squares + jnp.sum(vec_grad * vec_grad))
    clip = jnp.minimum(1.0, MAX_NORM / (grad_norm + 1e-06))
    attn_new, attn_first_new, attn_second_new = adam_step(
        attn_master, attn_first, attn_second, attn_owned * clip, RATE_ATTN, DECAY_RATE
    )
    ffn_new, ffn_first_new, ffn_second_new = adam_step(
        ffn_master, ffn_first, ffn_second, ffn_owned * clip, RATE_FFN, DECAY_RATE
    )
    vec_new, vec_first_new, vec_second_new = adam_step(
        vec_master, vec_first, vec_second, vec_grad * clip, RATE_VEC, 0.0
    )
    return (
        output[None],
        frames_grad[None],
        grad_norm,
        attn_new,
        attn_first_new,
        attn_second_new,
        attn_new.astype(BF16),
        ffn_new,
        ffn_first_new,
        ffn_second_new,
        ffn_new.astype(BF16),
        vec_new,
        vec_first_new,
        vec_second_new,
    )


def solution(mesh):
    return jax.shard_map(
        per_device,
        mesh=mesh,
        in_specs=(
            P("dp", "seq", None),
            P("dp", None),
            P("dp", None),
            P("dp", "seq", None),
            P("seq", "dp"),
            P("seq", "dp"),
            P("seq", "dp"),
            P("seq", "dp"),
            P("seq", "dp"),
            P("seq", "dp"),
            P(),
            P(),
            P(),
        ),
        out_specs=(
            P("dp", "seq", None),
            P("dp", "seq", None),
            P(),
            P("seq", "dp"),
            P("seq", "dp"),
            P("seq", "dp"),
            P("seq", "dp"),
            P("seq", "dp"),
            P("seq", "dp"),
            P("seq", "dp"),
            P("seq", "dp"),
            P(),
            P(),
            P(),
        ),
        check_vma=False,
    )
```

```python
import functools

import jax
import jax.numpy as jnp
from jax import lax
from jax.experimental import pallas as pl
from jax.experimental.pallas import tpu as pltpu
from jax.sharding import PartitionSpec as P

H = 16
SPAN = 10
STEP = 10

EPS_NORM = 1e-05
BETA_ONE = 0.9
BETA_TWO = 0.999
EPS_ADAM = 1e-08
RATE_ATTN = 0.12
RATE_FFN = 0.03
RATE_VEC = 0.5
DECAY_RATE = 0.01
MAX_NORM = 1.0
NEG_FILL = -1e30

SLABS = 8
LANES = 128
VMEM_LIMIT = 62 * 1024 * 1024
F32 = jnp.float32
BF16 = jnp.bfloat16
MESH = pl.DeviceIdType.MESH


def adam_step(master, first, second, grad, rate, decay):
    first_new = BETA_ONE * first + (1.0 - BETA_ONE) * grad
    second_new = BETA_TWO * second + (1.0 - BETA_TWO) * grad * grad
    first_hat = first_new / (1.0 - BETA_ONE**STEP)
    second_hat = second_new / (1.0 - BETA_TWO**STEP)
    master_new = master - rate * (first_hat / (jnp.sqrt(second_hat) + EPS_ADAM) + decay * master)
    return (master_new, first_new, second_new)


def nn(left, right):
    return lax.dot_general(left, right, (((1,), (0,)), ((), ())), preferred_element_type=F32)


def nt(left, right):
    return lax.dot_general(left, right, (((1,), (1,)), ((), ())), preferred_element_type=F32)


def tn(left, right):
    return lax.dot_general(left, right, (((0,), (0,)), ((), ())), preferred_element_type=F32)


def normalise(source):
    mean_val = jnp.mean(source, axis=-1, keepdims=True)
    centred = source - mean_val
    inv_std = lax.rsqrt(jnp.mean(centred * centred, axis=-1, keepdims=True) + EPS_NORM)
    return centred * inv_std, inv_std


def norm_back(grad_out, normed, inv_std, gain_row):
    scaled = grad_out * gain_row
    inner = (
        scaled
        - jnp.mean(scaled, axis=-1, keepdims=True)
        - normed * jnp.mean(scaled * normed, axis=-1, keepdims=True)
    )
    return inner * inv_std


def col_sum(value):
    return jnp.sum(value, axis=0, keepdims=True)


class Gather:
    def __init__(self, cp, buf, base, place, off, rows):
        self.cp, self.buf, self.b = cp, buf, base
        self.s, self.px, self.py, self.pd = place
        self.off, self.h = off, rows // 2

    def top(self, slot):
        return self.buf.at[slot, pl.ds(self.off, self.h)]

    def bot(self, slot):
        return self.buf.at[slot, pl.ds(self.off + self.h, self.h)]

    def c(self, part, slot, i, to):
        ref = part(slot)
        return self.cp(ref, ref, self.b + i, to)

    def start(self):
        self.c(self.top, self.s, 0, self.px).start()
        self.c(self.bot, self.s, 2, self.py).start()
        self.c(self.bot, self.s, 1, self.px).start()
        self.c(self.top, self.s, 3, self.py).start()

    def relay(self):
        self.c(self.top, self.px, 0, self.px).wait_recv()
        self.c(self.top, self.px, 4, self.py).start()
        self.c(self.bot, self.py, 2, self.py).wait_recv()
        self.c(self.bot, self.py, 5, self.px).start()

    def wait_x(self):
        self.c(self.bot, self.px, 1, self.px).wait_recv()

    def wait_y(self):
        self.c(self.top, self.py, 3, self.py).wait_recv()

    def wait_d(self):
        self.c(self.top, self.pd, 4, self.py).wait_recv()
        self.c(self.bot, self.pd, 5, self.px).wait_recv()

    def sent(self):
        for part, slot, i, to in (
            (self.top, self.s, 0, self.px),
            (self.bot, self.s, 2, self.py),
            (self.bot, self.s, 1, self.px),
            (self.top, self.s, 3, self.py),
            (self.top, self.px, 4, self.py),
            (self.bot, self.py, 5, self.px),
        ):
            self.c(part, slot, i, to).wait_send()


class Scatter:
    def __init__(self, cp, part, in_x, in_y, via_x, via_y, base, place):
        _, px, py, _ = place
        h = in_x.shape[1] // 2
        top, bot = pl.ds(0, h), pl.ds(h, h)
        self.to_x, self.to_y, self.via_x, self.via_y = part(1), part(2), via_x, via_y
        self.top, self.bot = top, bot
        far = part(3)
        self.copies = [
            cp(far.at[:, top], via_x, base, px),
            cp(far.at[:, bot], via_y, base + 1, py),
            cp(self.to_x.at[:, top], in_x.at[:, top], base + 2, px),
            cp(self.to_y.at[:, bot], in_y.at[:, bot], base + 3, py),
            cp(self.to_y.at[:, top], in_y.at[:, top], base + 4, py),
            cp(self.to_x.at[:, bot], in_x.at[:, bot], base + 5, px),
        ]

    def start(self, relation):
        for i in {3: (0, 1), 1: (2,), 2: (3,)}[relation]:
            self.copies[i].start()

    def relay(self):
        for i, ref, via, at in ((0, self.to_y, self.via_x, self.top), (1, self.to_x, self.via_y, self.bot)):
            self.copies[i].wait_recv()
            ref[:, at, :] = (ref[:, at, :].astype(F32) + via[...].astype(F32)).astype(BF16)
            self.copies[4 + i].start()

    def wait(self):
        for i in (2, 3, 4, 5):
            self.copies[i].wait_recv()

    def sent(self):
        for copy in self.copies:
            copy.wait_send()


class Line:
    def __init__(self, cp_dp, buf, base, chip, core, chips):
        self.cp, self.buf, self.b = cp_dp, buf, base
        self.z, self.core, self.n = chip, core, chips

    def c(self, shard, kind, to):
        at = 2 * shard + self.core
        return self.cp(self.buf.at[at], self.buf.at[at], self.b + kind * self.n + shard, to)

    def up(self, shard):
        return self.c(shard, 0, 2 * (self.z + 1) + self.core)

    def down(self, shard):
        return self.c(shard, 1, 2 * (self.z - 1) + self.core)

    def across(self, shard):
        return self.c(shard, 2, 2 * self.z + 1 - self.core)

    def start_up(self):
        @pl.when(self.z < self.n - 1)
        def _():
            self.up(self.z).start()

    def start_down(self):
        @pl.when(self.z > 0)
        def _():
            self.down(self.z).start()

    def start(self):
        self.start_up()
        self.start_down()
        self.across(self.z).start()

    def step(self, k):
        low, high = self.z - k, self.z + k

        @pl.when(low >= 0)
        def _():
            self.c(low, 0, 2 * self.z + 1 - self.core).wait_recv()

            @pl.when(self.z < self.n - 1)
            def _():
                self.up(low).start()

            self.across(low).start()

        @pl.when(high < self.n)
        def _():
            self.c(high, 1, 2 * self.z + 1 - self.core).wait_recv()

            @pl.when(self.z > 0)
            def _():
                self.down(high).start()

            self.across(high).start()

    def crossed(self, shard):
        other = 1 - self.core
        ref = self.buf.at[2 * shard + other]
        self.cp(ref, ref, self.b + 2 * self.n + shard, 2 * self.z + other).wait_recv()

    def sent(self):
        for shard in range(self.n):
            self.across(shard).wait_send()

            @pl.when(jnp.logical_and(shard <= self.z, self.z < self.n - 1))
            def _(shard=shard):
                self.up(shard).wait_send()

            @pl.when(jnp.logical_and(shard >= self.z, self.z > 0))
            def _(shard=shard):
                self.down(shard).wait_send()


class LineSum:
    def __init__(self, cp_dp, part, cross, landed, base, chip, core, chips):
        self.cp, self.part, self.cross, self.landed, self.b = cp_dp, part, cross, landed, base
        self.z, self.core, self.n = chip, core, chips

    def mine(self, shard):
        return 2 * shard + self.core

    def across(self, shard):
        src = self.part.at[2 * shard + 1 - self.core]
        return self.cp(src, self.cross.at[shard], self.b + shard, 2 * self.z + 1 - self.core)

    def up(self, shard):
        src = self.part.at[self.mine(shard)]
        return self.cp(src, self.landed.at[shard + 1], self.b + self.n + shard, 2 * (self.z + 1) + self.core)

    def down(self, shard):
        src = self.part.at[self.mine(shard)]
        return self.cp(src, self.landed.at[shard], self.b + 2 * self.n + shard, 2 * (self.z - 1) + self.core)

    def start(self, shard):
        self.across(shard).start()

    def add(self, shard, ref):
        size = min(256, ref.shape[0])

        def one(i, carry):
            at = pl.ds(pl.multiple_of(i * size, size), size)
            total = self.part[self.mine(shard), at, :].astype(F32) + ref[at, :].astype(F32)
            self.part[self.mine(shard), at, :] = total.astype(BF16)
            return carry

        lax.fori_loop(0, ref.shape[0] // size, one, 0)

    def fold(self, shard):
        self.across(shard).wait_recv()
        self.add(shard, self.cross.at[shard])

    def step(self, k):
        if k > self.n - 2:
            return
        up, down = self.n - 1 - k + self.z, k - (self.n - 1 - self.z)

        @pl.when(k >= self.z)
        def _():
            @pl.when(k > self.z)
            def _():
                self.up(up + 1).wait_send()

            @pl.when(self.z > 0)
            def _():
                self.up(up).wait_recv()
                self.add(up, self.landed.at[up + 1])

            self.up(up).start()

        @pl.when(k >= self.n - 1 - self.z)
        def _():
            @pl.when(k > self.n - 1 - self.z)
            def _():
                self.down(down - 1).wait_send()

            @pl.when(self.z < self.n - 1)
            def _():
                self.down(down).wait_recv()
                self.add(down, self.landed.at[down])

            self.down(down).start()

    def finish(self, owned):
        owned[...] = self.part[self.mine(self.z)].astype(F32)

        @pl.when(self.z > 0)
        def _():
            self.up(self.z).wait_recv()
            owned[...] += self.landed[self.z + 1].astype(F32)

        @pl.when(self.z < self.n - 1)
        def _():
            self.down(self.z).wait_recv()
            owned[...] += self.landed[self.z].astype(F32)

    def sent(self):
        for shard in range(self.n):
            self.across(shard).wait_send()

        @pl.when(self.z < self.n - 1)
        def _():
            self.up(self.z + 1).wait_send()

        @pl.when(self.z > 0)
        def _():
            self.down(self.z - 1).wait_send()


class Everyone:
    def __init__(self, cp_any, plane, line, base, s, chip, core, chips):
        self.cp, self.plane, self.line, self.b = cp_any, plane, line, base
        self.s, self.z, self.core, self.n = s, chip, core, chips
        self.me = 2 * s + core

    def to_plane(self, o):
        p = lax.rem(self.me + o, 8)
        return self.cp(self.plane.at[self.me], self.plane.at[self.me], self.b + o, p // 2, 2 * self.z + lax.rem(p, 2))

    def from_plane(self, o):
        p = lax.rem(self.me - o + 8, 8)
        return self.cp(self.plane.at[p], self.plane.at[p], self.b + o, p // 2, 2 * self.z + lax.rem(p, 2))

    def to_line(self, o):
        p = lax.rem(self.z + o, self.n)
        return self.cp(self.line.at[self.z], self.line.at[self.z], self.b + 7 + o, self.s, 2 * p + self.core)

    def from_line(self, o):
        p = lax.rem(self.z - o + self.n, self.n)
        return self.cp(self.line.at[p], self.line.at[p], self.b + 7 + o, self.s, 2 * p + self.core)

    def start(self, value):
        self.plane[self.me] = value
        for o in range(1, 8):
            self.to_plane(o).start()

    def middle(self):
        for o in range(1, 8):
            self.from_plane(o).wait_recv()
        total = self.plane[0]
        for p in range(1, 8):
            total = total + self.plane[p]
        self.line[self.z] = total
        for o in range(1, self.n):
            self.to_line(o).start()

    def end(self):
        for o in range(1, self.n):
            self.from_line(o).wait_recv()
        total = self.line[0]
        for p in range(1, self.n):
            total = total + self.line[p]
        return total

    def sent(self):
        for o in range(1, 8):
            self.to_plane(o).wait_send()
        for o in range(1, self.n):
            self.to_line(o).wait_send()


def layer_kernel(inside, chips, *refs):
    refs = list(refs)

    def take(count):
        head = refs[:count]
        del refs[:count]
        return head

    frames, segments, spans, cot, vec, attn_src, ffn_src = take(7)
    if inside:
        out, frames_grad, vec_out, norm_out, attn_owned, ffn_owned = take(6)
    else:
        out, frames_grad, early, late, g_attn, g_ffn = take(6)
        w_attn, w_ffn = attn_src, ffn_src
    fr_g, cot_g, a_g, wp, qa, ka, va, kt, att, b_g, gp_g = take(11)
    act_g = fr_g
    resid, own, part, in_x, in_y, via_x, via_y, in_x2, in_y2, via_x2, via_y2 = take(11)
    gsend, gm, dom, ga_g, gres, dqkv, dk_acc, dv_acc, mask_col, seg_q, seg_k = take(11)
    send_sem, recv_sem, local_sem = take(3)
    if inside:
        w_attn, w_ffn, g_attn, g_ffn, cross_a, cross_f, landed_a, landed_f = take(8)
        early, late, squares, planes, lines, planes_s, lines_s = take(7)
    s = lax.axis_index("seq")
    d = lax.axis_index("dp")
    core = lax.rem(d, 2)
    sib = d + 1 - 2 * core

    def peer(r):
        high = lax.rem(s // 2 + r // 2, 2)
        low = lax.rem(lax.rem(s, 2) + r % 2, 2)
        return 2 * high + low

    px, py, pd = peer(1), peer(2), peer(3)
    place = (s, px, py, pd)

    def cp(src, dst, i, to):
        return pltpu.make_async_remote_copy(
            src_ref=src,
            dst_ref=dst,
            send_sem=send_sem.at[i],
            recv_sem=recv_sem.at[i],
            device_id=(to, d),
            device_id_type=MESH,
        )

    def cp_any(src, dst, i, to_seq, to_dp):
        return pltpu.make_async_remote_copy(
            src_ref=src,
            dst_ref=dst,
            send_sem=send_sem.at[i],
            recv_sem=recv_sem.at[i],
            device_id=(to_seq, to_dp),
            device_id_type=MESH,
        )

    def cp_dp(src, dst, i, to):
        return cp_any(src, dst, i, s, to)

    def cp_sib(src, dst, i):
        return cp_any(src, dst, i, s, sib)

    def no_step(k):
        return None

    rows = frames.shape[0]
    width = frames.shape[1]
    local = width // 4
    slab_a = w_attn.shape[2]
    slab_f = w_ffn.shape[2]
    per_a = width // slab_a
    per_f = width // slab_f
    tile = 256
    chunk = 128
    small = 64

    cot_load = pltpu.make_async_copy(cot, cot_g.at[s], local_sem.at[0])
    cot_load.start()
    chip = d // 2
    loads = []
    if inside:
        loads = [pltpu.make_async_copy(attn_src, own.at[:, :slab_a], local_sem.at[1])]
        for i, spot in enumerate((dk_acc, dv_acc)):
            at = slice(i * LANES, (i + 1) * LANES)
            loads.append(pltpu.make_async_copy(ffn_src.at[:, at], spot, local_sem.at[2 + i]))
        for load in loads:
            load.start()

    barrier = pltpu.get_barrier_semaphore()
    if inside:
        for o in range(1, 8):
            p = lax.rem(2 * s + core + o, 8)
            to = (p // 2, 2 * chip + lax.rem(p, 2))
            pl.semaphore_signal(barrier, inc=1, device_id=to, device_id_type=MESH)
        for o in range(1, chips):
            to = (s, 2 * lax.rem(chip + o, chips) + core)
            pl.semaphore_signal(barrier, inc=1, device_id=to, device_id_type=MESH)
        pl.semaphore_wait(barrier, 6 + chips)
    else:
        for to in (px, py, pd):
            pl.semaphore_signal(barrier, inc=1, device_id=(to, d), device_id_type=MESH)
        pl.semaphore_signal(barrier, inc=1, device_id=(s, sib), device_id_type=MESH)
        pl.semaphore_wait(barrier, 4)

    fr_g[s] = frames[...]
    frames_in = Gather(cp, fr_g, 0, place, 0, rows)
    frames_in.start()
    cot_in = Gather(cp, cot_g, 15, place, 0, rows)
    attn_step = ffn_step = no_step
    if inside:
        line_a = Line(cp_dp, w_attn, 60, chip, core, chips)
        line_f = Line(cp_dp, w_ffn, 60 + 3 * chips, chip, core, chips)
        loads[0].wait()
        w_attn[d] = own[:, :slab_a].astype(BF16)
        line_a.start()
        attn_step, ffn_step = line_a.step, line_f.step
    half = rows // 2
    wp_off = pl.multiple_of(core * half, half)
    wp_in = Gather(cp, wp, 6, place, wp_off, half)
    wp_cross = [
        cp_sib(wp.at[p, pl.ds(wp_off, half)], wp.at[p, pl.ds(wp_off, half)], 12 + i) for i, p in enumerate((px, py, pd))
    ]
    early[...] = jnp.zeros_like(early)
    late[...] = jnp.zeros_like(late)

    group = 4 * rows
    position = lax.broadcasted_iota(jnp.int32, (group, spans.shape[1]), 0)
    starts = spans[...]
    covered = jnp.logical_and(position >= starts, position < starts + SPAN)
    mask_col[...] = jnp.max(jnp.where(covered, 1.0, 0.0), axis=1, keepdims=True)
    second = jnp.transpose(jnp.broadcast_to(segments[...].astype(F32), (LANES, group)))
    seg_lane = lax.broadcasted_iota(jnp.int32, (group, LANES), 1)
    fill = jnp.where(seg_lane == 0, second, jnp.where(seg_lane == 1, 1.0 - second, 0.0)) * NEG_FILL
    seg_q[...] = fill.astype(BF16)
    ones = jnp.where(seg_lane < 5, 1.0, 0.0)
    seg_k[...] = jnp.where(seg_lane == 0, 1.0 - second, jnp.where(seg_lane == 1, second, ones)).astype(BF16)
    half = rows // 2

    lane = lax.broadcasted_iota(jnp.int32, (rows, LANES), 1)
    low_head = lane < LANES // 2
    q_bias = vec[2:3, pl.ds(pl.multiple_of(s * local, local), local)]
    v_bias = vec[3:4, pl.ds(pl.multiple_of(s * local, local), local)]

    def weight_rows(first, count, start, size):
        return jnp.concatenate([w_attn[first + i, start : start + size, :] for i in range(count)], axis=1)

    def enter(blk):
        def norm_rows(i, carry):
            at = pl.ds(pl.multiple_of(i * chunk, chunk), chunk)
            at_all = pl.ds(pl.multiple_of(blk * rows + i * chunk, chunk), chunk)
            x = jnp.where(mask_col[at_all, :] > 0.0, vec[8:9, :], fr_g[blk, at, :].astype(F32))
            normed, _ = normalise(x)
            a_g[blk, at, :] = (normed * vec[0:1, :] + vec[1:2, :]).astype(BF16)
            return carry

        lax.fori_loop(0, rows // chunk, norm_rows, 0)

    def project_in(blk):
        a = a_g[blk]
        at_all = pl.ds(pl.multiple_of(blk * rows, rows), rows)
        q = (nt(a, weight_rows(0, per_a, 0, local)) + q_bias).astype(BF16).astype(F32) * 0.125
        for pair in range(2):
            both = q[:, pair * LANES : (pair + 1) * LANES]
            for h in range(2):
                keep = low_head if h == 0 else jnp.logical_not(low_head)
                qa[2 * pair + h, blk, :, :LANES] = jnp.where(keep, both, 0.0).astype(BF16)
                qa[2 * pair + h, blk, :, LANES:] = seg_q[at_all, :]
        k = nt(a, weight_rows(per_a, per_a, 0, local)).astype(BF16)
        for pair in range(2):
            both = k[:, pair * LANES : (pair + 1) * LANES]
            ka[pair, at_all, :LANES] = both
            ka[pair, at_all, LANES:] = seg_k[at_all, :]
            kt[pair, :, at_all] = jnp.transpose(both)
        v = (nt(a, weight_rows(2 * per_a, per_a, 0, local)) + v_bias).astype(BF16)
        for pair in range(2):
            va[pair, at_all, :] = v[:, pair * LANES : (pair + 1) * LANES]

    enter(s)
    if inside:
        for i, spot in enumerate((dk_acc, dv_acc)):
            loads[1 + i].wait()
            w_ffn[d, :, i * LANES : (i + 1) * LANES] = spot[...].astype(BF16)
    attn_step(1)
    frames_in.relay()
    attn_step(2)
    frames_in.wait_x()
    enter(px)
    frames_in.wait_y()
    enter(py)
    attn_step(3)
    if inside:
        line_f.start()
    frames_in.wait_d()
    enter(pd)
    if inside:
        for shard in range(chips):
            line_a.crossed(shard)
    for i in range(per_a):
        wp[s, :, i * slab_a : (i + 1) * slab_a] = w_attn[3 * per_a + i]
    wp_in.start()
    lax.fori_loop(0, 4, lambda j, carry: (project_in(j), carry)[1], 0)
    wp_in.relay()
    cot_load.wait()

    def att_x(j, slot):
        return cp(att.at[slot, j], att.at[slot, j], 21 + j, px)

    def att_y(j, slot):
        return cp(att.at[slot, j], att.at[slot, j], 25 + j, py)

    def att_relay(j, start):
        even = lax.rem(j, 2) == 0

        @pl.when(even)
        def _():
            if start:
                att_x(j, px).wait_recv()
                cp(att.at[px, j], att.at[px, j], 29 + j, py).start()
            else:
                cp(att.at[px, j], att.at[px, j], 29 + j, py).wait_send()

        @pl.when(jnp.logical_not(even))
        def _():
            if start:
                att_y(j, py).wait_recv()
                cp(att.at[py, j], att.at[py, j], 29 + j, px).start()
            else:
                cp(att.at[py, j], att.at[py, j], 29 + j, px).wait_send()

    def attend(j, carry):
        for pair in range(2):
            outs = []
            for h in range(2):
                head = 2 * pair + h
                scores = nt(qa[head, j], ka[pair])
                peak = jnp.max(scores, axis=-1, keepdims=True)
                terms = jnp.exp(scores - peak)
                total = jnp.sum(terms, axis=-1, keepdims=True)
                probs = (terms * (1.0 / total)).astype(BF16)
                outs.append(nn(probs, va[pair]))
                log_total = -(peak + jnp.log(total))
                part_one = log_total.astype(BF16).astype(F32)
                rest = log_total - part_one
                part_two = rest.astype(BF16).astype(F32)
                part_three = rest - part_two
                aug = qa[head, j, :, LANES:].astype(F32)
                aug = jnp.where(lane == 2, part_one, aug)
                aug = jnp.where(lane == 3, part_two, aug)
                aug = jnp.where(lane == 4, part_three, aug)
                qa[head, j, :, LANES:] = aug.astype(BF16)
            att[s, j, :, pair * LANES : (pair + 1) * LANES] = jnp.where(low_head, outs[0], outs[1]).astype(BF16)
        att_x(j, s).start()
        att_y(j, s).start()

        @pl.when(j > 0)
        def _():
            att_relay(j - 1, True)

        return carry

    lax.fori_loop(0, 2, attend, 0)
    wp_in.wait_x()
    wp_cross[0].start()
    wp_in.wait_y()
    wp_cross[1].start()
    wp_in.wait_d()
    wp_cross[2].start()
    lax.fori_loop(2, 3, attend, 0)
    ffn_step(1)
    lax.fori_loop(3, 4, attend, 0)
    att_relay(3, True)
    cot_in.start()
    other_off = pl.multiple_of((1 - core) * half, half)
    for i, p in enumerate((px, py, pd)):
        cp_sib(wp.at[p, pl.ds(other_off, half)], wp.at[p, pl.ds(other_off, half)], 12 + i).wait_recv()

    def project(j, carry):
        even = lax.rem(j, 2) == 0

        @pl.when(even)
        def _():
            att_y(j, py).wait_recv()
            cp(att.at[pd, j], att.at[pd, j], 29 + j, py).wait_recv()

        @pl.when(jnp.logical_not(even))
        def _():
            att_x(j, px).wait_recv()
            cp(att.at[pd, j], att.at[pd, j], 29 + j, px).wait_recv()

        left = jnp.concatenate([att[p, j] for p in range(4)], axis=1)
        for i in range(width // tile):
            right = jnp.concatenate([wp[p, :, i * tile : (i + 1) * tile] for p in range(4)], axis=0)
            own[:, i * tile : (i + 1) * tile] = nn(left, right)

        def norm_rows(i, inner):
            at = pl.ds(pl.multiple_of(i * chunk, chunk), chunk)
            at_all = pl.ds(pl.multiple_of(j * rows + i * chunk, chunk), chunk)
            x = jnp.where(mask_col[at_all, :] > 0.0, vec[8:9, :], fr_g[j, at, :].astype(F32))
            total = x + own[at, :] + vec[4:5, :]

            @pl.when(j == s)
            def _():
                resid[at, :] = total

            normed, _ = normalise(total)
            b_g[j, at, :] = (normed * vec[5:6, :] + vec[6:7, :]).astype(BF16)
            return inner

        lax.fori_loop(0, rows // chunk, norm_rows, 0)
        return carry

    lax.fori_loop(0, 2, project, 0)
    ffn_step(2)
    lax.fori_loop(2, 4, project, 0)
    cot_in.relay()
    ffn_step(3)
    if inside:
        for shard in range(chips):
            line_f.crossed(shard)
    frames_in.sent()

    def feed(r):
        blk = peer(r)

        def hidden_tile(i, carry):
            at = pl.ds(pl.multiple_of(i * tile, tile), tile)
            w_in = jnp.concatenate([w_ffn[k, at, :] for k in range(per_f)], axis=1)
            w_out = jnp.concatenate([w_ffn[per_f + k, at, :] for k in range(per_f)], axis=1)
            pre = nt(b_g[blk], w_in) + vec[pl.ds(9 + s, 1), at]
            grad_act = nt(cot_g[blk], w_out)
            cdf = 0.5 * (1.0 + lax.erf(pre * 0.7071067811865476))
            act_g[blk, :, at] = (pre * cdf).astype(BF16)
            density = jnp.exp(-0.5 * pre * pre) * 0.3989422804014327
            grad_pre = ((cdf + pre * density) * grad_act).astype(BF16)
            gp_g[blk, :, at] = grad_pre
            early[pl.ds(4 + s, 1), at] += col_sum(grad_pre.astype(F32))
            return carry

        lax.fori_loop(0, w_ffn.shape[1] // tile, hidden_tile, 0)
        left = gp_g[blk]
        for k in range(per_f):
            at = slice(k * slab_f, (k + 1) * slab_f)
            value = nn(left, w_ffn[k])
            if r == 0:
                own[:, at] = value
            else:
                part[r - 1, k] = value.astype(BF16)

    sum_b = Scatter(cp, lambda r: part.at[r - 1], in_x, in_y, via_x, via_y, 33, place)
    feed(0)
    cot_in.wait_x()
    feed(1)
    sum_b.start(1)
    cot_in.wait_y()
    feed(2)
    sum_b.start(2)
    cot_in.wait_d()
    feed(3)
    sum_b.start(3)

    def ffn_grads(i, carry):
        at = pl.ds(pl.multiple_of(i * tile, tile), tile)
        for left, right, first in ((gp_g, b_g, 0), (act_g, cot_g, per_f)):
            turned = jnp.transpose(jnp.concatenate([left[p, :, at] for p in range(4)], axis=0))
            for k in range(per_f):
                cols = jnp.concatenate([right[p, :, k * slab_f : (k + 1) * slab_f] for p in range(4)], axis=0)
                g_ffn[first + k, at, :] = nn(turned, cols).astype(BF16)
        return carry

    lax.fori_loop(0, w_ffn.shape[1] // tile, ffn_grads, 0)
    sum_step = no_step
    if inside:
        sum_f = LineSum(cp_dp, g_ffn, cross_f, landed_f, 60 + 6 * chips, chip, core, chips)
        sum_g = LineSum(cp_dp, g_attn, cross_a, landed_a, 60 + 9 * chips, chip, core, chips)
        all_early = Everyone(cp_any, planes.at[0], lines.at[0], 60 + 12 * chips, s, chip, core, chips)
        all_late = Everyone(cp_any, planes.at[1], lines.at[1], 67 + 13 * chips, s, chip, core, chips)
        all_squares = Everyone(cp_any, planes_s, lines_s, 74 + 14 * chips, s, chip, core, chips)
        sum_step = sum_f.step
        for shard in range(chips):
            sum_f.start(shard)
    sum_b.relay()
    if inside:
        for shard in range(chips):
            sum_f.fold(shard)
    sum_step(0)
    sum_b.wait()

    def landed(from_x, from_y, at):
        tiles = range(from_x.shape[0])
        return jnp.concatenate([from_x[t, at, :].astype(F32) + from_y[t, at, :].astype(F32) for t in tiles], axis=1)

    def back_two(i, carry):
        at = pl.ds(pl.multiple_of(i * small, small), small)
        grad_b = own[at, :] + landed(in_x, in_y, at)
        normed, inv_std = normalise(resid[at, :])
        grad_y = cot_g[s, at, :].astype(F32)
        grad_resid = grad_y + norm_back(grad_b, normed, inv_std, vec[5:6, :])
        gres[at, :] = grad_resid
        low = grad_resid.astype(BF16)
        ga_g[s, at, :] = low
        early[0:1, :] += col_sum(low.astype(F32))
        early[1:2, :] += col_sum(grad_b * normed)
        early[2:3, :] += col_sum(grad_b)
        early[3:4, :] += col_sum(grad_y)
        return carry

    lax.fori_loop(0, rows // small, back_two, 0)

    for i, r in enumerate((3, 1, 2)):
        gsend[r] = nt(ga_g[s], wp[peer(r)]).astype(BF16)
        cp(gsend.at[r], gm.at[s], 39 + i, peer(r)).start()
    gm[s] = nt(ga_g[s], wp[s]).astype(BF16)
    ga_in = Gather(cp, ga_g, 42, place, 0, rows)
    ga_in.start()
    sum_b.sent()
    if inside:
        all_early.start(early[...])

    def out_part(blk, k):
        return nn(act_g[blk], w_ffn[per_f + k])

    for j in range(4):
        att_x(j, s).wait_send()
        att_y(j, s).wait_send()
        att_relay(j, False)
    sum_o = Scatter(cp, lambda r: att.at[peer(r)], in_x2, in_y2, via_x2, via_y2, 48, place)
    for r in (3, 1, 2):
        for k in range(per_f):
            att[peer(r), k] = out_part(peer(r), k).astype(BF16)

    for i, r in enumerate((3, 1, 2)):
        cp(gsend.at[r], gm.at[peer(r)], 39 + i, peer(r)).wait_recv()

    def spread(j, carry):
        for pair in range(2):
            both = gm[j, :, pair * LANES : (pair + 1) * LANES].astype(F32)
            dom[2 * pair, j] = jnp.where(low_head, both, 0.0).astype(BF16)
            dom[2 * pair + 1, j] = jnp.where(low_head, 0.0, both).astype(BF16)
        return carry

    lax.fori_loop(0, 4, spread, 0)

    def back_pair(pair, between):
        dk_acc[...] = jnp.zeros_like(dk_acc)
        dv_acc[...] = jnp.zeros_like(dv_acc)

        def back_block(j, carry):
            sides = []
            for h in range(2):
                head = 2 * pair + h
                probs = jnp.exp(nt(ka[pair], qa[head, j]))
                grad_probs = nt(va[pair], dom[head, j])
                delta = jnp.sum(probs * grad_probs, axis=0, keepdims=True)
                grad_scores = (probs * (grad_probs - delta)).astype(BF16)
                dv_acc[...] += nn(probs.astype(BF16), dom[head, j])
                dk_acc[...] += nn(grad_scores, qa[head, j, :, :LANES])
                sides.append(nn(kt[pair], grad_scores))
            half_lane = LANES // 2
            turned = jnp.concatenate([sides[0][:half_lane], sides[1][half_lane:]], axis=0)
            dqkv[0, j, :, pair * LANES : (pair + 1) * LANES] = (jnp.transpose(turned) * 0.125).astype(BF16)
            return carry

        lax.fori_loop(0, 2, back_block, 0)
        between()
        lax.fori_loop(2, 4, back_block, 0)
        for j in range(4):
            at = slice(j * rows, (j + 1) * rows)
            dqkv[1, j, :, pair * LANES : (pair + 1) * LANES] = dk_acc[at, :].astype(BF16)
            dqkv[2, j, :, pair * LANES : (pair + 1) * LANES] = dv_acc[at, :].astype(BF16)

    back_pair(0, ga_in.relay)
    sum_step(1)
    back_pair(1, all_early.middle if inside else lambda: None)

    sum_a = Scatter(cp, lambda r: part.at[r - 1], in_x, in_y, via_x, via_y, 54, place)

    def grad_in(r):
        blk = peer(r)
        left = jnp.concatenate([dqkv[c, blk] for c in range(3)], axis=1)
        for k in range(per_a):
            at = slice(k * slab_a, (k + 1) * slab_a)
            right = jnp.concatenate([w_attn[c * per_a + k] for c in range(3)], axis=0)
            value = nn(left, right)
            if r == 0:
                own[:, at] = value
            else:
                per_tile = slab_a // tile
                for t in range(per_tile):
                    part[r - 1, k * per_tile + t] = value[:, t * tile : (t + 1) * tile].astype(BF16)

    for r in (3, 1, 2):
        grad_in(r)
        sum_a.start(r)
    grad_in(0)

    my_cols = pl.ds(pl.multiple_of(s * local, local), local)
    for j in range(4):
        late[2:3, my_cols] += col_sum(dqkv[0, j].astype(F32))
        late[3:4, my_cols] += col_sum(dqkv[2, j].astype(F32))

    def attn_grads(c):
        turned = jnp.transpose(jnp.concatenate([dqkv[c, p] for p in range(4)], axis=0))
        for k in range(per_a):
            cols = jnp.concatenate([a_g[p, :, k * slab_a : (k + 1) * slab_a] for p in range(4)], axis=0)
            g_attn[c * per_a + k] = nn(turned, cols).astype(BF16)

    attn_grads(0)
    attn_grads(1)
    attn_grads(2)
    ga_in.wait_x()
    ga_in.wait_y()
    ga_in.wait_d()
    turned = jnp.transpose(jnp.concatenate([att[s, p] for p in range(4)], axis=0))
    for k in range(per_a):
        cols = jnp.concatenate([ga_g[p, :, k * slab_a : (k + 1) * slab_a] for p in range(4)], axis=0)
        g_attn[3 * per_a + k] = nn(turned, cols).astype(BF16)

    if inside:
        for shard in range(chips):
            sum_g.start(shard)
    sum_a.relay()
    for r in (3, 1, 2):
        sum_o.start(r)
    sum_step(2)
    if inside:
        for shard in range(chips):
            sum_g.fold(shard)
        sum_g.step(0)
    sum_a.wait()

    def back_one(i, carry):
        at = pl.ds(pl.multiple_of(i * small, small), small)
        at_all = pl.ds(pl.multiple_of(s * rows + i * small, small), small)
        grad_a = own[at, :] + landed(in_x, in_y, at)
        masked = mask_col[at_all, :] > 0.0
        normed, inv_std = normalise(jnp.where(masked, vec[8:9, :], frames[at, :].astype(F32)))
        grad_x = gres[at, :] + norm_back(grad_a, normed, inv_std, vec[0:1, :])
        frames_grad[at, :] = jnp.where(masked, 0.0, grad_x)
        late[0:1, :] += col_sum(grad_a * normed)
        late[1:2, :] += col_sum(grad_a)
        late[4:5, :] += col_sum(jnp.where(masked, grad_x, 0.0))
        return carry

    lax.fori_loop(0, rows // small, back_one, 0)
    if inside:
        all_late.start(late[...])
        sum_f.finish(ffn_owned)
        squares[...] = jnp.zeros_like(squares)
        ffn_squares = col_sum(ffn_owned[...] * ffn_owned[...])
        sum_g.step(1)
    sum_o.relay()
    if inside:
        all_late.middle()
        sum_g.step(2)
    sum_o.wait()
    for k in range(per_f):
        at = slice(k * slab_f, (k + 1) * slab_f)
        total = out_part(s, k) + resid[:, at] + in_x2[k].astype(F32) + in_y2[k].astype(F32) + vec[7:8, at]
        out[:, at] = total.astype(BF16)

    if inside:
        whole_early = all_early.end()
        whole_late = all_late.end()
        vec_out[0:4, :] = whole_late[0:4]
        vec_out[4:8, :] = whole_early[0:4]
        vec_out[8:9, :] = whole_late[4:5]
        vec_out[9:13, :] = whole_early[4:8]
        vec_square = col_sum(vec_out[...] * vec_out[...])
        sum_g.finish(attn_owned)
        attn_squares = col_sum(attn_owned[...] * attn_owned[...])
        owned_squares = sum(attn_squares[:, i * LANES : (i + 1) * LANES] for i in range(slab_a // LANES))
        owned_squares += sum(ffn_squares[:, i * LANES : (i + 1) * LANES] for i in range(slab_f // LANES))
        squares[0:1, :] = owned_squares
        all_squares.start(squares[...])
        all_squares.middle()
        whole_squares = all_squares.end()
        total = jnp.sum(whole_squares[0:1], axis=1, keepdims=True) + jnp.sum(vec_square, axis=1, keepdims=True)
        norm_out[...] = jnp.broadcast_to(jnp.sqrt(total), norm_out.shape)
        line_a.sent()
        line_f.sent()
        sum_f.sent()
        sum_g.sent()
        all_early.sent()
        all_late.sent()
        all_squares.sent()

    wp_in.sent()
    for copy in wp_cross:
        copy.wait_send()
    cot_in.sent()

    for i, r in enumerate((3, 1, 2)):
        cp(gsend.at[r], gm.at[s], 39 + i, peer(r)).wait_send()
    ga_in.sent()
    sum_a.sent()
    sum_o.sent()


def run_layer(frames, segments, spans, cot, vec, attn_src, ffn_src, inside, chips):
    rows, width = frames.shape
    group = 4 * rows
    local = width // 4
    slab_count = 2 * chips if inside else SLABS
    hidden = ffn_src.shape[0] if inside else ffn_src.shape[1]
    attn_shape = (slab_count, local, attn_src.shape[-1])
    ffn_shape = (slab_count, hidden, ffn_src.shape[-1])
    vmem = pl.BlockSpec(memory_space=pltpu.VMEM)
    anywhere = pl.BlockSpec(memory_space=pl.ANY)
    source = anywhere if inside else vmem
    block = (4, rows, width)
    sums = (8, width)
    scratch = [
        pltpu.VMEM(block, BF16),
        pltpu.VMEM(block, BF16),
        pltpu.VMEM(block, BF16),
        pltpu.VMEM((4, local, width), BF16),
        pltpu.VMEM((4, 4, rows, 2 * LANES), BF16),
        pltpu.VMEM((2, group, 2 * LANES), BF16),
        pltpu.VMEM((2, group, LANES), BF16),
        pltpu.VMEM((2, LANES, group), BF16),
        pltpu.VMEM((4, 4, rows, local), BF16),
        pltpu.VMEM(block, BF16),
        pltpu.VMEM((4, rows, hidden), BF16),
        pltpu.VMEM((rows, width), F32),
        pltpu.VMEM((rows, width), F32),
        pltpu.VMEM((3, 4, rows, local), BF16),
        pltpu.VMEM((4, rows, local), BF16),
        pltpu.VMEM((4, rows, local), BF16),
        pltpu.VMEM((4, rows // 2, local), BF16),
        pltpu.VMEM((4, rows // 2, local), BF16),
        pltpu.VMEM((4, rows, local), BF16),
        pltpu.VMEM((4, rows, local), BF16),
        pltpu.VMEM((4, rows // 2, local), BF16),
        pltpu.VMEM((4, rows // 2, local), BF16),
        pltpu.VMEM((4, rows, local), BF16),
        pltpu.VMEM((4, rows, local), BF16),
        pltpu.VMEM((4, 4, rows, LANES), BF16),
        pltpu.VMEM(block, BF16),
        pltpu.VMEM((rows, width), F32),
        pltpu.VMEM((3, 4, rows, local), BF16),
        pltpu.VMEM((group, LANES), F32),
        pltpu.VMEM((group, LANES), F32),
        pltpu.VMEM((group, 1), F32),
        pltpu.VMEM((group, LANES), BF16),
        pltpu.VMEM((group, LANES), BF16),
    ]
    sem_count = 82 + 15 * chips if inside else 60
    scratch += [pltpu.SemaphoreType.DMA((sem_count,)), pltpu.SemaphoreType.DMA((sem_count,))]
    scratch.append(pltpu.SemaphoreType.DMA((4,)))
    if inside:
        scratch += [
            pltpu.VMEM(attn_shape, BF16),
            pltpu.VMEM(ffn_shape, BF16),
            pltpu.VMEM(attn_shape, BF16),
            pltpu.VMEM(ffn_shape, BF16),
            pltpu.VMEM((chips, *attn_shape[1:]), BF16),
            pltpu.VMEM((chips, *ffn_shape[1:]), BF16),
            pltpu.VMEM((chips + 1, *attn_shape[1:]), BF16),
            pltpu.VMEM((chips + 1, *ffn_shape[1:]), BF16),
            pltpu.VMEM(sums, F32),
            pltpu.VMEM(sums, F32),
            pltpu.VMEM((8, LANES), F32),
            pltpu.VMEM((2, 8, *sums), F32),
            pltpu.VMEM((2, chips, *sums), F32),
            pltpu.VMEM((8, 8, LANES), F32),
            pltpu.VMEM((chips, 8, LANES), F32),
        ]
        last = (
            jax.ShapeDtypeStruct(vec.shape, F32),
            jax.ShapeDtypeStruct((8, LANES), F32),
            jax.ShapeDtypeStruct(attn_shape[1:], F32),
            jax.ShapeDtypeStruct(ffn_shape[1:], F32),
        )
    else:
        last = (
            jax.ShapeDtypeStruct(sums, F32),
            jax.ShapeDtypeStruct(sums, F32),
            jax.ShapeDtypeStruct(attn_shape, BF16),
            jax.ShapeDtypeStruct(ffn_shape, BF16),
        )
    return pl.pallas_call(
        functools.partial(layer_kernel, inside, chips),
        out_shape=(jax.ShapeDtypeStruct((rows, width), BF16), jax.ShapeDtypeStruct((rows, width), F32), *last),
        in_specs=[vmem, vmem, vmem, anywhere, vmem, source, source],
        out_specs=(vmem,) * 6,
        scratch_shapes=scratch,
        compiler_params=pltpu.CompilerParams(
            collective_id=0, has_side_effects=True, vmem_limit_bytes=VMEM_LIMIT
        ),
    )(frames, segments, spans, cot, vec, attn_src, ffn_src)


def adam_kernel(norm, *refs):
    clip = jnp.minimum(1.0, MAX_NORM / (norm[0, 0] + 1e-06))
    attn, ffn, vec = refs[0:4], refs[4:8], refs[8:12]
    attn_to, ffn_to, vec_to, norm_to = refs[12:16], refs[16:20], refs[20:23], refs[23]

    def update(source, target, rate, decay):
        master, first, second, grad = (ref[...] for ref in source)
        for ref, value in zip(target, adam_step(master, first, second, grad * clip, rate, decay)):
            ref[...] = value
        if len(target) > 3:
            target[3][...] = target[0][...].astype(BF16)

    update(attn, attn_to, RATE_ATTN, DECAY_RATE)
    update(ffn, ffn_to, RATE_FFN, DECAY_RATE)

    @pl.when(pl.program_id(0) == 0)
    def _():
        update(vec, vec_to, RATE_VEC, 0.0)
        norm_to[0, 0] = norm[0, 0]


def run_adam(norm, attn, ffn, vec):
    steps = 4

    def split(array):
        return pl.BlockSpec((array.shape[0] // steps, array.shape[1]), lambda i: (i, 0))

    whole = pl.BlockSpec(vec[0].shape, lambda i: (0, 0))
    scalar = pl.BlockSpec(memory_space=pltpu.SMEM)

    def shapes(array, copy):
        types = (F32, F32, F32, BF16) if copy else (F32, F32, F32)
        return tuple(jax.ShapeDtypeStruct(array.shape, t) for t in types)

    return pl.pallas_call(
        adam_kernel,
        grid=(steps,),
        out_shape=(
            *shapes(attn[0], True),
            *shapes(ffn[0], True),
            *shapes(vec[0], False),
            jax.ShapeDtypeStruct((1, 1), F32),
        ),
        in_specs=[scalar] + [split(attn[0])] * 4 + [split(ffn[0])] * 4 + [whole] * 4,
        out_specs=(*[split(attn[0])] * 4, *[split(ffn[0])] * 4, *[whole] * 3, scalar),
        compiler_params=pltpu.CompilerParams(vmem_limit_bytes=VMEM_LIMIT),
    )(norm, *attn, *ffn, *vec)


def per_device(
    frames,
    segment_ids,
    span_starts,
    cotangent,
    attn_master,
    attn_first,
    attn_second,
    ffn_master,
    ffn_first,
    ffn_second,
    vec_master,
    vec_first,
    vec_second,
):
    dp_count = lax.axis_size("dp")

    def gather_slabs(master):
        shard = master.astype(BF16)
        whole = lax.all_gather(shard, "dp", axis=1, tiled=True)
        return whole.reshape(shard.shape[0], SLABS, -1).transpose(1, 0, 2)

    inside = attn_master.shape[1] % 256 == 0 and ffn_master.shape[1] % 256 == 0 and dp_count in (4, 8)
    head = (frames[0], segment_ids, span_starts, cotangent[0], vec_master)
    if inside:
        output, frames_grad, vec_grad, norm, attn_owned, ffn_owned = run_layer(
            *head, attn_master, ffn_master, True, dp_count // 2
        )
    else:
        output, frames_grad, early, late, g_attn, g_ffn = run_layer(
            *head, gather_slabs(attn_master), gather_slabs(ffn_master), False, dp_count // 2
        )
        vec_local = jnp.concatenate([late[0:4], early[0:4], late[4:5], early[4:8]], axis=0)

        def scatter_slabs(slabs):
            whole = slabs.astype(F32).transpose(1, 0, 2).reshape(slabs.shape[1], -1)
            return lax.psum_scatter(whole, "dp", scatter_dimension=1, tiled=True)

        attn_owned = scatter_slabs(g_attn)
        ffn_owned = scatter_slabs(g_ffn)
        owned_squares = jnp.sum(attn_owned * attn_owned) + jnp.sum(ffn_owned * ffn_owned)
        vec_grad, total_squares = lax.psum((vec_local, owned_squares), ("seq", "dp"))
        norm = jnp.broadcast_to(jnp.sqrt(total_squares + jnp.sum(vec_grad * vec_grad)), (8, LANES))
    updated = run_adam(
        norm,
        (attn_master, attn_first, attn_second, attn_owned),
        (ffn_master, ffn_first, ffn_second, ffn_owned),
        (vec_master, vec_first, vec_second, vec_grad),
    )
    return (output[None], frames_grad[None], updated[-1].reshape(()), *updated[:-1])


def solution(mesh):
    return jax.shard_map(
        per_device,
        mesh=mesh,
        in_specs=(
            P("dp", "seq", None),
            P("dp", None),
            P("dp", None),
            P("dp", "seq", None),
            P("seq", "dp"),
            P("seq", "dp"),
            P("seq", "dp"),
            P("seq", "dp"),
            P("seq", "dp"),
            P("seq", "dp"),
            P(),
            P(),
            P(),
        ),
        out_specs=(
            P("dp", "seq", None),
            P("dp", "seq", None),
            P(),
            P("seq", "dp"),
            P("seq", "dp"),
            P("seq", "dp"),
            P("seq", "dp"),
            P("seq", "dp"),
            P("seq", "dp"),
            P("seq", "dp"),
            P("seq", "dp"),
            P(),
            P(),
            P(),
        ),
        check_vma=False,
    )
```

```python
import functools

import jax
import jax.numpy as jnp
from jax import lax
from jax.experimental import pallas as pl
from jax.experimental.pallas import tpu as pltpu
from jax.sharding import PartitionSpec as P

H = 16
SPAN = 10
STEP = 10

EPS_NORM = 1e-05
BETA_ONE = 0.9
BETA_TWO = 0.999
EPS_ADAM = 1e-08
RATE_ATTN = 0.12
RATE_FFN = 0.03
RATE_VEC = 0.5
DECAY_RATE = 0.01
MAX_NORM = 1.0
NEG_FILL = -1e30

SLABS = 8
LANES = 128
VMEM_LIMIT = 62 * 1024 * 1024
F32 = jnp.float32
BF16 = jnp.bfloat16
MESH = pl.DeviceIdType.MESH


def adam_step(master, first, second, grad, rate, decay):
    first_new = BETA_ONE * first + (1.0 - BETA_ONE) * grad
    second_new = BETA_TWO * second + (1.0 - BETA_TWO) * grad * grad
    first_hat = first_new * (1.0 / (1.0 - BETA_ONE**STEP))
    second_hat = second_new * (1.0 / (1.0 - BETA_TWO**STEP))
    master_new = master - rate * (first_hat / (jnp.sqrt(second_hat) + EPS_ADAM) + decay * master)
    return (master_new, first_new, second_new)


def nn(left, right):
    return lax.dot_general(left, right, (((1,), (0,)), ((), ())), preferred_element_type=F32)


def nt(left, right):
    return lax.dot_general(left, right, (((1,), (1,)), ((), ())), preferred_element_type=F32)


def tn(left, right):
    return lax.dot_general(left, right, (((0,), (0,)), ((), ())), preferred_element_type=F32)


def normalise(source):
    mean_val = jnp.mean(source, axis=-1, keepdims=True)
    centred = source - mean_val
    inv_std = lax.rsqrt(jnp.mean(centred * centred, axis=-1, keepdims=True) + EPS_NORM)
    return centred * inv_std, inv_std


def norm_back(grad_out, normed, inv_std, gain_row):
    scaled = grad_out * gain_row
    inner = (
        scaled
        - jnp.mean(scaled, axis=-1, keepdims=True)
        - normed * jnp.mean(scaled * normed, axis=-1, keepdims=True)
    )
    return inner * inv_std


def col_sum(value):
    return jnp.sum(value, axis=0, keepdims=True)


class Gather:
    def __init__(self, cp, buf, base, place, off, rows):
        self.cp, self.buf, self.b = cp, buf, base
        self.s, self.px, self.py, self.pd = place
        self.off, self.h = off, rows // 2

    def top(self, slot):
        return self.buf.at[slot, pl.ds(self.off, self.h)]

    def bot(self, slot):
        return self.buf.at[slot, pl.ds(self.off + self.h, self.h)]

    def c(self, part, slot, i, to):
        ref = part(slot)
        return self.cp(ref, ref, self.b + i, to)

    def start(self):
        self.c(self.top, self.s, 0, self.px).start()
        self.c(self.bot, self.s, 2, self.py).start()
        self.c(self.bot, self.s, 1, self.px).start()
        self.c(self.top, self.s, 3, self.py).start()

    def relay(self):
        self.c(self.top, self.px, 0, self.px).wait_recv()
        self.c(self.top, self.px, 4, self.py).start()
        self.c(self.bot, self.py, 2, self.py).wait_recv()
        self.c(self.bot, self.py, 5, self.px).start()

    def wait_x(self):
        self.c(self.bot, self.px, 1, self.px).wait_recv()

    def wait_y(self):
        self.c(self.top, self.py, 3, self.py).wait_recv()

    def wait_d(self):
        self.c(self.top, self.pd, 4, self.py).wait_recv()
        self.c(self.bot, self.pd, 5, self.px).wait_recv()

    def sent(self):
        for part, slot, i, to in (
            (self.top, self.s, 0, self.px),
            (self.bot, self.s, 2, self.py),
            (self.bot, self.s, 1, self.px),
            (self.top, self.s, 3, self.py),
            (self.top, self.px, 4, self.py),
            (self.bot, self.py, 5, self.px),
        ):
            self.c(part, slot, i, to).wait_send()


class Scatter:
    def __init__(self, cp, part, in_x, in_y, via_x, via_y, base, place):
        _, px, py, _ = place
        h = in_x.shape[1] // 2
        top, bot = pl.ds(0, h), pl.ds(h, h)
        self.to_x, self.to_y, self.via_x, self.via_y = part(1), part(2), via_x, via_y
        self.top, self.bot = top, bot
        far = part(3)
        self.copies = [
            cp(far.at[:, top], via_x, base, px),
            cp(far.at[:, bot], via_y, base + 1, py),
            cp(self.to_x.at[:, top], in_x.at[:, top], base + 2, px),
            cp(self.to_y.at[:, bot], in_y.at[:, bot], base + 3, py),
            cp(self.to_y.at[:, top], in_y.at[:, top], base + 4, py),
            cp(self.to_x.at[:, bot], in_x.at[:, bot], base + 5, px),
        ]

    def start(self, relation):
        for i in {3: (0, 1), 1: (2,), 2: (3,)}[relation]:
            self.copies[i].start()

    def relay(self):
        for i, ref, via, at in ((0, self.to_y, self.via_x, self.top), (1, self.to_x, self.via_y, self.bot)):
            self.copies[i].wait_recv()
            ref[:, at, :] = (ref[:, at, :].astype(F32) + via[...].astype(F32)).astype(BF16)
            self.copies[4 + i].start()

    def wait(self):
        for i in (2, 3, 4, 5):
            self.copies[i].wait_recv()

    def sent(self):
        for copy in self.copies:
            copy.wait_send()


class Line:
    def __init__(self, cp_dp, buf, base, chip, core, chips):
        self.cp, self.buf, self.b = cp_dp, buf, base
        self.z, self.core, self.n = chip, core, chips

    def c(self, shard, kind, hop):
        ref = self.buf.at[2 * shard + self.core]
        return self.cp(ref, ref, self.b + kind, 2 * (self.z + hop) + self.core)

    def has(self, hop):
        return jnp.logical_and(self.z + hop >= 0, self.z + hop < self.n)

    def across(self, shard):
        ref = self.buf.at[2 * shard + self.core]
        return self.cp(ref, ref, self.b + 6 + shard, 2 * self.z + 1 - self.core)

    def start_first(self):
        for step in (1, -1):
            kind = (1 - step) // 2
            far = self.has(3 * step)

            @pl.when(far)
            def _(kind=kind, step=step):
                self.c(self.z, 2 + kind, 2 * step).start()

            @pl.when(jnp.logical_and(jnp.logical_not(self.has(2 * step)), self.has(step)))
            def _(kind=kind, step=step):
                self.c(self.z, kind, step).start()

        self.across(self.z).start()

    def start_rest(self):
        for step in (1, -1):
            kind = (1 - step) // 2
            far = self.has(3 * step)

            @pl.when(far)
            def _(kind=kind, step=step):
                self.c(self.z, kind, step).start()

            @pl.when(jnp.logical_and(jnp.logical_not(far), self.has(2 * step)))
            def _(kind=kind, step=step):
                self.c(self.z, 2 + kind, 2 * step).start()
                self.c(self.z, kind, step).start()

    def relay(self):
        for kind, hop, on in ((2, -2, 1), (3, 2, -1)):

            @pl.when(jnp.logical_and(self.has(hop), self.has(on)))
            def _(kind=kind, hop=hop, on=on):
                self.c(self.z + hop, kind, hop).wait_recv()
                self.c(self.z + hop, kind + 2, on).start()
                self.across(self.z + hop).start()

    def settle(self):
        for kind, hop, on in ((0, -1, 0), (1, 1, 0), (2, -2, 1), (3, 2, -1), (4, -3, 0), (5, 3, 0)):
            due = self.has(hop)
            if on:
                due = jnp.logical_and(due, jnp.logical_not(self.has(on)))

            @pl.when(due)
            def _(kind=kind, hop=hop):
                self.c(self.z + hop, kind, hop).wait_recv()
                self.across(self.z + hop).start()

        other = 1 - self.core
        for shard in range(self.n):
            ref = self.buf.at[2 * shard + other]
            self.cp(ref, ref, self.b + 6 + shard, 2 * self.z + other).wait_recv()

    def sent(self):
        for shard in range(self.n):
            self.across(shard).wait_send()
        for kind, hop in ((0, 1), (1, -1), (2, 2), (3, -2)):

            @pl.when(self.has(hop))
            def _(kind=kind, hop=hop):
                self.c(self.z, kind, hop).wait_send()

        for kind, hop, on in ((4, -2, 1), (5, 2, -1)):

            @pl.when(jnp.logical_and(self.has(hop), self.has(on)))
            def _(kind=kind, hop=hop, on=on):
                self.c(self.z + hop, kind, on).wait_send()


class LineSum:
    def __init__(self, cp_dp, part, cross, landed, base, chip, core, chips):
        self.cp, self.part, self.cross, self.landed, self.b = cp_dp, part, cross, landed, base
        self.z, self.core, self.n = chip, core, chips

    def mine(self, shard):
        return 2 * shard + self.core

    def has(self, hop):
        return jnp.logical_and(self.z + hop >= 0, self.z + hop < self.n)

    def across(self, shard, half):
        rows = self.part.shape[1] // 2
        at = pl.ds(half * rows, rows)
        src = self.part.at[2 * shard + 1 - self.core, at]
        return self.cp(src, self.cross.at[shard, at], self.b + 6 + 2 * shard + half, 2 * self.z + 1 - self.core)

    def direct(self, kind, hop):
        src = self.part.at[self.mine(self.z + hop)]
        return self.cp(src, self.landed.at[self.z], self.b + kind, 2 * (self.z + hop) + self.core)

    def via(self, kind, hop, step):
        src = self.part.at[self.mine(self.z + hop)]
        return self.cp(src, self.landed.at[self.z + step], self.b + kind, 2 * (self.z + step) + self.core)

    def start(self, half):
        for shard in range(self.n):
            self.across(shard, half).start()

    def add(self, shard, ref, first, rows):
        size = min(256, rows)

        def one(i, carry):
            at = pl.ds(pl.multiple_of(first + i * size, size), size)
            total = self.part[self.mine(shard), at, :].astype(F32) + ref[at, :].astype(F32)
            self.part[self.mine(shard), at, :] = total.astype(BF16)
            return carry

        lax.fori_loop(0, rows // size, one, 0)

    def fold(self, half):
        rows = self.part.shape[1] // 2
        for shard in range(self.n):
            self.across(shard, half).wait_recv()
            self.add(shard, self.cross.at[shard], half * rows, rows)

    def launch(self):
        for step in (1, -1):
            kind = (1 - step) // 2
            far = self.has(3 * step)

            @pl.when(far)
            def _(kind=kind, step=step):
                self.via(4 + kind, 3 * step, step).start()

            @pl.when(jnp.logical_and(jnp.logical_not(far), self.has(step)))
            def _(kind=kind, step=step):
                self.direct(kind, step).start()

    def follow(self):
        for step in (1, -1):
            kind = (1 - step) // 2

            @pl.when(self.has(3 * step))
            def _(kind=kind, step=step):
                self.direct(2 + kind, 2 * step).start()
                self.direct(kind, step).start()

            @pl.when(jnp.logical_and(jnp.logical_not(self.has(3 * step)), self.has(2 * step)))
            def _(kind=kind, step=step):
                @pl.when(self.has(-step))
                def _():
                    here = self.landed.at[self.z]
                    self.cp(here, here, self.b + 4 + kind, 2 * (self.z + step) + self.core).wait_recv()
                    self.add(self.z + 2 * step, here, 0, self.part.shape[1])

                self.direct(2 + kind, 2 * step).start()

    def finish(self, owned):
        owned[...] = self.part[self.mine(self.z)].astype(F32)
        for kind, hop in ((0, -1), (1, 1), (2, -2), (3, 2)):

            @pl.when(self.has(hop))
            def _(kind=kind, hop=hop):
                there = self.landed.at[self.z + hop]
                self.cp(there, there, self.b + kind, 2 * (self.z + hop) + self.core).wait_recv()
                owned[...] += there[...].astype(F32)

    def sent(self):
        for shard in range(self.n):
            for half in range(2):
                self.across(shard, half).wait_send()
        for step in (1, -1):
            kind = (1 - step) // 2
            for hops in (1, 2):

                @pl.when(self.has(hops * step))
                def _(kind=kind, step=step, hops=hops):
                    self.direct(kind + 2 * (hops - 1), hops * step).wait_send()

            @pl.when(self.has(3 * step))
            def _(kind=kind, step=step):
                self.via(4 + kind, 3 * step, step).wait_send()


class Everyone:
    def __init__(self, cp_any, plane, line, base, s, chip, core, chips):
        self.cp, self.plane, self.line, self.b = cp_any, plane, line, base
        self.s, self.z, self.core, self.n = s, chip, core, chips
        self.me = 2 * s + core

    def to_plane(self, o):
        p = lax.rem(self.me + o, 8)
        return self.cp(self.plane.at[self.me], self.plane.at[self.me], self.b + o, p // 2, 2 * self.z + lax.rem(p, 2))

    def from_plane(self, o):
        p = lax.rem(self.me - o + 8, 8)
        return self.cp(self.plane.at[p], self.plane.at[p], self.b + o, p // 2, 2 * self.z + lax.rem(p, 2))

    def to_line(self, o):
        p = lax.rem(self.z + o, self.n)
        return self.cp(self.line.at[self.z], self.line.at[self.z], self.b + 7 + o, self.s, 2 * p + self.core)

    def from_line(self, o):
        p = lax.rem(self.z - o + self.n, self.n)
        return self.cp(self.line.at[p], self.line.at[p], self.b + 7 + o, self.s, 2 * p + self.core)

    def start(self, value):
        self.plane[self.me] = value
        for o in range(1, 8):
            self.to_plane(o).start()

    def middle(self):
        for o in range(1, 8):
            self.from_plane(o).wait_recv()
        total = self.plane[0]
        for p in range(1, 8):
            total = total + self.plane[p]
        self.line[self.z] = total
        for o in range(1, self.n):
            self.to_line(o).start()

    def end(self):
        for o in range(1, self.n):
            self.from_line(o).wait_recv()
        total = self.line[0]
        for p in range(1, self.n):
            total = total + self.line[p]
        return total

    def sent(self):
        for o in range(1, 8):
            self.to_plane(o).wait_send()
        for o in range(1, self.n):
            self.to_line(o).wait_send()


def layer_kernel(inside, chips, *refs):
    refs = list(refs)

    def take(count):
        head = refs[:count]
        del refs[:count]
        return head

    frames, segments, spans, cot, vec, attn_src, ffn_src = take(7)
    if inside:
        out, frames_grad, vec_out, norm_out, attn_owned, ffn_owned = take(6)
    else:
        out, frames_grad, early, late, g_attn, g_ffn = take(6)
        w_attn, w_ffn = attn_src, ffn_src
    fr_g, cot_g, a_g, wp, qa, ka, va, kt, att, b_g, gp_g = take(11)
    act_g = fr_g
    resid, own, part, in_x, in_y, via_x, via_y, in_x2, in_y2, via_x2, via_y2 = take(11)
    gsend, gm, dom, ga_g, gres, dqkv, dk_acc, dv_acc, mask_col, seg_q, seg_k = take(11)
    send_sem, recv_sem, local_sem = take(3)
    if inside:
        w_attn, w_ffn, g_attn, g_ffn, cross_a, cross_f, landed_a, landed_f = take(8)
        early, late, squares, planes, lines, planes_s, lines_s = take(7)
    s = lax.axis_index("seq")
    d = lax.axis_index("dp")
    core = lax.rem(d, 2)
    sib = d + 1 - 2 * core

    def peer(r):
        half = r // 2
        high = lax.rem(s // 2 + half, 2)
        low = lax.rem(lax.rem(s, 2) + (r - 2 * half), 2)
        return 2 * high + low

    px, py, pd = peer(1), peer(2), peer(3)
    place = (s, px, py, pd)

    def cp(src, dst, i, to):
        return pltpu.make_async_remote_copy(
            src_ref=src,
            dst_ref=dst,
            send_sem=send_sem.at[i],
            recv_sem=recv_sem.at[i],
            device_id=(to, d),
            device_id_type=MESH,
        )

    def cp_any(src, dst, i, to_seq, to_dp):
        return pltpu.make_async_remote_copy(
            src_ref=src,
            dst_ref=dst,
            send_sem=send_sem.at[i],
            recv_sem=recv_sem.at[i],
            device_id=(to_seq, to_dp),
            device_id_type=MESH,
        )

    def cp_dp(src, dst, i, to):
        return cp_any(src, dst, i, s, to)

    def cp_sib(src, dst, i):
        return cp_any(src, dst, i, s, sib)


    rows = frames.shape[0]
    width = frames.shape[1]
    local = width // 4
    slab_a = w_attn.shape[2]
    slab_f = w_ffn.shape[2]
    per_a = width // slab_a
    per_f = width // slab_f
    tile = 256
    chunk = 128
    small = 64

    cot_load = pltpu.make_async_copy(cot, cot_g.at[s], local_sem.at[0])
    cot_load.start()
    chip = d // 2
    loads = []
    if inside:
        loads = [pltpu.make_async_copy(attn_src, own.at[:, :slab_a], local_sem.at[1])]
        for i, spot in enumerate((dk_acc, dv_acc)):
            at = slice(i * LANES, (i + 1) * LANES)
            loads.append(pltpu.make_async_copy(ffn_src.at[:, at], spot, local_sem.at[2 + i]))
        for load in loads:
            load.start()

    barrier = pltpu.get_barrier_semaphore()
    if inside:
        for o in range(1, 8):
            p = lax.rem(2 * s + core + o, 8)
            to = (p // 2, 2 * chip + lax.rem(p, 2))
            pl.semaphore_signal(barrier, inc=1, device_id=to, device_id_type=MESH)
        for o in range(1, chips):
            to = (s, 2 * lax.rem(chip + o, chips) + core)
            pl.semaphore_signal(barrier, inc=1, device_id=to, device_id_type=MESH)
        pl.semaphore_wait(barrier, 6 + chips)
    else:
        for to in (px, py, pd):
            pl.semaphore_signal(barrier, inc=1, device_id=(to, d), device_id_type=MESH)
        pl.semaphore_signal(barrier, inc=1, device_id=(s, sib), device_id_type=MESH)
        pl.semaphore_wait(barrier, 4)

    fr_g[s] = frames[...]
    frames_in = Gather(cp, fr_g, 0, place, 0, rows)
    frames_in.start()
    cot_in = Gather(cp, cot_g, 15, place, 0, rows)
    if inside:
        line_a = Line(cp_dp, w_attn, 60, chip, core, chips)
        line_f = Line(cp_dp, w_ffn, 66 + chips, chip, core, chips)
        loads[0].wait()
        w_attn[d] = own[:, :slab_a].astype(BF16)
        line_a.start_first()
    half = rows // 2
    wp_off = pl.multiple_of(core * half, half)
    wp_in = Gather(cp, wp, 6, place, wp_off, half)
    wp_cross = [
        cp_sib(wp.at[p, pl.ds(wp_off, half)], wp.at[p, pl.ds(wp_off, half)], 12 + i) for i, p in enumerate((px, py, pd))
    ]
    early[...] = jnp.zeros_like(early)
    late[...] = jnp.zeros_like(late)

    group = 4 * rows
    position = lax.broadcasted_iota(jnp.int32, (group, spans.shape[1]), 0)
    starts = spans[...]
    covered = jnp.logical_and(position >= starts, position < starts + SPAN)
    mask_col[...] = jnp.max(jnp.where(covered, 1.0, 0.0), axis=1, keepdims=True)
    second = jnp.transpose(jnp.broadcast_to(segments[...].astype(F32), (LANES, group)))
    seg_lane = lax.broadcasted_iota(jnp.int32, (group, LANES), 1)
    fill = jnp.where(seg_lane == 0, second, jnp.where(seg_lane == 1, 1.0 - second, 0.0)) * NEG_FILL
    seg_q[...] = fill.astype(BF16)
    ones = jnp.where(seg_lane < 5, 1.0, 0.0)
    seg_k[...] = jnp.where(seg_lane == 0, 1.0 - second, jnp.where(seg_lane == 1, second, ones)).astype(BF16)
    half = rows // 2

    lane = lax.broadcasted_iota(jnp.int32, (rows, LANES), 1)
    low_head = lane < LANES // 2
    q_bias = vec[2:3, pl.ds(pl.multiple_of(s * local, local), local)]
    v_bias = vec[3:4, pl.ds(pl.multiple_of(s * local, local), local)]

    def weight_rows(first, count, start, size):
        return jnp.concatenate([w_attn[first + i, start : start + size, :] for i in range(count)], axis=1)

    def enter(blk):
        def norm_rows(i, carry):
            at = pl.ds(pl.multiple_of(i * chunk, chunk), chunk)
            at_all = pl.ds(pl.multiple_of(blk * rows + i * chunk, chunk), chunk)
            x = jnp.where(mask_col[at_all, :] > 0.0, vec[8:9, :], fr_g[blk, at, :].astype(F32))
            normed, _ = normalise(x)
            a_g[blk, at, :] = (normed * vec[0:1, :] + vec[1:2, :]).astype(BF16)
            return carry

        lax.fori_loop(0, rows // chunk, norm_rows, 0)

    def project_in(blk):
        a = a_g[blk]
        at_all = pl.ds(pl.multiple_of(blk * rows, rows), rows)
        q = (nt(a, weight_rows(0, per_a, 0, local)) + q_bias).astype(BF16).astype(F32) * 0.125
        for pair in range(2):
            both = q[:, pair * LANES : (pair + 1) * LANES]
            for h in range(2):
                keep = low_head if h == 0 else jnp.logical_not(low_head)
                qa[2 * pair + h, blk, :, :LANES] = jnp.where(keep, both, 0.0).astype(BF16)
                qa[2 * pair + h, blk, :, LANES:] = seg_q[at_all, :]
        k = nt(a, weight_rows(per_a, per_a, 0, local)).astype(BF16)
        for pair in range(2):
            both = k[:, pair * LANES : (pair + 1) * LANES]
            ka[pair, at_all, :LANES] = both
            ka[pair, at_all, LANES:] = seg_k[at_all, :]
            kt[pair, :, at_all] = jnp.transpose(both)
        v = (nt(a, weight_rows(2 * per_a, per_a, 0, local)) + v_bias).astype(BF16)
        for pair in range(2):
            va[pair, at_all, :] = v[:, pair * LANES : (pair + 1) * LANES]

    enter(s)
    if inside:
        for i, spot in enumerate((dk_acc, dv_acc)):
            loads[1 + i].wait()
            w_ffn[d, :, i * LANES : (i + 1) * LANES] = spot[...].astype(BF16)
    if inside:
        line_a.start_rest()
        line_a.relay()
    frames_in.relay()
    frames_in.wait_x()
    enter(px)
    frames_in.wait_y()
    enter(py)
    frames_in.wait_d()
    enter(pd)
    if inside:
        line_a.settle()
        line_f.start_first()
    for i in range(per_a):
        wp[s, :, i * slab_a : (i + 1) * slab_a] = w_attn[3 * per_a + i]
    wp_in.start()
    lax.fori_loop(0, 4, lambda j, carry: (project_in(j), carry)[1], 0)
    cot_load.wait()

    def att_x(j, slot):
        return cp(att.at[slot, j], att.at[slot, j], 21 + j, px)

    def att_y(j, slot):
        return cp(att.at[slot, j], att.at[slot, j], 25 + j, py)

    def att_relay(j, start):
        even = lax.rem(j, 2) == 0

        @pl.when(even)
        def _():
            if start:
                att_x(j, px).wait_recv()
                cp(att.at[px, j], att.at[px, j], 29 + j, py).start()
            else:
                cp(att.at[px, j], att.at[px, j], 29 + j, py).wait_send()

        @pl.when(jnp.logical_not(even))
        def _():
            if start:
                att_y(j, py).wait_recv()
                cp(att.at[py, j], att.at[py, j], 29 + j, px).start()
            else:
                cp(att.at[py, j], att.at[py, j], 29 + j, px).wait_send()

    def attend(j, carry):
        for pair in range(2):
            outs = []
            for h in range(2):
                head = 2 * pair + h
                scores = nt(qa[head, j], ka[pair])
                peak = jnp.max(scores, axis=-1, keepdims=True)
                terms = jnp.exp(scores - peak)
                total = jnp.sum(terms, axis=-1, keepdims=True)
                probs = (terms * (1.0 / total)).astype(BF16)
                outs.append(nn(probs, va[pair]))
                log_total = -(peak + jnp.log(total))
                part_one = log_total.astype(BF16).astype(F32)
                rest = log_total - part_one
                part_two = rest.astype(BF16).astype(F32)
                part_three = rest - part_two
                aug = qa[head, j, :, LANES:].astype(F32)
                aug = jnp.where(lane == 2, part_one, aug)
                aug = jnp.where(lane == 3, part_two, aug)
                aug = jnp.where(lane == 4, part_three, aug)
                qa[head, j, :, LANES:] = aug.astype(BF16)
            att[s, j, :, pair * LANES : (pair + 1) * LANES] = jnp.where(low_head, outs[0], outs[1]).astype(BF16)
        att_x(j, s).start()
        att_y(j, s).start()

        @pl.when(j > 0)
        def _():
            att_relay(j - 1, True)

        return carry

    lax.fori_loop(0, 2, attend, 0)
    wp_in.relay()
    if inside:
        line_f.start_rest()
        line_f.relay()
    lax.fori_loop(2, 4, attend, 0)
    wp_in.wait_x()
    wp_cross[0].start()
    wp_in.wait_y()
    wp_cross[1].start()
    wp_in.wait_d()
    wp_cross[2].start()
    att_relay(3, True)
    other_off = pl.multiple_of((1 - core) * half, half)
    for i, p in enumerate((px, py, pd)):
        cp_sib(wp.at[p, pl.ds(other_off, half)], wp.at[p, pl.ds(other_off, half)], 12 + i).wait_recv()

    def project(j, carry):
        even = lax.rem(j, 2) == 0

        @pl.when(even)
        def _():
            att_y(j, py).wait_recv()
            cp(att.at[pd, j], att.at[pd, j], 29 + j, py).wait_recv()

        @pl.when(jnp.logical_not(even))
        def _():
            att_x(j, px).wait_recv()
            cp(att.at[pd, j], att.at[pd, j], 29 + j, px).wait_recv()

        left = jnp.concatenate([att[p, j] for p in range(4)], axis=1)
        for i in range(width // tile):
            right = jnp.concatenate([wp[p, :, i * tile : (i + 1) * tile] for p in range(4)], axis=0)
            own[:, i * tile : (i + 1) * tile] = nn(left, right)

        def norm_rows(i, inner):
            at = pl.ds(pl.multiple_of(i * chunk, chunk), chunk)
            at_all = pl.ds(pl.multiple_of(j * rows + i * chunk, chunk), chunk)
            x = jnp.where(mask_col[at_all, :] > 0.0, vec[8:9, :], fr_g[j, at, :].astype(F32))
            total = x + own[at, :] + vec[4:5, :]

            @pl.when(j == s)
            def _():
                resid[at, :] = total

            normed, _ = normalise(total)
            b_g[j, at, :] = (normed * vec[5:6, :] + vec[6:7, :]).astype(BF16)
            return inner

        lax.fori_loop(0, rows // chunk, norm_rows, 0)
        return carry

    lax.fori_loop(0, 1, project, 0)
    cot_in.start()
    lax.fori_loop(1, 4, project, 0)
    cot_in.relay()
    if inside:
        line_f.settle()
    frames_in.sent()

    def feed(r):
        blk = peer(r)

        def hidden_tile(i, carry):
            at = pl.ds(pl.multiple_of(i * tile, tile), tile)
            w_in = jnp.concatenate([w_ffn[k, at, :] for k in range(per_f)], axis=1)
            w_out = jnp.concatenate([w_ffn[per_f + k, at, :] for k in range(per_f)], axis=1)
            pre = nt(b_g[blk], w_in) + vec[pl.ds(9 + s, 1), at]
            grad_act = nt(cot_g[blk], w_out)
            cdf = 0.5 * (1.0 + lax.erf(pre * 0.7071067811865476))
            act_g[blk, :, at] = (pre * cdf).astype(BF16)
            density = jnp.exp(-0.5 * pre * pre) * 0.3989422804014327
            grad_pre = ((cdf + pre * density) * grad_act).astype(BF16)
            gp_g[blk, :, at] = grad_pre
            early[pl.ds(4 + s, 1), at] += col_sum(grad_pre.astype(F32))
            return carry

        lax.fori_loop(0, w_ffn.shape[1] // tile, hidden_tile, 0)
        left = gp_g[blk]
        for k in range(per_f):
            at = slice(k * slab_f, (k + 1) * slab_f)
            value = nn(left, w_ffn[k])
            if r == 0:
                own[:, at] = value
            else:
                part[r - 1, k] = value.astype(BF16)

    sum_b = Scatter(cp, lambda r: part.at[r - 1], in_x, in_y, via_x, via_y, 33, place)
    cot_in.wait_d()
    feed(3)
    sum_b.start(3)
    cot_in.wait_x()
    feed(1)
    sum_b.start(1)
    cot_in.wait_y()
    feed(2)
    sum_b.start(2)
    sum_b.relay()
    feed(0)

    def ffn_grads(i, carry):
        at = pl.ds(pl.multiple_of(i * tile, tile), tile)
        for left, right, first in ((gp_g, b_g, 0), (act_g, cot_g, per_f)):
            turned = jnp.transpose(jnp.concatenate([left[p, :, at] for p in range(4)], axis=0))
            for k in range(per_f):
                cols = jnp.concatenate([right[p, :, k * slab_f : (k + 1) * slab_f] for p in range(4)], axis=0)
                g_ffn[first + k, at, :] = nn(turned, cols).astype(BF16)
        return carry

    f_tiles = w_ffn.shape[1] // tile
    if inside:
        sum_f = LineSum(cp_dp, g_ffn, cross_f, landed_f, 72 + 2 * chips, chip, core, chips)
        sum_g = LineSum(cp_dp, g_attn, cross_a, landed_a, 78 + 4 * chips, chip, core, chips)
        all_early = Everyone(cp_any, planes.at[0], lines.at[0], 84 + 6 * chips, s, chip, core, chips)
        all_late = Everyone(cp_any, planes.at[1], lines.at[1], 91 + 7 * chips, s, chip, core, chips)
        all_squares = Everyone(cp_any, planes_s, lines_s, 98 + 8 * chips, s, chip, core, chips)
    lax.fori_loop(0, f_tiles // 2, ffn_grads, 0)
    if inside:
        sum_f.start(0)
    lax.fori_loop(f_tiles // 2, f_tiles, ffn_grads, 0)
    if inside:
        sum_f.start(1)
    if inside:
        sum_f.fold(0)
        sum_f.fold(1)
        sum_f.launch()

    def out_part(blk, k):
        return nn(act_g[blk], w_ffn[per_f + k])

    for j in range(4):
        att_x(j, s).wait_send()
        att_y(j, s).wait_send()
        att_relay(j, False)
    sum_o = Scatter(cp, lambda r: att.at[peer(r)], in_x2, in_y2, via_x2, via_y2, 48, place)
    for r in (3, 1, 2):
        for k in range(per_f):
            att[peer(r), k] = out_part(peer(r), k).astype(BF16)
    sum_b.wait()
    sum_o.start(3)

    def landed(from_x, from_y, at):
        tiles = range(from_x.shape[0])
        return jnp.concatenate([from_x[t, at, :].astype(F32) + from_y[t, at, :].astype(F32) for t in tiles], axis=1)

    def back_two(i, carry):
        at = pl.ds(pl.multiple_of(i * small, small), small)
        grad_b = own[at, :] + landed(in_x, in_y, at)
        normed, inv_std = normalise(resid[at, :])
        grad_y = cot_g[s, at, :].astype(F32)
        grad_resid = grad_y + norm_back(grad_b, normed, inv_std, vec[5:6, :])
        gres[at, :] = grad_resid
        low = grad_resid.astype(BF16)
        ga_g[s, at, :] = low
        early[0:1, :] += col_sum(low.astype(F32))
        early[1:2, :] += col_sum(grad_b * normed)
        early[2:3, :] += col_sum(grad_b)
        early[3:4, :] += col_sum(grad_y)
        return carry

    lax.fori_loop(0, rows // small, back_two, 0)

    for i, r in enumerate((3, 1, 2)):
        gsend[r] = nt(ga_g[s], wp[peer(r)]).astype(BF16)
        cp(gsend.at[r], gm.at[s], 39 + i, peer(r)).start()
    gm[s] = nt(ga_g[s], wp[s]).astype(BF16)
    ga_in = Gather(cp, ga_g, 42, place, 0, rows)
    ga_in.start()
    sum_b.sent()

    def spread(j):
        for pair in range(2):
            both = gm[j, :, pair * LANES : (pair + 1) * LANES].astype(F32)
            dom[2 * pair, j] = jnp.where(low_head, both, 0.0).astype(BF16)
            dom[2 * pair + 1, j] = jnp.where(low_head, 0.0, both).astype(BF16)

    def arrive(i, r):
        cp(gsend.at[r], gm.at[peer(r)], 39 + i, peer(r)).wait_recv()
        spread(peer(r))

    spread(s)

    def back_pair(pair, first, second):
        dk_acc[...] = jnp.zeros_like(dk_acc)
        dv_acc[...] = jnp.zeros_like(dv_acc)

        def back_block(r, carry):
            j = peer(r)
            sides = []
            for h in range(2):
                head = 2 * pair + h
                probs = jnp.exp(nt(ka[pair], qa[head, j]))
                grad_probs = nt(va[pair], dom[head, j])
                delta = jnp.sum(probs * grad_probs, axis=0, keepdims=True)
                grad_scores = (probs * (grad_probs - delta)).astype(BF16)
                dv_acc[...] += nn(probs.astype(BF16), dom[head, j])
                dk_acc[...] += nn(grad_scores, qa[head, j, :, :LANES])
                sides.append(nn(kt[pair], grad_scores))
            half_lane = LANES // 2
            turned = jnp.concatenate([sides[0][:half_lane], sides[1][half_lane:]], axis=0)
            dqkv[0, j, :, pair * LANES : (pair + 1) * LANES] = (jnp.transpose(turned) * 0.125).astype(BF16)
            return carry

        lax.fori_loop(0, 1, back_block, 0)
        first()
        lax.fori_loop(1, 3, back_block, 0)
        second()
        lax.fori_loop(3, 4, back_block, 0)
        for j in range(4):
            at = slice(j * rows, (j + 1) * rows)
            dqkv[1, j, :, pair * LANES : (pair + 1) * LANES] = dk_acc[at, :].astype(BF16)
            dqkv[2, j, :, pair * LANES : (pair + 1) * LANES] = dv_acc[at, :].astype(BF16)

    def after_own():
        arrive(1, 1)
        arrive(2, 2)

    def after_near():
        arrive(0, 3)
        if inside:
            sum_f.follow()
            all_early.start(early[...])

    back_pair(0, after_own, after_near)
    back_pair(1, lambda: None, ga_in.relay)

    sum_a = Scatter(cp, lambda r: part.at[r - 1], in_x, in_y, via_x, via_y, 54, place)

    def grad_in(r):
        blk = peer(r)
        left = jnp.concatenate([dqkv[c, blk] for c in range(3)], axis=1)
        for k in range(per_a):
            at = slice(k * slab_a, (k + 1) * slab_a)
            right = jnp.concatenate([w_attn[c * per_a + k] for c in range(3)], axis=0)
            value = nn(left, right)
            if r == 0:
                own[:, at] = value
            else:
                per_tile = slab_a // tile
                for t in range(per_tile):
                    part[r - 1, k * per_tile + t] = value[:, t * tile : (t + 1) * tile].astype(BF16)

    for r in (3, 1, 2):
        grad_in(r)
        sum_a.start(r)
    grad_in(0)

    my_cols = pl.ds(pl.multiple_of(s * local, local), local)
    for j in range(4):
        late[2:3, my_cols] += col_sum(dqkv[0, j].astype(F32))
        late[3:4, my_cols] += col_sum(dqkv[2, j].astype(F32))

    def attn_grads(c):
        turned = jnp.transpose(jnp.concatenate([dqkv[c, p] for p in range(4)], axis=0))
        for k in range(per_a):
            cols = jnp.concatenate([a_g[p, :, k * slab_a : (k + 1) * slab_a] for p in range(4)], axis=0)
            g_attn[c * per_a + k] = nn(turned, cols).astype(BF16)

    attn_grads(0)
    attn_grads(1)
    attn_grads(2)
    ga_in.wait_x()
    ga_in.wait_y()
    ga_in.wait_d()
    turned = jnp.transpose(jnp.concatenate([att[s, p] for p in range(4)], axis=0))
    for k in range(per_a):
        cols = jnp.concatenate([ga_g[p, :, k * slab_a : (k + 1) * slab_a] for p in range(4)], axis=0)
        g_attn[3 * per_a + k] = nn(turned, cols).astype(BF16)

    if inside:
        sum_g.start(0)
        sum_g.start(1)
    sum_a.relay()
    if inside:
        sum_g.fold(0)
        sum_g.fold(1)
        sum_g.launch()
    if inside:
        sum_f.finish(ffn_owned)
        ffn_squares = col_sum(ffn_owned[...] * ffn_owned[...])
        squares[...] = jnp.zeros_like(squares)
        sum_g.follow()
    sum_a.wait()
    sum_o.start(1)
    sum_o.start(2)
    sum_o.relay()

    def back_one(i, carry):
        at = pl.ds(pl.multiple_of(i * small, small), small)
        at_all = pl.ds(pl.multiple_of(s * rows + i * small, small), small)
        grad_a = own[at, :] + landed(in_x, in_y, at)
        masked = mask_col[at_all, :] > 0.0
        normed, inv_std = normalise(jnp.where(masked, vec[8:9, :], frames[at, :].astype(F32)))
        grad_x = gres[at, :] + norm_back(grad_a, normed, inv_std, vec[0:1, :])
        frames_grad[at, :] = jnp.where(masked, 0.0, grad_x)
        late[0:1, :] += col_sum(grad_a * normed)
        late[1:2, :] += col_sum(grad_a)
        late[4:5, :] += col_sum(jnp.where(masked, grad_x, 0.0))
        return carry

    lax.fori_loop(0, rows // small, back_one, 0)
    if inside:
        all_late.start(late[...])
        all_early.middle()
        sum_g.finish(attn_owned)
        attn_squares = col_sum(attn_owned[...] * attn_owned[...])
        owned_squares = sum(attn_squares[:, i * LANES : (i + 1) * LANES] for i in range(slab_a // LANES))
        owned_squares += sum(ffn_squares[:, i * LANES : (i + 1) * LANES] for i in range(slab_f // LANES))
        squares[0:1, :] = owned_squares
        all_squares.start(squares[...])
        all_late.middle()
        whole_early = all_early.end()
        all_squares.middle()
        whole_late = all_late.end()
        vec_out[0:4, :] = whole_late[0:4]
        vec_out[4:8, :] = whole_early[0:4]
        vec_out[8:9, :] = whole_late[4:5]
        vec_out[9:13, :] = whole_early[4:8]
        vec_square = col_sum(vec_out[...] * vec_out[...])

    sum_o.wait()
    for k in range(per_f):
        at = slice(k * slab_f, (k + 1) * slab_f)
        total = out_part(s, k) + resid[:, at] + in_x2[k].astype(F32) + in_y2[k].astype(F32) + vec[7:8, at]
        out[:, at] = total.astype(BF16)

    if inside:
        whole_squares = all_squares.end()
        total = jnp.sum(whole_squares[0:1], axis=1, keepdims=True) + jnp.sum(vec_square, axis=1, keepdims=True)
        norm_out[...] = jnp.broadcast_to(jnp.sqrt(total), norm_out.shape)
        line_a.sent()
        line_f.sent()
        sum_f.sent()
        sum_g.sent()
        all_early.sent()
        all_late.sent()
        all_squares.sent()

    wp_in.sent()
    for copy in wp_cross:
        copy.wait_send()
    cot_in.sent()

    for i, r in enumerate((3, 1, 2)):
        cp(gsend.at[r], gm.at[s], 39 + i, peer(r)).wait_send()
    ga_in.sent()
    sum_a.sent()
    sum_o.sent()


def run_layer(frames, segments, spans, cot, vec, attn_src, ffn_src, inside, chips):
    rows, width = frames.shape
    group = 4 * rows
    local = width // 4
    slab_count = 2 * chips if inside else SLABS
    hidden = ffn_src.shape[0] if inside else ffn_src.shape[1]
    attn_shape = (slab_count, local, attn_src.shape[-1])
    ffn_shape = (slab_count, hidden, ffn_src.shape[-1])
    vmem = pl.BlockSpec(memory_space=pltpu.VMEM)
    anywhere = pl.BlockSpec(memory_space=pl.ANY)
    source = anywhere if inside else vmem
    block = (4, rows, width)
    sums = (8, width)
    scratch = [
        pltpu.VMEM(block, BF16),
        pltpu.VMEM(block, BF16),
        pltpu.VMEM(block, BF16),
        pltpu.VMEM((4, local, width), BF16),
        pltpu.VMEM((4, 4, rows, 2 * LANES), BF16),
        pltpu.VMEM((2, group, 2 * LANES), BF16),
        pltpu.VMEM((2, group, LANES), BF16),
        pltpu.VMEM((2, LANES, group), BF16),
        pltpu.VMEM((4, 4, rows, local), BF16),
        pltpu.VMEM(block, BF16),
        pltpu.VMEM((4, rows, hidden), BF16),
        pltpu.VMEM((rows, width), F32),
        pltpu.VMEM((rows, width), F32),
        pltpu.VMEM((3, 4, rows, local), BF16),
        pltpu.VMEM((4, rows, local), BF16),
        pltpu.VMEM((4, rows, local), BF16),
        pltpu.VMEM((4, rows // 2, local), BF16),
        pltpu.VMEM((4, rows // 2, local), BF16),
        pltpu.VMEM((4, rows, local), BF16),
        pltpu.VMEM((4, rows, local), BF16),
        pltpu.VMEM((4, rows // 2, local), BF16),
        pltpu.VMEM((4, rows // 2, local), BF16),
        pltpu.VMEM((4, rows, local), BF16),
        pltpu.VMEM((4, rows, local), BF16),
        pltpu.VMEM((4, 4, rows, LANES), BF16),
        pltpu.VMEM(block, BF16),
        pltpu.VMEM((rows, width), F32),
        pltpu.VMEM((3, 4, rows, local), BF16),
        pltpu.VMEM((group, LANES), F32),
        pltpu.VMEM((group, LANES), F32),
        pltpu.VMEM((group, 1), F32),
        pltpu.VMEM((group, LANES), BF16),
        pltpu.VMEM((group, LANES), BF16),
    ]
    sem_count = 106 + 9 * chips if inside else 60
    scratch += [pltpu.SemaphoreType.DMA((sem_count,)), pltpu.SemaphoreType.DMA((sem_count,))]
    scratch.append(pltpu.SemaphoreType.DMA((4,)))
    if inside:
        scratch += [
            pltpu.VMEM(attn_shape, BF16),
            pltpu.VMEM(ffn_shape, BF16),
            pltpu.VMEM(attn_shape, BF16),
            pltpu.VMEM(ffn_shape, BF16),
            pltpu.VMEM((chips, *attn_shape[1:]), BF16),
            pltpu.VMEM((chips, *ffn_shape[1:]), BF16),
            pltpu.VMEM((chips, *attn_shape[1:]), BF16),
            pltpu.VMEM((chips, *ffn_shape[1:]), BF16),
            pltpu.VMEM(sums, F32),
            pltpu.VMEM(sums, F32),
            pltpu.VMEM((8, LANES), F32),
            pltpu.VMEM((2, 8, *sums), F32),
            pltpu.VMEM((2, chips, *sums), F32),
            pltpu.VMEM((8, 8, LANES), F32),
            pltpu.VMEM((chips, 8, LANES), F32),
        ]
        last = (
            jax.ShapeDtypeStruct(vec.shape, F32),
            jax.ShapeDtypeStruct((8, LANES), F32),
            jax.ShapeDtypeStruct(attn_shape[1:], F32),
            jax.ShapeDtypeStruct(ffn_shape[1:], F32),
        )
    else:
        last = (
            jax.ShapeDtypeStruct(sums, F32),
            jax.ShapeDtypeStruct(sums, F32),
            jax.ShapeDtypeStruct(attn_shape, BF16),
            jax.ShapeDtypeStruct(ffn_shape, BF16),
        )
    return pl.pallas_call(
        functools.partial(layer_kernel, inside, chips),
        out_shape=(jax.ShapeDtypeStruct((rows, width), BF16), jax.ShapeDtypeStruct((rows, width), F32), *last),
        in_specs=[vmem, vmem, vmem, anywhere, vmem, source, source],
        out_specs=(vmem,) * 6,
        scratch_shapes=scratch,
        compiler_params=pltpu.CompilerParams(
            collective_id=0, has_side_effects=True, vmem_limit_bytes=VMEM_LIMIT
        ),
    )(frames, segments, spans, cot, vec, attn_src, ffn_src)


def adam_kernel(norm, *refs):
    clip = jnp.minimum(1.0, MAX_NORM / (norm[0, 0] + 1e-06))
    attn, ffn, vec = refs[0:4], refs[4:8], refs[8:12]
    attn_to, ffn_to, vec_to, norm_to = refs[12:16], refs[16:20], refs[20:23], refs[23]

    def update(source, target, rate, decay):
        master, first, second, grad = (ref[...] for ref in source)
        for ref, value in zip(target, adam_step(master, first, second, grad * clip, rate, decay)):
            ref[...] = value
        if len(target) > 3:
            target[3][...] = target[0][...].astype(BF16)

    update(attn, attn_to, RATE_ATTN, DECAY_RATE)
    update(ffn, ffn_to, RATE_FFN, DECAY_RATE)

    @pl.when(pl.program_id(0) == 0)
    def _():
        update(vec, vec_to, RATE_VEC, 0.0)
        norm_to[0, 0] = norm[0, 0]


def run_adam(norm, attn, ffn, vec):
    steps = 2

    def split(array):
        return pl.BlockSpec((array.shape[0] // steps, array.shape[1]), lambda i: (i, 0))

    whole = pl.BlockSpec(vec[0].shape, lambda i: (0, 0))
    scalar = pl.BlockSpec(memory_space=pltpu.SMEM)

    def shapes(array, copy):
        types = (F32, F32, F32, BF16) if copy else (F32, F32, F32)
        return tuple(jax.ShapeDtypeStruct(array.shape, t) for t in types)

    return pl.pallas_call(
        adam_kernel,
        grid=(steps,),
        out_shape=(
            *shapes(attn[0], True),
            *shapes(ffn[0], True),
            *shapes(vec[0], False),
            jax.ShapeDtypeStruct((1, 1), F32),
        ),
        in_specs=[scalar] + [split(attn[0])] * 4 + [split(ffn[0])] * 4 + [whole] * 4,
        out_specs=(*[split(attn[0])] * 4, *[split(ffn[0])] * 4, *[whole] * 3, scalar),
        compiler_params=pltpu.CompilerParams(vmem_limit_bytes=VMEM_LIMIT),
    )(norm, *attn, *ffn, *vec)


def per_device(
    frames,
    segment_ids,
    span_starts,
    cotangent,
    attn_master,
    attn_first,
    attn_second,
    ffn_master,
    ffn_first,
    ffn_second,
    vec_master,
    vec_first,
    vec_second,
):
    dp_count = lax.axis_size("dp")

    def gather_slabs(master):
        shard = master.astype(BF16)
        whole = lax.all_gather(shard, "dp", axis=1, tiled=True)
        return whole.reshape(shard.shape[0], SLABS, -1).transpose(1, 0, 2)

    inside = attn_master.shape[1] % 256 == 0 and ffn_master.shape[1] % 256 == 0 and dp_count in (4, 8)
    head = (frames[0], segment_ids, span_starts, cotangent[0], vec_master)
    if inside:
        output, frames_grad, vec_grad, norm, attn_owned, ffn_owned = run_layer(
            *head, attn_master, ffn_master, True, dp_count // 2
        )
    else:
        output, frames_grad, early, late, g_attn, g_ffn = run_layer(
            *head, gather_slabs(attn_master), gather_slabs(ffn_master), False, dp_count // 2
        )
        vec_local = jnp.concatenate([late[0:4], early[0:4], late[4:5], early[4:8]], axis=0)

        def scatter_slabs(slabs):
            whole = slabs.astype(F32).transpose(1, 0, 2).reshape(slabs.shape[1], -1)
            return lax.psum_scatter(whole, "dp", scatter_dimension=1, tiled=True)

        attn_owned = scatter_slabs(g_attn)
        ffn_owned = scatter_slabs(g_ffn)
        owned_squares = jnp.sum(attn_owned * attn_owned) + jnp.sum(ffn_owned * ffn_owned)
        vec_grad, total_squares = lax.psum((vec_local, owned_squares), ("seq", "dp"))
        norm = jnp.broadcast_to(jnp.sqrt(total_squares + jnp.sum(vec_grad * vec_grad)), (8, LANES))
    updated = run_adam(
        norm,
        (attn_master, attn_first, attn_second, attn_owned),
        (ffn_master, ffn_first, ffn_second, ffn_owned),
        (vec_master, vec_first, vec_second, vec_grad),
    )
    return (output[None], frames_grad[None], updated[-1].reshape(()), *updated[:-1])


def solution(mesh):
    return jax.shard_map(
        per_device,
        mesh=mesh,
        in_specs=(
            P("dp", "seq", None),
            P("dp", None),
            P("dp", None),
            P("dp", "seq", None),
            P("seq", "dp"),
            P("seq", "dp"),
            P("seq", "dp"),
            P("seq", "dp"),
            P("seq", "dp"),
            P("seq", "dp"),
            P(),
            P(),
            P(),
        ),
        out_specs=(
            P("dp", "seq", None),
            P("dp", "seq", None),
            P(),
            P("seq", "dp"),
            P("seq", "dp"),
            P("seq", "dp"),
            P("seq", "dp"),
            P("seq", "dp"),
            P("seq", "dp"),
            P("seq", "dp"),
            P("seq", "dp"),
            P(),
            P(),
            P(),
        ),
        check_vma=False,
    )
```

```python
import functools

import jax
import jax.numpy as jnp
from jax import lax
from jax.experimental import pallas as pl
from jax.experimental.pallas import tpu as pltpu
from jax.sharding import PartitionSpec as P

H = 16
SPAN = 10
STEP = 10

EPS_NORM = 1e-05
BETA_ONE = 0.9
BETA_TWO = 0.999
EPS_ADAM = 1e-08
RATE_ATTN = 0.12
RATE_FFN = 0.03
RATE_VEC = 0.5
DECAY_RATE = 0.01
MAX_NORM = 1.0
NEG_FILL = -1e30

SLABS = 8
LANES = 128
VMEM_LIMIT = 62 * 1024 * 1024
F32 = jnp.float32
BF16 = jnp.bfloat16
MESH = pl.DeviceIdType.MESH


def adam_step(master, first, second, grad, rate, decay):
    first_new = BETA_ONE * first + (1.0 - BETA_ONE) * grad
    second_new = BETA_TWO * second + (1.0 - BETA_TWO) * grad * grad
    first_hat = first_new * (1.0 / (1.0 - BETA_ONE**STEP))
    second_hat = second_new * (1.0 / (1.0 - BETA_TWO**STEP))
    master_new = master - rate * (first_hat / (jnp.sqrt(second_hat) + EPS_ADAM) + decay * master)
    return (master_new, first_new, second_new)


def nn(left, right):
    return lax.dot_general(left, right, (((1,), (0,)), ((), ())), preferred_element_type=F32)


def nt(left, right):
    return lax.dot_general(left, right, (((1,), (1,)), ((), ())), preferred_element_type=F32)


def tn(left, right):
    return lax.dot_general(left, right, (((0,), (0,)), ((), ())), preferred_element_type=F32)


def normalise(source):
    mean_val = jnp.mean(source, axis=-1, keepdims=True)
    centred = source - mean_val
    inv_std = lax.rsqrt(jnp.mean(centred * centred, axis=-1, keepdims=True) + EPS_NORM)
    return centred * inv_std, inv_std


def norm_back(grad_out, normed, inv_std, gain_row):
    scaled = grad_out * gain_row
    inner = (
        scaled
        - jnp.mean(scaled, axis=-1, keepdims=True)
        - normed * jnp.mean(scaled * normed, axis=-1, keepdims=True)
    )
    return inner * inv_std


def col_sum(value):
    return jnp.sum(value, axis=0, keepdims=True)


class Gather:
    def __init__(self, cp, buf, base, place, off, rows):
        self.cp, self.buf, self.b = cp, buf, base
        self.s, self.px, self.py, self.pd = place
        self.off, self.h = off, rows // 2

    def top(self, slot):
        return self.buf.at[slot, pl.ds(self.off, self.h)]

    def bot(self, slot):
        return self.buf.at[slot, pl.ds(self.off + self.h, self.h)]

    def c(self, part, slot, i, to):
        ref = part(slot)
        return self.cp(ref, ref, self.b + i, to)

    def start(self):
        self.c(self.top, self.s, 0, self.px).start()
        self.c(self.bot, self.s, 2, self.py).start()
        self.c(self.bot, self.s, 1, self.px).start()
        self.c(self.top, self.s, 3, self.py).start()

    def relay(self):
        self.c(self.top, self.px, 0, self.px).wait_recv()
        self.c(self.top, self.px, 4, self.py).start()
        self.c(self.bot, self.py, 2, self.py).wait_recv()
        self.c(self.bot, self.py, 5, self.px).start()

    def wait_x(self):
        self.c(self.bot, self.px, 1, self.px).wait_recv()

    def wait_y(self):
        self.c(self.top, self.py, 3, self.py).wait_recv()

    def wait_d(self):
        self.c(self.top, self.pd, 4, self.py).wait_recv()
        self.c(self.bot, self.pd, 5, self.px).wait_recv()

    def sent(self):
        for part, slot, i, to in (
            (self.top, self.s, 0, self.px),
            (self.bot, self.s, 2, self.py),
            (self.bot, self.s, 1, self.px),
            (self.top, self.s, 3, self.py),
            (self.top, self.px, 4, self.py),
            (self.bot, self.py, 5, self.px),
        ):
            self.c(part, slot, i, to).wait_send()


class Scatter:
    def __init__(self, cp, part, in_x, in_y, via_x, via_y, base, place):
        _, px, py, _ = place
        h = in_x.shape[1] // 2
        top, bot = pl.ds(0, h), pl.ds(h, h)
        self.to_x, self.to_y, self.via_x, self.via_y = part(1), part(2), via_x, via_y
        self.top, self.bot = top, bot
        far = part(3)
        self.copies = [
            cp(far.at[:, top], via_x, base, px),
            cp(far.at[:, bot], via_y, base + 1, py),
            cp(self.to_x.at[:, top], in_x.at[:, top], base + 2, px),
            cp(self.to_y.at[:, bot], in_y.at[:, bot], base + 3, py),
            cp(self.to_y.at[:, top], in_y.at[:, top], base + 4, py),
            cp(self.to_x.at[:, bot], in_x.at[:, bot], base + 5, px),
        ]

    def start(self, relation):
        for i in {3: (0, 1), 1: (2,), 2: (3,)}[relation]:
            self.copies[i].start()

    def relay(self):
        for i, ref, via, at in ((0, self.to_y, self.via_x, self.top), (1, self.to_x, self.via_y, self.bot)):
            self.copies[i].wait_recv()
            ref[:, at, :] = (ref[:, at, :].astype(F32) + via[...].astype(F32)).astype(BF16)
            self.copies[4 + i].start()

    def wait(self):
        for i in (2, 3, 4, 5):
            self.copies[i].wait_recv()

    def sent(self):
        for copy in self.copies:
            copy.wait_send()


class Line:
    def __init__(self, cp_dp, buf, base, chip, core, chips):
        self.cp, self.buf, self.b = cp_dp, buf, base
        self.z, self.core, self.n = chip, core, chips

    def c(self, shard, kind, hop):
        ref = self.buf.at[2 * shard + self.core]
        return self.cp(ref, ref, self.b + kind, 2 * (self.z + hop) + self.core)

    def has(self, hop):
        return jnp.logical_and(self.z + hop >= 0, self.z + hop < self.n)

    def across(self, shard):
        ref = self.buf.at[2 * shard + self.core]
        return self.cp(ref, ref, self.b + 6 + shard, 2 * self.z + 1 - self.core)

    def start_first(self):
        for step in (1, -1):
            kind = (1 - step) // 2
            far = self.has(3 * step)

            @pl.when(far)
            def _(kind=kind, step=step):
                self.c(self.z, 2 + kind, 2 * step).start()

            @pl.when(jnp.logical_and(jnp.logical_not(self.has(2 * step)), self.has(step)))
            def _(kind=kind, step=step):
                self.c(self.z, kind, step).start()

        self.across(self.z).start()

    def start_rest(self):
        for step in (1, -1):
            kind = (1 - step) // 2
            far = self.has(3 * step)

            @pl.when(far)
            def _(kind=kind, step=step):
                self.c(self.z, kind, step).start()

            @pl.when(jnp.logical_and(jnp.logical_not(far), self.has(2 * step)))
            def _(kind=kind, step=step):
                self.c(self.z, 2 + kind, 2 * step).start()
                self.c(self.z, kind, step).start()

    def relay(self):
        for kind, hop, on in ((2, -2, 1), (3, 2, -1)):

            @pl.when(jnp.logical_and(self.has(hop), self.has(on)))
            def _(kind=kind, hop=hop, on=on):
                self.c(self.z + hop, kind, hop).wait_recv()
                self.c(self.z + hop, kind + 2, on).start()
                self.across(self.z + hop).start()

    def settle(self):
        for kind, hop, on in ((0, -1, 0), (1, 1, 0), (2, -2, 1), (3, 2, -1), (4, -3, 0), (5, 3, 0)):
            due = self.has(hop)
            if on:
                due = jnp.logical_and(due, jnp.logical_not(self.has(on)))

            @pl.when(due)
            def _(kind=kind, hop=hop):
                self.c(self.z + hop, kind, hop).wait_recv()
                self.across(self.z + hop).start()

        other = 1 - self.core
        for shard in range(self.n):
            ref = self.buf.at[2 * shard + other]
            self.cp(ref, ref, self.b + 6 + shard, 2 * self.z + other).wait_recv()

    def sent(self):
        for shard in range(self.n):
            self.across(shard).wait_send()
        for kind, hop in ((0, 1), (1, -1), (2, 2), (3, -2)):

            @pl.when(self.has(hop))
            def _(kind=kind, hop=hop):
                self.c(self.z, kind, hop).wait_send()

        for kind, hop, on in ((4, -2, 1), (5, 2, -1)):

            @pl.when(jnp.logical_and(self.has(hop), self.has(on)))
            def _(kind=kind, hop=hop, on=on):
                self.c(self.z + hop, kind, on).wait_send()


class LineSum:
    def __init__(self, cp_dp, part, cross, landed, base, chip, core, chips):
        self.cp, self.part, self.cross, self.landed, self.b = cp_dp, part, cross, landed, base
        self.z, self.core, self.n = chip, core, chips

    def mine(self, shard):
        return 2 * shard + self.core

    def has(self, hop):
        return jnp.logical_and(self.z + hop >= 0, self.z + hop < self.n)

    def across(self, shard, half):
        rows = self.part.shape[1] // 2
        at = pl.ds(half * rows, rows)
        src = self.part.at[2 * shard + 1 - self.core, at]
        return self.cp(src, self.cross.at[shard, at], self.b + 6 + 2 * shard + half, 2 * self.z + 1 - self.core)

    def direct(self, kind, hop):
        src = self.part.at[self.mine(self.z + hop)]
        return self.cp(src, self.landed.at[self.z], self.b + kind, 2 * (self.z + hop) + self.core)

    def via(self, kind, hop, step):
        src = self.part.at[self.mine(self.z + hop)]
        return self.cp(src, self.landed.at[self.z + step], self.b + kind, 2 * (self.z + step) + self.core)

    def start(self, half):
        for shard in range(self.n):
            self.across(shard, half).start()

    def add(self, shard, ref, first, rows):
        size = min(256, rows)

        def one(i, carry):
            at = pl.ds(pl.multiple_of(first + i * size, size), size)
            total = self.part[self.mine(shard), at, :].astype(F32) + ref[at, :].astype(F32)
            self.part[self.mine(shard), at, :] = total.astype(BF16)
            return carry

        lax.fori_loop(0, rows // size, one, 0)

    def fold(self, half):
        rows = self.part.shape[1] // 2
        for shard in range(self.n):
            self.across(shard, half).wait_recv()
            self.add(shard, self.cross.at[shard], half * rows, rows)

    def launch(self):
        for step in (1, -1):
            kind = (1 - step) // 2
            far = self.has(3 * step)

            @pl.when(far)
            def _(kind=kind, step=step):
                self.via(4 + kind, 3 * step, step).start()

            @pl.when(jnp.logical_and(jnp.logical_not(far), self.has(step)))
            def _(kind=kind, step=step):
                self.direct(kind, step).start()

    def follow(self):
        for step in (1, -1):
            kind = (1 - step) // 2

            @pl.when(self.has(3 * step))
            def _(kind=kind, step=step):
                self.direct(2 + kind, 2 * step).start()
                self.direct(kind, step).start()

            @pl.when(jnp.logical_and(jnp.logical_not(self.has(3 * step)), self.has(2 * step)))
            def _(kind=kind, step=step):
                @pl.when(self.has(-step))
                def _():
                    here = self.landed.at[self.z]
                    self.cp(here, here, self.b + 4 + kind, 2 * (self.z + step) + self.core).wait_recv()
                    self.add(self.z + 2 * step, here, 0, self.part.shape[1])

                self.direct(2 + kind, 2 * step).start()

    def finish(self, owned):
        owned[...] = self.part[self.mine(self.z)].astype(F32)
        for kind, hop in ((0, -1), (1, 1), (2, -2), (3, 2)):

            @pl.when(self.has(hop))
            def _(kind=kind, hop=hop):
                there = self.landed.at[self.z + hop]
                self.cp(there, there, self.b + kind, 2 * (self.z + hop) + self.core).wait_recv()
                owned[...] += there[...].astype(F32)

    def sent(self):
        for shard in range(self.n):
            for half in range(2):
                self.across(shard, half).wait_send()
        for step in (1, -1):
            kind = (1 - step) // 2
            for hops in (1, 2):

                @pl.when(self.has(hops * step))
                def _(kind=kind, step=step, hops=hops):
                    self.direct(kind + 2 * (hops - 1), hops * step).wait_send()

            @pl.when(self.has(3 * step))
            def _(kind=kind, step=step):
                self.via(4 + kind, 3 * step, step).wait_send()


class Everyone:
    def __init__(self, cp_any, plane, line, base, s, chip, core, chips):
        self.cp, self.plane, self.line, self.b = cp_any, plane, line, base
        self.s, self.z, self.core, self.n = s, chip, core, chips
        self.me = 2 * s + core

    def to_plane(self, o):
        p = lax.rem(self.me + o, 8)
        return self.cp(self.plane.at[self.me], self.plane.at[self.me], self.b + o, p // 2, 2 * self.z + lax.rem(p, 2))

    def from_plane(self, o):
        p = lax.rem(self.me - o + 8, 8)
        return self.cp(self.plane.at[p], self.plane.at[p], self.b + o, p // 2, 2 * self.z + lax.rem(p, 2))

    def to_line(self, o):
        p = lax.rem(self.z + o, self.n)
        return self.cp(self.line.at[self.z], self.line.at[self.z], self.b + 7 + o, self.s, 2 * p + self.core)

    def from_line(self, o):
        p = lax.rem(self.z - o + self.n, self.n)
        return self.cp(self.line.at[p], self.line.at[p], self.b + 7 + o, self.s, 2 * p + self.core)

    def start(self, value):
        self.plane[self.me] = value
        for o in range(1, 8):
            self.to_plane(o).start()

    def middle(self):
        for o in range(1, 8):
            self.from_plane(o).wait_recv()
        total = self.plane[0]
        for p in range(1, 8):
            total = total + self.plane[p]
        self.line[self.z] = total
        for o in range(1, self.n):
            self.to_line(o).start()

    def end(self):
        for o in range(1, self.n):
            self.from_line(o).wait_recv()
        total = self.line[0]
        for p in range(1, self.n):
            total = total + self.line[p]
        return total

    def sent(self):
        for o in range(1, 8):
            self.to_plane(o).wait_send()
        for o in range(1, self.n):
            self.to_line(o).wait_send()


def layer_kernel(inside, chips, *refs):
    refs = list(refs)

    def take(count):
        head = refs[:count]
        del refs[:count]
        return head

    frames, segments, spans, cot, vec, attn_src, ffn_src = take(7)
    if inside:
        out, frames_grad, vec_out, norm_out, attn_owned, ffn_owned = take(6)
    else:
        out, frames_grad, early, late, g_attn, g_ffn = take(6)
        w_attn, w_ffn = attn_src, ffn_src
    fr_g, cot_g, a_g, wp, qa, ka, va, kt, att, b_g, gp_g = take(11)
    act_g = fr_g
    resid, own, part, in_x, in_y, via_x, via_y, in_x2, in_y2, via_x2, via_y2 = take(11)
    gsend, gm, dom, ga_g, gres, dqkv, dk_acc, dv_acc, mask_col, seg_q, seg_k = take(11)
    send_sem, recv_sem, local_sem = take(3)
    if inside:
        w_attn, w_ffn, g_attn, g_ffn, cross_a, cross_f, landed_a, landed_f = take(8)
        early, late, squares, planes, lines, planes_s, lines_s = take(7)
    s = lax.axis_index("seq")
    d = lax.axis_index("dp")
    core = lax.rem(d, 2)
    sib = d + 1 - 2 * core

    def peer(r):
        half = r // 2
        high = lax.rem(s // 2 + half, 2)
        low = lax.rem(lax.rem(s, 2) + (r - 2 * half), 2)
        return 2 * high + low

    px, py, pd = peer(1), peer(2), peer(3)
    place = (s, px, py, pd)

    def cp(src, dst, i, to):
        return pltpu.make_async_remote_copy(
            src_ref=src,
            dst_ref=dst,
            send_sem=send_sem.at[i],
            recv_sem=recv_sem.at[i],
            device_id=(to, d),
            device_id_type=MESH,
        )

    def cp_any(src, dst, i, to_seq, to_dp):
        return pltpu.make_async_remote_copy(
            src_ref=src,
            dst_ref=dst,
            send_sem=send_sem.at[i],
            recv_sem=recv_sem.at[i],
            device_id=(to_seq, to_dp),
            device_id_type=MESH,
        )

    def cp_dp(src, dst, i, to):
        return cp_any(src, dst, i, s, to)

    def cp_sib(src, dst, i):
        return cp_any(src, dst, i, s, sib)


    rows = frames.shape[0]
    width = frames.shape[1]
    local = width // 4
    slab_a = w_attn.shape[2]
    slab_f = w_ffn.shape[2]
    per_a = width // slab_a
    per_f = width // slab_f
    tile = 256
    chunk = 128
    small = 64

    cot_load = pltpu.make_async_copy(cot, cot_g.at[s], local_sem.at[0])
    cot_load.start()
    chip = d // 2
    loads = []
    if inside:
        loads = [pltpu.make_async_copy(attn_src, own.at[:, :slab_a], local_sem.at[1])]
        for i, spot in enumerate((dk_acc, dv_acc)):
            at = slice(i * LANES, (i + 1) * LANES)
            loads.append(pltpu.make_async_copy(ffn_src.at[:, at], spot, local_sem.at[2 + i]))
        for load in loads:
            load.start()

    barrier = pltpu.get_barrier_semaphore()
    if inside:
        for o in range(1, 8):
            p = lax.rem(2 * s + core + o, 8)
            to = (p // 2, 2 * chip + lax.rem(p, 2))
            pl.semaphore_signal(barrier, inc=1, device_id=to, device_id_type=MESH)
        for o in range(1, chips):
            to = (s, 2 * lax.rem(chip + o, chips) + core)
            pl.semaphore_signal(barrier, inc=1, device_id=to, device_id_type=MESH)
        pl.semaphore_wait(barrier, 6 + chips)
    else:
        for to in (px, py, pd):
            pl.semaphore_signal(barrier, inc=1, device_id=(to, d), device_id_type=MESH)
        pl.semaphore_signal(barrier, inc=1, device_id=(s, sib), device_id_type=MESH)
        pl.semaphore_wait(barrier, 4)

    fr_g[s] = frames[...]
    frames_in = Gather(cp, fr_g, 0, place, 0, rows)
    frames_in.start()
    cot_in = Gather(cp, cot_g, 15, place, 0, rows)
    if inside:
        line_a = Line(cp_dp, w_attn, 60, chip, core, chips)
        line_f = Line(cp_dp, w_ffn, 66 + chips, chip, core, chips)
        loads[0].wait()
        w_attn[d] = own[:, :slab_a].astype(BF16)
        line_a.start_first()
    half = rows // 2
    wp_off = pl.multiple_of(core * half, half)
    wp_in = Gather(cp, wp, 6, place, wp_off, half)
    wp_cross = [
        cp_sib(wp.at[p, pl.ds(wp_off, half)], wp.at[p, pl.ds(wp_off, half)], 12 + i) for i, p in enumerate((px, py, pd))
    ]
    early[...] = jnp.zeros_like(early)
    late[...] = jnp.zeros_like(late)

    group = 4 * rows
    position = lax.broadcasted_iota(jnp.int32, (group, spans.shape[1]), 0)
    starts = spans[...]
    covered = jnp.logical_and(position >= starts, position < starts + SPAN)
    mask_col[...] = jnp.max(jnp.where(covered, 1.0, 0.0), axis=1, keepdims=True)
    second = jnp.transpose(jnp.broadcast_to(segments[...].astype(F32), (LANES, group)))
    seg_lane = lax.broadcasted_iota(jnp.int32, (group, LANES), 1)
    fill = jnp.where(seg_lane == 0, second, jnp.where(seg_lane == 1, 1.0 - second, 0.0)) * NEG_FILL
    seg_q[...] = fill.astype(BF16)
    ones = jnp.where(seg_lane < 5, 1.0, 0.0)
    seg_k[...] = jnp.where(seg_lane == 0, 1.0 - second, jnp.where(seg_lane == 1, second, ones)).astype(BF16)
    half = rows // 2

    lane = lax.broadcasted_iota(jnp.int32, (rows, LANES), 1)
    low_head = lane < LANES // 2
    q_bias = vec[2:3, pl.ds(pl.multiple_of(s * local, local), local)]
    v_bias = vec[3:4, pl.ds(pl.multiple_of(s * local, local), local)]

    def weight_rows(first, count, start, size):
        return jnp.concatenate([w_attn[first + i, start : start + size, :] for i in range(count)], axis=1)

    def enter(blk):
        def norm_rows(i, carry):
            at = pl.ds(pl.multiple_of(i * chunk, chunk), chunk)
            at_all = pl.ds(pl.multiple_of(blk * rows + i * chunk, chunk), chunk)
            x = jnp.where(mask_col[at_all, :] > 0.0, vec[8:9, :], fr_g[blk, at, :].astype(F32))
            normed, _ = normalise(x)
            a_g[blk, at, :] = (normed * vec[0:1, :] + vec[1:2, :]).astype(BF16)
            return carry

        lax.fori_loop(0, rows // chunk, norm_rows, 0)

    def project_in(blk):
        a = a_g[blk]
        at_all = pl.ds(pl.multiple_of(blk * rows, rows), rows)
        q = (nt(a, weight_rows(0, per_a, 0, local)) + q_bias).astype(BF16).astype(F32) * 0.125
        for pair in range(2):
            both = q[:, pair * LANES : (pair + 1) * LANES]
            for h in range(2):
                keep = low_head if h == 0 else jnp.logical_not(low_head)
                qa[2 * pair + h, blk, :, :LANES] = jnp.where(keep, both, 0.0).astype(BF16)
                qa[2 * pair + h, blk, :, LANES:] = seg_q[at_all, :]
        k = nt(a, weight_rows(per_a, per_a, 0, local)).astype(BF16)
        for pair in range(2):
            both = k[:, pair * LANES : (pair + 1) * LANES]
            ka[pair, at_all, :LANES] = both
            ka[pair, at_all, LANES:] = seg_k[at_all, :]
            kt[pair, :, at_all] = jnp.transpose(both)
        v = (nt(a, weight_rows(2 * per_a, per_a, 0, local)) + v_bias).astype(BF16)
        for pair in range(2):
            va[pair, at_all, :] = v[:, pair * LANES : (pair + 1) * LANES]

    enter(s)
    if inside:
        for i, spot in enumerate((dk_acc, dv_acc)):
            loads[1 + i].wait()
            w_ffn[d, :, i * LANES : (i + 1) * LANES] = spot[...].astype(BF16)
    if inside:
        line_a.start_rest()
        line_a.relay()
    frames_in.relay()
    frames_in.wait_x()
    enter(px)
    frames_in.wait_y()
    enter(py)
    frames_in.wait_d()
    enter(pd)
    if inside:
        line_a.settle()
        line_f.start_first()
    for i in range(per_a):
        wp[s, :, i * slab_a : (i + 1) * slab_a] = w_attn[3 * per_a + i]
    wp_in.start()
    lax.fori_loop(0, 4, lambda j, carry: (project_in(j), carry)[1], 0)
    cot_load.wait()

    def att_x(j, slot):
        return cp(att.at[slot, j], att.at[slot, j], 21 + j, px)

    def att_y(j, slot):
        return cp(att.at[slot, j], att.at[slot, j], 25 + j, py)

    def att_relay(j, start):
        even = lax.rem(j, 2) == 0

        @pl.when(even)
        def _():
            if start:
                att_x(j, px).wait_recv()
                cp(att.at[px, j], att.at[px, j], 29 + j, py).start()
            else:
                cp(att.at[px, j], att.at[px, j], 29 + j, py).wait_send()

        @pl.when(jnp.logical_not(even))
        def _():
            if start:
                att_y(j, py).wait_recv()
                cp(att.at[py, j], att.at[py, j], 29 + j, px).start()
            else:
                cp(att.at[py, j], att.at[py, j], 29 + j, px).wait_send()

    def attend(j, carry):
        @pl.when(j == 2)
        def _():
            wp_in.relay()
            if inside:
                line_f.start_rest()
                line_f.relay()

        for pair in range(2):
            outs = []
            for h in range(2):
                head = 2 * pair + h
                scores = nt(qa[head, j], ka[pair])
                peak = jnp.max(scores, axis=-1, keepdims=True)
                terms = jnp.exp(scores - peak)
                total = jnp.sum(terms, axis=-1, keepdims=True)
                probs = (terms * (1.0 / total)).astype(BF16)
                outs.append(nn(probs, va[pair]))
                log_total = -(peak + jnp.log(total))
                part_one = log_total.astype(BF16).astype(F32)
                rest = log_total - part_one
                part_two = rest.astype(BF16).astype(F32)
                part_three = rest - part_two
                aug = qa[head, j, :, LANES:].astype(F32)
                aug = jnp.where(lane == 2, part_one, aug)
                aug = jnp.where(lane == 3, part_two, aug)
                aug = jnp.where(lane == 4, part_three, aug)
                qa[head, j, :, LANES:] = aug.astype(BF16)
            att[s, j, :, pair * LANES : (pair + 1) * LANES] = jnp.where(low_head, outs[0], outs[1]).astype(BF16)
        att_x(j, s).start()
        att_y(j, s).start()

        @pl.when(j > 0)
        def _():
            att_relay(j - 1, True)

        return carry

    lax.fori_loop(0, 4, attend, 0)
    wp_in.wait_x()
    wp_cross[0].start()
    wp_in.wait_y()
    wp_cross[1].start()
    wp_in.wait_d()
    wp_cross[2].start()
    att_relay(3, True)
    other_off = pl.multiple_of((1 - core) * half, half)
    for i, p in enumerate((px, py, pd)):
        cp_sib(wp.at[p, pl.ds(other_off, half)], wp.at[p, pl.ds(other_off, half)], 12 + i).wait_recv()

    def project(j, carry):
        @pl.when(j == 1)
        def _():
            cot_in.start()

        even = lax.rem(j, 2) == 0

        @pl.when(even)
        def _():
            att_y(j, py).wait_recv()
            cp(att.at[pd, j], att.at[pd, j], 29 + j, py).wait_recv()

        @pl.when(jnp.logical_not(even))
        def _():
            att_x(j, px).wait_recv()
            cp(att.at[pd, j], att.at[pd, j], 29 + j, px).wait_recv()

        left = jnp.concatenate([att[p, j] for p in range(4)], axis=1)
        for i in range(width // tile):
            right = jnp.concatenate([wp[p, :, i * tile : (i + 1) * tile] for p in range(4)], axis=0)
            own[:, i * tile : (i + 1) * tile] = nn(left, right)

        def norm_rows(i, inner):
            at = pl.ds(pl.multiple_of(i * chunk, chunk), chunk)
            at_all = pl.ds(pl.multiple_of(j * rows + i * chunk, chunk), chunk)
            x = jnp.where(mask_col[at_all, :] > 0.0, vec[8:9, :], fr_g[j, at, :].astype(F32))
            total = x + own[at, :] + vec[4:5, :]

            @pl.when(j == s)
            def _():
                resid[at, :] = total

            normed, _ = normalise(total)
            b_g[j, at, :] = (normed * vec[5:6, :] + vec[6:7, :]).astype(BF16)
            return inner

        lax.fori_loop(0, rows // chunk, norm_rows, 0)
        return carry

    lax.fori_loop(0, 4, project, 0)
    cot_in.relay()
    if inside:
        line_f.settle()
    frames_in.sent()

    def feed(r):
        blk = peer(r)

        def hidden_tile(i, carry):
            at = pl.ds(pl.multiple_of(i * tile, tile), tile)
            w_in = jnp.concatenate([w_ffn[k, at, :] for k in range(per_f)], axis=1)
            w_out = jnp.concatenate([w_ffn[per_f + k, at, :] for k in range(per_f)], axis=1)
            pre = nt(b_g[blk], w_in) + vec[pl.ds(9 + s, 1), at]
            grad_act = nt(cot_g[blk], w_out)
            cdf = 0.5 * (1.0 + lax.erf(pre * 0.7071067811865476))
            act_g[blk, :, at] = (pre * cdf).astype(BF16)
            density = jnp.exp(-0.5 * pre * pre) * 0.3989422804014327
            grad_pre = ((cdf + pre * density) * grad_act).astype(BF16)
            gp_g[blk, :, at] = grad_pre
            early[pl.ds(4 + s, 1), at] += col_sum(grad_pre.astype(F32))
            return carry

        lax.fori_loop(0, w_ffn.shape[1] // tile, hidden_tile, 0)
        left = gp_g[blk]
        for k in range(per_f):
            at = slice(k * slab_f, (k + 1) * slab_f)
            value = nn(left, w_ffn[k])
            if r == 0:
                own[:, at] = value
            else:
                part[r - 1, k] = value.astype(BF16)

    sum_b = Scatter(cp, lambda r: part.at[r - 1], in_x, in_y, via_x, via_y, 33, place)
    cot_in.wait_d()
    feed(3)
    sum_b.start(3)
    cot_in.wait_x()
    feed(1)
    sum_b.start(1)
    cot_in.wait_y()
    feed(2)
    sum_b.start(2)
    sum_b.relay()
    feed(0)

    def ffn_grads(i, carry):
        at = pl.ds(pl.multiple_of(i * tile, tile), tile)
        for left, right, first in ((gp_g, b_g, 0), (act_g, cot_g, per_f)):
            turned = jnp.transpose(jnp.concatenate([left[p, :, at] for p in range(4)], axis=0))
            for k in range(per_f):
                cols = jnp.concatenate([right[p, :, k * slab_f : (k + 1) * slab_f] for p in range(4)], axis=0)
                g_ffn[first + k, at, :] = nn(turned, cols).astype(BF16)
        return carry

    f_tiles = w_ffn.shape[1] // tile
    if inside:
        sum_f = LineSum(cp_dp, g_ffn, cross_f, landed_f, 72 + 2 * chips, chip, core, chips)
        sum_g = LineSum(cp_dp, g_attn, cross_a, landed_a, 78 + 4 * chips, chip, core, chips)
        all_early = Everyone(cp_any, planes.at[0], lines.at[0], 84 + 6 * chips, s, chip, core, chips)
        all_late = Everyone(cp_any, planes.at[1], lines.at[1], 91 + 7 * chips, s, chip, core, chips)
        all_squares = Everyone(cp_any, planes_s, lines_s, 98 + 8 * chips, s, chip, core, chips)
    def ffn_grads_sent(i, carry):
        if inside:

            @pl.when(i == f_tiles // 2)
            def _():
                sum_f.start(0)

        return ffn_grads(i, carry)

    lax.fori_loop(0, f_tiles, ffn_grads_sent, 0)
    if inside:
        sum_f.start(1)
    if inside:
        sum_f.fold(0)
        sum_f.fold(1)
        sum_f.launch()

    def out_part(blk, k):
        return nn(act_g[blk], w_ffn[per_f + k])

    for j in range(4):
        att_x(j, s).wait_send()
        att_y(j, s).wait_send()
        att_relay(j, False)
    sum_o = Scatter(cp, lambda r: att.at[peer(r)], in_x2, in_y2, via_x2, via_y2, 48, place)
    for r in (3, 1, 2):
        for k in range(per_f):
            att[peer(r), k] = out_part(peer(r), k).astype(BF16)
    sum_b.wait()
    sum_o.start(3)

    def landed(from_x, from_y, at):
        tiles = range(from_x.shape[0])
        return jnp.concatenate([from_x[t, at, :].astype(F32) + from_y[t, at, :].astype(F32) for t in tiles], axis=1)

    def back_two(i, carry):
        at = pl.ds(pl.multiple_of(i * small, small), small)
        grad_b = own[at, :] + landed(in_x, in_y, at)
        normed, inv_std = normalise(resid[at, :])
        grad_y = cot_g[s, at, :].astype(F32)
        grad_resid = grad_y + norm_back(grad_b, normed, inv_std, vec[5:6, :])
        gres[at, :] = grad_resid
        low = grad_resid.astype(BF16)
        ga_g[s, at, :] = low
        early[0:1, :] += col_sum(low.astype(F32))
        early[1:2, :] += col_sum(grad_b * normed)
        early[2:3, :] += col_sum(grad_b)
        early[3:4, :] += col_sum(grad_y)
        return carry

    lax.fori_loop(0, rows // small, back_two, 0)

    for i, r in enumerate((3, 1, 2)):
        gsend[r] = nt(ga_g[s], wp[peer(r)]).astype(BF16)
        cp(gsend.at[r], gm.at[s], 39 + i, peer(r)).start()
    gm[s] = nt(ga_g[s], wp[s]).astype(BF16)
    ga_in = Gather(cp, ga_g, 42, place, 0, rows)
    ga_in.start()
    sum_b.sent()

    def spread(j):
        for pair in range(2):
            both = gm[j, :, pair * LANES : (pair + 1) * LANES].astype(F32)
            dom[2 * pair, j] = jnp.where(low_head, both, 0.0).astype(BF16)
            dom[2 * pair + 1, j] = jnp.where(low_head, 0.0, both).astype(BF16)

    def arrive(i, r):
        cp(gsend.at[r], gm.at[peer(r)], 39 + i, peer(r)).wait_recv()
        spread(peer(r))

    spread(s)

    def back_pair(pair, first, second):
        dk_acc[...] = jnp.zeros_like(dk_acc)
        dv_acc[...] = jnp.zeros_like(dv_acc)

        def back_block(r, carry):
            j = peer(r)
            for at_block, task in ((1, first), (3, second)):
                if task is not None:
                    pl.when(r == at_block)(task)
            sides = []
            for h in range(2):
                head = 2 * pair + h
                probs = jnp.exp(nt(ka[pair], qa[head, j]))
                grad_probs = nt(va[pair], dom[head, j])
                delta = jnp.sum(probs * grad_probs, axis=0, keepdims=True)
                grad_scores = (probs * (grad_probs - delta)).astype(BF16)
                dv_acc[...] += nn(probs.astype(BF16), dom[head, j])
                dk_acc[...] += nn(grad_scores, qa[head, j, :, :LANES])
                sides.append(nn(kt[pair], grad_scores))
            half_lane = LANES // 2
            turned = jnp.concatenate([sides[0][:half_lane], sides[1][half_lane:]], axis=0)
            dqkv[0, j, :, pair * LANES : (pair + 1) * LANES] = (jnp.transpose(turned) * 0.125).astype(BF16)
            return carry

        lax.fori_loop(0, 4, back_block, 0)
        for j in range(4):
            at = slice(j * rows, (j + 1) * rows)
            dqkv[1, j, :, pair * LANES : (pair + 1) * LANES] = dk_acc[at, :].astype(BF16)
            dqkv[2, j, :, pair * LANES : (pair + 1) * LANES] = dv_acc[at, :].astype(BF16)

    def after_own():
        arrive(1, 1)
        arrive(2, 2)

    def after_near():
        arrive(0, 3)
        if inside:
            sum_f.follow()
            all_early.start(early[...])

    back_pair(0, after_own, after_near)
    back_pair(1, None, ga_in.relay)

    sum_a = Scatter(cp, lambda r: part.at[r - 1], in_x, in_y, via_x, via_y, 54, place)

    def grad_in(r):
        blk = peer(r)
        left = jnp.concatenate([dqkv[c, blk] for c in range(3)], axis=1)
        for k in range(per_a):
            at = slice(k * slab_a, (k + 1) * slab_a)
            right = jnp.concatenate([w_attn[c * per_a + k] for c in range(3)], axis=0)
            value = nn(left, right)
            if r == 0:
                own[:, at] = value
            else:
                per_tile = slab_a // tile
                for t in range(per_tile):
                    part[r - 1, k * per_tile + t] = value[:, t * tile : (t + 1) * tile].astype(BF16)

    for r in (3, 1, 2):
        grad_in(r)
        sum_a.start(r)
    grad_in(0)

    my_cols = pl.ds(pl.multiple_of(s * local, local), local)
    for j in range(4):
        late[2:3, my_cols] += col_sum(dqkv[0, j].astype(F32))
        late[3:4, my_cols] += col_sum(dqkv[2, j].astype(F32))

    def attn_grads(c):
        turned = jnp.transpose(jnp.concatenate([dqkv[c, p] for p in range(4)], axis=0))
        for k in range(per_a):
            cols = jnp.concatenate([a_g[p, :, k * slab_a : (k + 1) * slab_a] for p in range(4)], axis=0)
            g_attn[c * per_a + k] = nn(turned, cols).astype(BF16)

    attn_grads(0)
    attn_grads(1)
    attn_grads(2)
    ga_in.wait_x()
    ga_in.wait_y()
    ga_in.wait_d()
    turned = jnp.transpose(jnp.concatenate([att[s, p] for p in range(4)], axis=0))
    for k in range(per_a):
        cols = jnp.concatenate([ga_g[p, :, k * slab_a : (k + 1) * slab_a] for p in range(4)], axis=0)
        g_attn[3 * per_a + k] = nn(turned, cols).astype(BF16)

    if inside:
        sum_g.start(0)
        sum_g.start(1)
    sum_a.relay()
    if inside:
        sum_g.fold(0)
        sum_g.fold(1)
        sum_g.launch()
    if inside:
        sum_f.finish(ffn_owned)
        ffn_squares = col_sum(ffn_owned[...] * ffn_owned[...])
        squares[...] = jnp.zeros_like(squares)
        sum_g.follow()
    sum_a.wait()
    sum_o.start(1)
    sum_o.start(2)
    sum_o.relay()

    def back_one(i, carry):
        at = pl.ds(pl.multiple_of(i * small, small), small)
        at_all = pl.ds(pl.multiple_of(s * rows + i * small, small), small)
        grad_a = own[at, :] + landed(in_x, in_y, at)
        masked = mask_col[at_all, :] > 0.0
        normed, inv_std = normalise(jnp.where(masked, vec[8:9, :], frames[at, :].astype(F32)))
        grad_x = gres[at, :] + norm_back(grad_a, normed, inv_std, vec[0:1, :])
        frames_grad[at, :] = jnp.where(masked, 0.0, grad_x)
        late[0:1, :] += col_sum(grad_a * normed)
        late[1:2, :] += col_sum(grad_a)
        late[4:5, :] += col_sum(jnp.where(masked, grad_x, 0.0))
        return carry

    lax.fori_loop(0, rows // small, back_one, 0)
    if inside:
        all_late.start(late[...])
        all_early.middle()
        sum_g.finish(attn_owned)
        attn_squares = col_sum(attn_owned[...] * attn_owned[...])
        owned_squares = sum(attn_squares[:, i * LANES : (i + 1) * LANES] for i in range(slab_a // LANES))
        owned_squares += sum(ffn_squares[:, i * LANES : (i + 1) * LANES] for i in range(slab_f // LANES))
        squares[0:1, :] = owned_squares
        all_squares.start(squares[...])
        all_late.middle()
        whole_early = all_early.end()
        all_squares.middle()
        whole_late = all_late.end()
        vec_out[0:4, :] = whole_late[0:4]
        vec_out[4:8, :] = whole_early[0:4]
        vec_out[8:9, :] = whole_late[4:5]
        vec_out[9:13, :] = whole_early[4:8]
        vec_square = col_sum(vec_out[...] * vec_out[...])

    sum_o.wait()
    for k in range(per_f):
        at = slice(k * slab_f, (k + 1) * slab_f)
        total = out_part(s, k) + resid[:, at] + in_x2[k].astype(F32) + in_y2[k].astype(F32) + vec[7:8, at]
        out[:, at] = total.astype(BF16)

    if inside:
        whole_squares = all_squares.end()
        total = jnp.sum(whole_squares[0:1], axis=1, keepdims=True) + jnp.sum(vec_square, axis=1, keepdims=True)
        norm_out[...] = jnp.broadcast_to(jnp.sqrt(total), norm_out.shape)
        line_a.sent()
        line_f.sent()
        sum_f.sent()
        sum_g.sent()
        all_early.sent()
        all_late.sent()
        all_squares.sent()

    wp_in.sent()
    for copy in wp_cross:
        copy.wait_send()
    cot_in.sent()

    for i, r in enumerate((3, 1, 2)):
        cp(gsend.at[r], gm.at[s], 39 + i, peer(r)).wait_send()
    ga_in.sent()
    sum_a.sent()
    sum_o.sent()


def run_layer(frames, segments, spans, cot, vec, attn_src, ffn_src, inside, chips):
    rows, width = frames.shape
    group = 4 * rows
    local = width // 4
    slab_count = 2 * chips if inside else SLABS
    hidden = ffn_src.shape[0] if inside else ffn_src.shape[1]
    attn_shape = (slab_count, local, attn_src.shape[-1])
    ffn_shape = (slab_count, hidden, ffn_src.shape[-1])
    vmem = pl.BlockSpec(memory_space=pltpu.VMEM)
    anywhere = pl.BlockSpec(memory_space=pl.ANY)
    source = anywhere if inside else vmem
    block = (4, rows, width)
    sums = (8, width)
    scratch = [
        pltpu.VMEM(block, BF16),
        pltpu.VMEM(block, BF16),
        pltpu.VMEM(block, BF16),
        pltpu.VMEM((4, local, width), BF16),
        pltpu.VMEM((4, 4, rows, 2 * LANES), BF16),
        pltpu.VMEM((2, group, 2 * LANES), BF16),
        pltpu.VMEM((2, group, LANES), BF16),
        pltpu.VMEM((2, LANES, group), BF16),
        pltpu.VMEM((4, 4, rows, local), BF16),
        pltpu.VMEM(block, BF16),
        pltpu.VMEM((4, rows, hidden), BF16),
        pltpu.VMEM((rows, width), F32),
        pltpu.VMEM((rows, width), F32),
        pltpu.VMEM((3, 4, rows, local), BF16),
        pltpu.VMEM((4, rows, local), BF16),
        pltpu.VMEM((4, rows, local), BF16),
        pltpu.VMEM((4, rows // 2, local), BF16),
        pltpu.VMEM((4, rows // 2, local), BF16),
        pltpu.VMEM((4, rows, local), BF16),
        pltpu.VMEM((4, rows, local), BF16),
        pltpu.VMEM((4, rows // 2, local), BF16),
        pltpu.VMEM((4, rows // 2, local), BF16),
        pltpu.VMEM((4, rows, local), BF16),
        pltpu.VMEM((4, rows, local), BF16),
        pltpu.VMEM((4, 4, rows, LANES), BF16),
        pltpu.VMEM(block, BF16),
        pltpu.VMEM((rows, width), F32),
        pltpu.VMEM((3, 4, rows, local), BF16),
        pltpu.VMEM((group, LANES), F32),
        pltpu.VMEM((group, LANES), F32),
        pltpu.VMEM((group, 1), F32),
        pltpu.VMEM((group, LANES), BF16),
        pltpu.VMEM((group, LANES), BF16),
    ]
    sem_count = 106 + 9 * chips if inside else 60
    scratch += [pltpu.SemaphoreType.DMA((sem_count,)), pltpu.SemaphoreType.DMA((sem_count,))]
    scratch.append(pltpu.SemaphoreType.DMA((4,)))
    if inside:
        scratch += [
            pltpu.VMEM(attn_shape, BF16),
            pltpu.VMEM(ffn_shape, BF16),
            pltpu.VMEM(attn_shape, BF16),
            pltpu.VMEM(ffn_shape, BF16),
            pltpu.VMEM((chips, *attn_shape[1:]), BF16),
            pltpu.VMEM((chips, *ffn_shape[1:]), BF16),
            pltpu.VMEM((chips, *attn_shape[1:]), BF16),
            pltpu.VMEM((chips, *ffn_shape[1:]), BF16),
            pltpu.VMEM(sums, F32),
            pltpu.VMEM(sums, F32),
            pltpu.VMEM((8, LANES), F32),
            pltpu.VMEM((2, 8, *sums), F32),
            pltpu.VMEM((2, chips, *sums), F32),
            pltpu.VMEM((8, 8, LANES), F32),
            pltpu.VMEM((chips, 8, LANES), F32),
        ]
        last = (
            jax.ShapeDtypeStruct(vec.shape, F32),
            jax.ShapeDtypeStruct((8, LANES), F32),
            jax.ShapeDtypeStruct(attn_shape[1:], F32),
            jax.ShapeDtypeStruct(ffn_shape[1:], F32),
        )
    else:
        last = (
            jax.ShapeDtypeStruct(sums, F32),
            jax.ShapeDtypeStruct(sums, F32),
            jax.ShapeDtypeStruct(attn_shape, BF16),
            jax.ShapeDtypeStruct(ffn_shape, BF16),
        )
    return pl.pallas_call(
        functools.partial(layer_kernel, inside, chips),
        out_shape=(jax.ShapeDtypeStruct((rows, width), BF16), jax.ShapeDtypeStruct((rows, width), F32), *last),
        in_specs=[vmem, vmem, vmem, anywhere, vmem, source, source],
        out_specs=(vmem,) * 6,
        scratch_shapes=scratch,
        compiler_params=pltpu.CompilerParams(
            collective_id=0, has_side_effects=True, vmem_limit_bytes=VMEM_LIMIT
        ),
    )(frames, segments, spans, cot, vec, attn_src, ffn_src)


def adam_kernel(norm, *refs):
    clip = jnp.minimum(1.0, MAX_NORM / (norm[0, 0] + 1e-06))
    attn, ffn, vec = refs[0:4], refs[4:8], refs[8:12]
    attn_to, ffn_to, vec_to, norm_to = refs[12:16], refs[16:20], refs[20:23], refs[23]

    def update(source, target, rate, decay):
        master, first, second, grad = (ref[...] for ref in source)
        for ref, value in zip(target, adam_step(master, first, second, grad * clip, rate, decay)):
            ref[...] = value
        if len(target) > 3:
            target[3][...] = target[0][...].astype(BF16)

    update(attn, attn_to, RATE_ATTN, DECAY_RATE)
    update(ffn, ffn_to, RATE_FFN, DECAY_RATE)

    @pl.when(pl.program_id(0) == 0)
    def _():
        update(vec, vec_to, RATE_VEC, 0.0)
        norm_to[0, 0] = norm[0, 0]


def run_adam(norm, attn, ffn, vec):
    steps = 2

    def split(array):
        return pl.BlockSpec((array.shape[0] // steps, array.shape[1]), lambda i: (i, 0))

    whole = pl.BlockSpec(vec[0].shape, lambda i: (0, 0))
    scalar = pl.BlockSpec(memory_space=pltpu.SMEM)

    def shapes(array, copy):
        types = (F32, F32, F32, BF16) if copy else (F32, F32, F32)
        return tuple(jax.ShapeDtypeStruct(array.shape, t) for t in types)

    return pl.pallas_call(
        adam_kernel,
        grid=(steps,),
        out_shape=(
            *shapes(attn[0], True),
            *shapes(ffn[0], True),
            *shapes(vec[0], False),
            jax.ShapeDtypeStruct((1, 1), F32),
        ),
        in_specs=[scalar] + [split(attn[0])] * 4 + [split(ffn[0])] * 4 + [whole] * 4,
        out_specs=(*[split(attn[0])] * 4, *[split(ffn[0])] * 4, *[whole] * 3, scalar),
        compiler_params=pltpu.CompilerParams(vmem_limit_bytes=VMEM_LIMIT),
    )(norm, *attn, *ffn, *vec)


def per_device(
    frames,
    segment_ids,
    span_starts,
    cotangent,
    attn_master,
    attn_first,
    attn_second,
    ffn_master,
    ffn_first,
    ffn_second,
    vec_master,
    vec_first,
    vec_second,
):
    dp_count = lax.axis_size("dp")

    def gather_slabs(master):
        shard = master.astype(BF16)
        whole = lax.all_gather(shard, "dp", axis=1, tiled=True)
        return whole.reshape(shard.shape[0], SLABS, -1).transpose(1, 0, 2)

    inside = attn_master.shape[1] % 256 == 0 and ffn_master.shape[1] % 256 == 0 and dp_count in (4, 8)
    head = (frames[0], segment_ids, span_starts, cotangent[0], vec_master)
    if inside:
        output, frames_grad, vec_grad, norm, attn_owned, ffn_owned = run_layer(
            *head, attn_master, ffn_master, True, dp_count // 2
        )
    else:
        output, frames_grad, early, late, g_attn, g_ffn = run_layer(
            *head, gather_slabs(attn_master), gather_slabs(ffn_master), False, dp_count // 2
        )
        vec_local = jnp.concatenate([late[0:4], early[0:4], late[4:5], early[4:8]], axis=0)

        def scatter_slabs(slabs):
            whole = slabs.astype(F32).transpose(1, 0, 2).reshape(slabs.shape[1], -1)
            return lax.psum_scatter(whole, "dp", scatter_dimension=1, tiled=True)

        attn_owned = scatter_slabs(g_attn)
        ffn_owned = scatter_slabs(g_ffn)
        owned_squares = jnp.sum(attn_owned * attn_owned) + jnp.sum(ffn_owned * ffn_owned)
        vec_grad, total_squares = lax.psum((vec_local, owned_squares), ("seq", "dp"))
        norm = jnp.broadcast_to(jnp.sqrt(total_squares + jnp.sum(vec_grad * vec_grad)), (8, LANES))
    updated = run_adam(
        norm,
        (attn_master, attn_first, attn_second, attn_owned),
        (ffn_master, ffn_first, ffn_second, ffn_owned),
        (vec_master, vec_first, vec_second, vec_grad),
    )
    return (output[None], frames_grad[None], updated[-1].reshape(()), *updated[:-1])


def solution(mesh):
    return jax.shard_map(
        per_device,
        mesh=mesh,
        in_specs=(
            P("dp", "seq", None),
            P("dp", None),
            P("dp", None),
            P("dp", "seq", None),
            P("seq", "dp"),
            P("seq", "dp"),
            P("seq", "dp"),
            P("seq", "dp"),
            P("seq", "dp"),
            P("seq", "dp"),
            P(),
            P(),
            P(),
        ),
        out_specs=(
            P("dp", "seq", None),
            P("dp", "seq", None),
            P(),
            P("seq", "dp"),
            P("seq", "dp"),
            P("seq", "dp"),
            P("seq", "dp"),
            P("seq", "dp"),
            P("seq", "dp"),
            P("seq", "dp"),
            P("seq", "dp"),
            P(),
            P(),
            P(),
        ),
        check_vma=False,
    )
```

```python
import functools

import jax
import jax.numpy as jnp
from jax import lax
from jax.experimental import pallas as pl
from jax.experimental.pallas import tpu as pltpu
from jax.sharding import PartitionSpec as P

H = 16
SPAN = 10
STEP = 10

EPS_NORM = 1e-05
BETA_ONE = 0.9
BETA_TWO = 0.999
EPS_ADAM = 1e-08
RATE_ATTN = 0.12
RATE_FFN = 0.03
RATE_VEC = 0.5
DECAY_RATE = 0.01
MAX_NORM = 1.0
NEG_FILL = -1e30

SLABS = 8
LANES = 128
VMEM_LIMIT = 62 * 1024 * 1024
F32 = jnp.float32
BF16 = jnp.bfloat16
MESH = pl.DeviceIdType.MESH


def adam_step(master, first, second, grad, rate, decay):
    first_new = BETA_ONE * first + (1.0 - BETA_ONE) * grad
    second_new = BETA_TWO * second + (1.0 - BETA_TWO) * grad * grad
    first_hat = first_new * (1.0 / (1.0 - BETA_ONE**STEP))
    second_hat = second_new * (1.0 / (1.0 - BETA_TWO**STEP))
    master_new = master - rate * (first_hat / (jnp.sqrt(second_hat) + EPS_ADAM) + decay * master)
    return (master_new, first_new, second_new)


def nn(left, right):
    return lax.dot_general(left, right, (((1,), (0,)), ((), ())), preferred_element_type=F32)


def nt(left, right):
    return lax.dot_general(left, right, (((1,), (1,)), ((), ())), preferred_element_type=F32)


def tn(left, right):
    return lax.dot_general(left, right, (((0,), (0,)), ((), ())), preferred_element_type=F32)


def normalise(source):
    mean_val = jnp.mean(source, axis=-1, keepdims=True)
    centred = source - mean_val
    inv_std = lax.rsqrt(jnp.mean(centred * centred, axis=-1, keepdims=True) + EPS_NORM)
    return centred * inv_std, inv_std


def norm_back(grad_out, normed, inv_std, gain_row):
    scaled = grad_out * gain_row
    inner = (
        scaled
        - jnp.mean(scaled, axis=-1, keepdims=True)
        - normed * jnp.mean(scaled * normed, axis=-1, keepdims=True)
    )
    return inner * inv_std


def col_sum(value):
    return jnp.sum(value, axis=0, keepdims=True)


class Gather:
    def __init__(self, cp, buf, base, place, off, rows):
        self.cp, self.buf, self.b = cp, buf, base
        self.s, self.px, self.py, self.pd = place
        self.off, self.h = off, rows // 2

    def top(self, slot):
        return self.buf.at[slot, pl.ds(self.off, self.h)]

    def bot(self, slot):
        return self.buf.at[slot, pl.ds(self.off + self.h, self.h)]

    def c(self, part, slot, i, to):
        ref = part(slot)
        return self.cp(ref, ref, self.b + i, to)

    def start(self):
        self.c(self.top, self.s, 0, self.px).start()
        self.c(self.bot, self.s, 2, self.py).start()
        self.c(self.bot, self.s, 1, self.px).start()
        self.c(self.top, self.s, 3, self.py).start()

    def relay(self):
        self.c(self.top, self.px, 0, self.px).wait_recv()
        self.c(self.top, self.px, 4, self.py).start()
        self.c(self.bot, self.py, 2, self.py).wait_recv()
        self.c(self.bot, self.py, 5, self.px).start()

    def wait_x(self):
        self.c(self.bot, self.px, 1, self.px).wait_recv()

    def wait_y(self):
        self.c(self.top, self.py, 3, self.py).wait_recv()

    def wait_d(self):
        self.c(self.top, self.pd, 4, self.py).wait_recv()
        self.c(self.bot, self.pd, 5, self.px).wait_recv()

    def sent(self):
        for part, slot, i, to in (
            (self.top, self.s, 0, self.px),
            (self.bot, self.s, 2, self.py),
            (self.bot, self.s, 1, self.px),
            (self.top, self.s, 3, self.py),
            (self.top, self.px, 4, self.py),
            (self.bot, self.py, 5, self.px),
        ):
            self.c(part, slot, i, to).wait_send()


class Scatter:
    def __init__(self, cp, part, in_x, in_y, via_x, via_y, base, place):
        _, px, py, _ = place
        h = in_x.shape[1] // 2
        top, bot = pl.ds(0, h), pl.ds(h, h)
        self.to_x, self.to_y, self.via_x, self.via_y = part(1), part(2), via_x, via_y
        self.top, self.bot = top, bot
        far = part(3)
        self.copies = [
            cp(far.at[:, top], via_x, base, px),
            cp(far.at[:, bot], via_y, base + 1, py),
            cp(self.to_x.at[:, top], in_x.at[:, top], base + 2, px),
            cp(self.to_y.at[:, bot], in_y.at[:, bot], base + 3, py),
            cp(self.to_y.at[:, top], in_y.at[:, top], base + 4, py),
            cp(self.to_x.at[:, bot], in_x.at[:, bot], base + 5, px),
        ]

    def start(self, relation):
        for i in {3: (0, 1), 1: (2,), 2: (3,)}[relation]:
            self.copies[i].start()

    def relay(self):
        for i, ref, via, at in ((0, self.to_y, self.via_x, self.top), (1, self.to_x, self.via_y, self.bot)):
            self.copies[i].wait_recv()
            ref[:, at, :] = (ref[:, at, :].astype(F32) + via[...].astype(F32)).astype(BF16)
            self.copies[4 + i].start()

    def wait(self):
        for i in (2, 3, 4, 5):
            self.copies[i].wait_recv()

    def sent(self):
        for copy in self.copies:
            copy.wait_send()


class Line:
    def __init__(self, cp_dp, buf, base, chip, core, chips):
        self.cp, self.buf, self.b = cp_dp, buf, base
        self.z, self.core, self.n = chip, core, chips

    def c(self, shard, kind, hop):
        ref = self.buf.at[2 * shard + self.core]
        return self.cp(ref, ref, self.b + kind, 2 * (self.z + hop) + self.core)

    def has(self, hop):
        return jnp.logical_and(self.z + hop >= 0, self.z + hop < self.n)

    def across(self, shard):
        ref = self.buf.at[2 * shard + self.core]
        return self.cp(ref, ref, self.b + 6 + shard, 2 * self.z + 1 - self.core)

    def start_first(self):
        for step in (1, -1):
            kind = (1 - step) // 2
            far = self.has(3 * step)

            @pl.when(far)
            def _(kind=kind, step=step):
                self.c(self.z, 2 + kind, 2 * step).start()

            @pl.when(jnp.logical_and(jnp.logical_not(self.has(2 * step)), self.has(step)))
            def _(kind=kind, step=step):
                self.c(self.z, kind, step).start()

        self.across(self.z).start()

    def start_rest(self):
        for step in (1, -1):
            kind = (1 - step) // 2
            far = self.has(3 * step)

            @pl.when(far)
            def _(kind=kind, step=step):
                self.c(self.z, kind, step).start()

            @pl.when(jnp.logical_and(jnp.logical_not(far), self.has(2 * step)))
            def _(kind=kind, step=step):
                self.c(self.z, 2 + kind, 2 * step).start()
                self.c(self.z, kind, step).start()

    def relay(self):
        for kind, hop, on in ((2, -2, 1), (3, 2, -1)):

            @pl.when(jnp.logical_and(self.has(hop), self.has(on)))
            def _(kind=kind, hop=hop, on=on):
                self.c(self.z + hop, kind, hop).wait_recv()
                self.c(self.z + hop, kind + 2, on).start()
                self.across(self.z + hop).start()

    def settle(self):
        for kind, hop, on in ((0, -1, 0), (1, 1, 0), (2, -2, 1), (3, 2, -1), (4, -3, 0), (5, 3, 0)):
            due = self.has(hop)
            if on:
                due = jnp.logical_and(due, jnp.logical_not(self.has(on)))

            @pl.when(due)
            def _(kind=kind, hop=hop):
                self.c(self.z + hop, kind, hop).wait_recv()
                self.across(self.z + hop).start()

        other = 1 - self.core
        for shard in range(self.n):
            ref = self.buf.at[2 * shard + other]
            self.cp(ref, ref, self.b + 6 + shard, 2 * self.z + other).wait_recv()

    def sent(self):
        for shard in range(self.n):
            self.across(shard).wait_send()
        for kind, hop in ((0, 1), (1, -1), (2, 2), (3, -2)):

            @pl.when(self.has(hop))
            def _(kind=kind, hop=hop):
                self.c(self.z, kind, hop).wait_send()

        for kind, hop, on in ((4, -2, 1), (5, 2, -1)):

            @pl.when(jnp.logical_and(self.has(hop), self.has(on)))
            def _(kind=kind, hop=hop, on=on):
                self.c(self.z + hop, kind, on).wait_send()


class LineSum:
    def __init__(self, cp_dp, part, cross, landed, base, chip, core, chips):
        self.cp, self.part, self.cross, self.landed, self.b = cp_dp, part, cross, landed, base
        self.z, self.core, self.n = chip, core, chips

    def mine(self, shard):
        return 2 * shard + self.core

    def has(self, hop):
        return jnp.logical_and(self.z + hop >= 0, self.z + hop < self.n)

    def across(self, shard, half):
        rows = self.part.shape[1] // 2
        at = pl.ds(half * rows, rows)
        src = self.part.at[2 * shard + 1 - self.core, at]
        return self.cp(src, self.cross.at[shard, at], self.b + 6 + 2 * shard + half, 2 * self.z + 1 - self.core)

    def direct(self, kind, hop):
        src = self.part.at[self.mine(self.z + hop)]
        return self.cp(src, self.landed.at[self.z], self.b + kind, 2 * (self.z + hop) + self.core)

    def via(self, kind, hop, step):
        src = self.part.at[self.mine(self.z + hop)]
        return self.cp(src, self.landed.at[self.z + step], self.b + kind, 2 * (self.z + step) + self.core)

    def start(self, half):
        for shard in range(self.n):
            self.across(shard, half).start()

    def add(self, shard, ref, first, rows):
        size = min(256, rows)

        def one(i, carry):
            at = pl.ds(pl.multiple_of(first + i * size, size), size)
            total = self.part[self.mine(shard), at, :].astype(F32) + ref[at, :].astype(F32)
            self.part[self.mine(shard), at, :] = total.astype(BF16)
            return carry

        lax.fori_loop(0, rows // size, one, 0)

    def fold(self, half):
        rows = self.part.shape[1] // 2
        for shard in range(self.n):
            self.across(shard, half).wait_recv()
            self.add(shard, self.cross.at[shard], half * rows, rows)

    def launch(self):
        for step in (1, -1):
            kind = (1 - step) // 2
            far = self.has(3 * step)

            @pl.when(far)
            def _(kind=kind, step=step):
                self.via(4 + kind, 3 * step, step).start()

            @pl.when(jnp.logical_and(jnp.logical_not(far), self.has(step)))
            def _(kind=kind, step=step):
                self.direct(kind, step).start()

    def follow(self):
        for step in (1, -1):
            kind = (1 - step) // 2

            @pl.when(self.has(3 * step))
            def _(kind=kind, step=step):
                self.direct(2 + kind, 2 * step).start()
                self.direct(kind, step).start()

            @pl.when(jnp.logical_and(jnp.logical_not(self.has(3 * step)), self.has(2 * step)))
            def _(kind=kind, step=step):
                @pl.when(self.has(-step))
                def _():
                    here = self.landed.at[self.z]
                    self.cp(here, here, self.b + 4 + kind, 2 * (self.z + step) + self.core).wait_recv()
                    self.add(self.z + 2 * step, here, 0, self.part.shape[1])

                self.direct(2 + kind, 2 * step).start()

    def finish(self, owned):
        owned[...] = self.part[self.mine(self.z)].astype(F32)
        for kind, hop in ((0, -1), (1, 1), (2, -2), (3, 2)):

            @pl.when(self.has(hop))
            def _(kind=kind, hop=hop):
                there = self.landed.at[self.z + hop]
                self.cp(there, there, self.b + kind, 2 * (self.z + hop) + self.core).wait_recv()
                owned[...] += there[...].astype(F32)

    def sent(self):
        for shard in range(self.n):
            for half in range(2):
                self.across(shard, half).wait_send()
        for step in (1, -1):
            kind = (1 - step) // 2
            for hops in (1, 2):

                @pl.when(self.has(hops * step))
                def _(kind=kind, step=step, hops=hops):
                    self.direct(kind + 2 * (hops - 1), hops * step).wait_send()

            @pl.when(self.has(3 * step))
            def _(kind=kind, step=step):
                self.via(4 + kind, 3 * step, step).wait_send()


class Everyone:
    def __init__(self, cp_any, plane, line, base, s, chip, core, chips):
        self.cp, self.plane, self.line, self.b = cp_any, plane, line, base
        self.s, self.z, self.core, self.n = s, chip, core, chips
        self.me = 2 * s + core

    def to_plane(self, o):
        p = lax.rem(self.me + o, 8)
        return self.cp(self.plane.at[self.me], self.plane.at[self.me], self.b + o, p // 2, 2 * self.z + lax.rem(p, 2))

    def from_plane(self, o):
        p = lax.rem(self.me - o + 8, 8)
        return self.cp(self.plane.at[p], self.plane.at[p], self.b + o, p // 2, 2 * self.z + lax.rem(p, 2))

    def to_line(self, o):
        p = lax.rem(self.z + o, self.n)
        return self.cp(self.line.at[self.z], self.line.at[self.z], self.b + 7 + o, self.s, 2 * p + self.core)

    def from_line(self, o):
        p = lax.rem(self.z - o + self.n, self.n)
        return self.cp(self.line.at[p], self.line.at[p], self.b + 7 + o, self.s, 2 * p + self.core)

    def start(self, value):
        self.plane[self.me] = value
        for o in range(1, 8):
            self.to_plane(o).start()

    def middle(self):
        for o in range(1, 8):
            self.from_plane(o).wait_recv()
        total = self.plane[0]
        for p in range(1, 8):
            total = total + self.plane[p]
        self.line[self.z] = total
        for o in range(1, self.n):
            self.to_line(o).start()

    def end(self):
        for o in range(1, self.n):
            self.from_line(o).wait_recv()
        total = self.line[0]
        for p in range(1, self.n):
            total = total + self.line[p]
        return total

    def sent(self):
        for o in range(1, 8):
            self.to_plane(o).wait_send()
        for o in range(1, self.n):
            self.to_line(o).wait_send()


def layer_kernel(inside, chips, *refs):
    refs = list(refs)

    def take(count):
        head = refs[:count]
        del refs[:count]
        return head

    frames, segments, spans, cot, vec, attn_src, ffn_src = take(7)
    if inside:
        out, frames_grad, vec_out, norm_out, attn_owned, ffn_owned = take(6)
    else:
        out, frames_grad, early, late, g_attn, g_ffn = take(6)
        w_attn, w_ffn = attn_src, ffn_src
    fr_g, cot_g, a_g, wp, qa, ka, va, kt, att, b_g, gp_g = take(11)
    act_g = fr_g
    resid, own, part, in_x, in_y, via_x, via_y, in_x2, in_y2, via_x2, via_y2 = take(11)
    gsend, gm, dom, ga_g, gres, dqkv, dk_acc, dv_acc, mask_col, seg_q, seg_k = take(11)
    send_sem, recv_sem, local_sem = take(3)
    if inside:
        w_attn, w_ffn, g_attn, g_ffn, cross_a, cross_f, landed_a, landed_f = take(8)
        early, late, squares, planes, lines, planes_s, lines_s = take(7)
    s = lax.axis_index("seq")
    d = lax.axis_index("dp")
    core = lax.rem(d, 2)
    sib = d + 1 - 2 * core

    def peer(r):
        half = r // 2
        high = lax.rem(s // 2 + half, 2)
        low = lax.rem(lax.rem(s, 2) + (r - 2 * half), 2)
        return 2 * high + low

    px, py, pd = peer(1), peer(2), peer(3)
    place = (s, px, py, pd)

    def cp(src, dst, i, to):
        return pltpu.make_async_remote_copy(
            src_ref=src,
            dst_ref=dst,
            send_sem=send_sem.at[i],
            recv_sem=recv_sem.at[i],
            device_id=(to, d),
            device_id_type=MESH,
        )

    def cp_any(src, dst, i, to_seq, to_dp):
        return pltpu.make_async_remote_copy(
            src_ref=src,
            dst_ref=dst,
            send_sem=send_sem.at[i],
            recv_sem=recv_sem.at[i],
            device_id=(to_seq, to_dp),
            device_id_type=MESH,
        )

    def cp_dp(src, dst, i, to):
        return cp_any(src, dst, i, s, to)

    def cp_sib(src, dst, i):
        return cp_any(src, dst, i, s, sib)


    rows = frames.shape[0]
    width = frames.shape[1]
    local = width // 4
    slab_a = w_attn.shape[2]
    slab_f = w_ffn.shape[2]
    per_a = width // slab_a
    per_f = width // slab_f
    tile = 256
    chunk = 128
    small = 64

    cot_load = pltpu.make_async_copy(cot, cot_g.at[s], local_sem.at[0])
    cot_load.start()
    chip = d // 2
    loads = []
    if inside:
        loads = [pltpu.make_async_copy(attn_src, own.at[:, :slab_a], local_sem.at[1])]
        for i, spot in enumerate((dk_acc, dv_acc)):
            at = slice(i * LANES, (i + 1) * LANES)
            loads.append(pltpu.make_async_copy(ffn_src.at[:, at], spot, local_sem.at[2 + i]))
        for load in loads:
            load.start()

    barrier = pltpu.get_barrier_semaphore()
    if inside:
        for o in range(1, 8):
            p = lax.rem(2 * s + core + o, 8)
            to = (p // 2, 2 * chip + lax.rem(p, 2))
            pl.semaphore_signal(barrier, inc=1, device_id=to, device_id_type=MESH)
        for o in range(1, chips):
            to = (s, 2 * lax.rem(chip + o, chips) + core)
            pl.semaphore_signal(barrier, inc=1, device_id=to, device_id_type=MESH)
        pl.semaphore_wait(barrier, 6 + chips)
    else:
        for to in (px, py, pd):
            pl.semaphore_signal(barrier, inc=1, device_id=(to, d), device_id_type=MESH)
        pl.semaphore_signal(barrier, inc=1, device_id=(s, sib), device_id_type=MESH)
        pl.semaphore_wait(barrier, 4)

    fr_g[s] = frames[...]
    frames_in = Gather(cp, fr_g, 0, place, 0, rows)
    frames_in.start()
    cot_in = Gather(cp, cot_g, 15, place, 0, rows)
    if inside:
        line_a = Line(cp_dp, w_attn, 60, chip, core, chips)
        line_f = Line(cp_dp, w_ffn, 66 + chips, chip, core, chips)
        loads[0].wait()
        w_attn[d] = own[:, :slab_a].astype(BF16)
        line_a.start_first()
    half = rows // 2
    wp_off = pl.multiple_of(core * half, half)
    wp_in = Gather(cp, wp, 6, place, wp_off, half)
    wp_cross = [
        cp_sib(wp.at[p, pl.ds(wp_off, half)], wp.at[p, pl.ds(wp_off, half)], 12 + i) for i, p in enumerate((px, py, pd))
    ]
    early[...] = jnp.zeros_like(early)
    late[...] = jnp.zeros_like(late)

    group = 4 * rows
    position = lax.broadcasted_iota(jnp.int32, (group, spans.shape[1]), 0)
    starts = spans[...]
    covered = jnp.logical_and(position >= starts, position < starts + SPAN)
    mask_col[...] = jnp.max(jnp.where(covered, 1.0, 0.0), axis=1, keepdims=True)
    second = jnp.transpose(jnp.broadcast_to(segments[...].astype(F32), (LANES, group)))
    seg_lane = lax.broadcasted_iota(jnp.int32, (group, LANES), 1)
    fill = jnp.where(seg_lane == 0, second, jnp.where(seg_lane == 1, 1.0 - second, 0.0)) * NEG_FILL
    seg_q[...] = fill.astype(BF16)
    ones = jnp.where(seg_lane < 5, 1.0, 0.0)
    seg_k[...] = jnp.where(seg_lane == 0, 1.0 - second, jnp.where(seg_lane == 1, second, ones)).astype(BF16)
    half = rows // 2

    lane = lax.broadcasted_iota(jnp.int32, (rows, LANES), 1)
    low_head = lane < LANES // 2
    q_bias = vec[2:3, pl.ds(pl.multiple_of(s * local, local), local)]
    v_bias = vec[3:4, pl.ds(pl.multiple_of(s * local, local), local)]

    def weight_rows(first, count, start, size):
        return jnp.concatenate([w_attn[first + i, start : start + size, :] for i in range(count)], axis=1)

    def enter(blk):
        def norm_rows(i, carry):
            at = pl.ds(pl.multiple_of(i * chunk, chunk), chunk)
            at_all = pl.ds(pl.multiple_of(blk * rows + i * chunk, chunk), chunk)
            x = jnp.where(mask_col[at_all, :] > 0.0, vec[8:9, :], fr_g[blk, at, :].astype(F32))
            normed, _ = normalise(x)
            a_g[blk, at, :] = (normed * vec[0:1, :] + vec[1:2, :]).astype(BF16)
            return carry

        lax.fori_loop(0, rows // chunk, norm_rows, 0)

    def project_in(blk):
        a = a_g[blk]
        at_all = pl.ds(pl.multiple_of(blk * rows, rows), rows)
        q = (nt(a, weight_rows(0, per_a, 0, local)) + q_bias).astype(BF16).astype(F32) * 0.125
        for pair in range(2):
            both = q[:, pair * LANES : (pair + 1) * LANES]
            for h in range(2):
                keep = low_head if h == 0 else jnp.logical_not(low_head)
                qa[2 * pair + h, blk, :, :LANES] = jnp.where(keep, both, 0.0).astype(BF16)
                qa[2 * pair + h, blk, :, LANES:] = seg_q[at_all, :]
        k = nt(a, weight_rows(per_a, per_a, 0, local)).astype(BF16)
        for pair in range(2):
            both = k[:, pair * LANES : (pair + 1) * LANES]
            ka[pair, at_all, :LANES] = both
            ka[pair, at_all, LANES:] = seg_k[at_all, :]
            kt[pair, :, at_all] = jnp.transpose(both)
        v = (nt(a, weight_rows(2 * per_a, per_a, 0, local)) + v_bias).astype(BF16)
        for pair in range(2):
            va[pair, at_all, :] = v[:, pair * LANES : (pair + 1) * LANES]

    enter(s)
    if inside:
        for i, spot in enumerate((dk_acc, dv_acc)):
            loads[1 + i].wait()
            w_ffn[d, :, i * LANES : (i + 1) * LANES] = spot[...].astype(BF16)
    if inside:
        line_a.start_rest()
        line_a.relay()
    frames_in.relay()
    frames_in.wait_x()
    enter(px)
    frames_in.wait_y()
    enter(py)
    frames_in.wait_d()
    enter(pd)
    if inside:
        line_a.settle()
        line_f.start_first()
    for i in range(per_a):
        wp[s, :, i * slab_a : (i + 1) * slab_a] = w_attn[3 * per_a + i]
    wp_in.start()
    lax.fori_loop(0, 4, lambda j, carry: (project_in(j), carry)[1], 0)
    cot_load.wait()

    def att_x(j, slot):
        return cp(att.at[slot, j], att.at[slot, j], 21 + j, px)

    def att_y(j, slot):
        return cp(att.at[slot, j], att.at[slot, j], 25 + j, py)

    def att_relay(j, start):
        even = lax.rem(j, 2) == 0

        @pl.when(even)
        def _():
            if start:
                att_x(j, px).wait_recv()
                cp(att.at[px, j], att.at[px, j], 29 + j, py).start()
            else:
                cp(att.at[px, j], att.at[px, j], 29 + j, py).wait_send()

        @pl.when(jnp.logical_not(even))
        def _():
            if start:
                att_y(j, py).wait_recv()
                cp(att.at[py, j], att.at[py, j], 29 + j, px).start()
            else:
                cp(att.at[py, j], att.at[py, j], 29 + j, px).wait_send()

    def attend(j, carry):
        @pl.when(j == 2)
        def _():
            wp_in.relay()
            if inside:
                line_f.start_rest()
                line_f.relay()

        for pair in range(2):
            outs = []
            for h in range(2):
                head = 2 * pair + h
                scores = nt(qa[head, j], ka[pair])
                peak = jnp.max(scores, axis=-1, keepdims=True)
                terms = jnp.exp(scores - peak)
                total = jnp.sum(terms, axis=-1, keepdims=True)
                probs = (terms * (1.0 / total)).astype(BF16)
                outs.append(nn(probs, va[pair]))
                log_total = -(peak + jnp.log(total))
                part_one = log_total.astype(BF16).astype(F32)
                rest = log_total - part_one
                part_two = rest.astype(BF16).astype(F32)
                part_three = rest - part_two
                aug = qa[head, j, :, LANES:].astype(F32)
                aug = jnp.where(lane == 2, part_one, aug)
                aug = jnp.where(lane == 3, part_two, aug)
                aug = jnp.where(lane == 4, part_three, aug)
                qa[head, j, :, LANES:] = aug.astype(BF16)
            att[s, j, :, pair * LANES : (pair + 1) * LANES] = jnp.where(low_head, outs[0], outs[1]).astype(BF16)
        att_x(j, s).start()
        att_y(j, s).start()

        @pl.when(j > 0)
        def _():
            att_relay(j - 1, True)

        return carry

    lax.fori_loop(0, 4, attend, 0)
    wp_in.wait_x()
    wp_cross[0].start()
    wp_in.wait_y()
    wp_cross[1].start()
    wp_in.wait_d()
    wp_cross[2].start()
    att_relay(3, True)
    other_off = pl.multiple_of((1 - core) * half, half)
    for i, p in enumerate((px, py, pd)):
        cp_sib(wp.at[p, pl.ds(other_off, half)], wp.at[p, pl.ds(other_off, half)], 12 + i).wait_recv()

    def project(j, carry):
        @pl.when(j == 1)
        def _():
            cot_in.start()

        even = lax.rem(j, 2) == 0

        @pl.when(even)
        def _():
            att_y(j, py).wait_recv()
            cp(att.at[pd, j], att.at[pd, j], 29 + j, py).wait_recv()

        @pl.when(jnp.logical_not(even))
        def _():
            att_x(j, px).wait_recv()
            cp(att.at[pd, j], att.at[pd, j], 29 + j, px).wait_recv()

        left = jnp.concatenate([att[p, j] for p in range(4)], axis=1)
        for i in range(width // tile):
            right = jnp.concatenate([wp[p, :, i * tile : (i + 1) * tile] for p in range(4)], axis=0)
            own[:, i * tile : (i + 1) * tile] = nn(left, right)

        def norm_rows(i, inner):
            at = pl.ds(pl.multiple_of(i * chunk, chunk), chunk)
            at_all = pl.ds(pl.multiple_of(j * rows + i * chunk, chunk), chunk)
            x = jnp.where(mask_col[at_all, :] > 0.0, vec[8:9, :], fr_g[j, at, :].astype(F32))
            total = x + own[at, :] + vec[4:5, :]

            @pl.when(j == s)
            def _():
                resid[at, :] = total

            normed, _ = normalise(total)
            b_g[j, at, :] = (normed * vec[5:6, :] + vec[6:7, :]).astype(BF16)
            return inner

        lax.fori_loop(0, rows // chunk, norm_rows, 0)
        return carry

    lax.fori_loop(0, 4, project, 0)
    cot_in.relay()
    if inside:
        line_f.settle()
    frames_in.sent()

    def feed(r):
        blk = peer(r)

        def hidden_tile(i, carry):
            at = pl.ds(pl.multiple_of(i * tile, tile), tile)
            w_in = jnp.concatenate([w_ffn[k, at, :] for k in range(per_f)], axis=1)
            w_out = jnp.concatenate([w_ffn[per_f + k, at, :] for k in range(per_f)], axis=1)
            pre = nt(b_g[blk], w_in) + vec[pl.ds(9 + s, 1), at]
            grad_act = nt(cot_g[blk], w_out)
            cdf = 0.5 * (1.0 + lax.erf(pre * 0.7071067811865476))
            act_g[blk, :, at] = (pre * cdf).astype(BF16)
            density = jnp.exp(-0.5 * pre * pre) * 0.3989422804014327
            grad_pre = ((cdf + pre * density) * grad_act).astype(BF16)
            gp_g[blk, :, at] = grad_pre
            early[pl.ds(4 + s, 1), at] += col_sum(grad_pre.astype(F32))
            return carry

        lax.fori_loop(0, w_ffn.shape[1] // tile, hidden_tile, 0)
        left = gp_g[blk]
        for k in range(per_f):
            at = slice(k * slab_f, (k + 1) * slab_f)
            value = nn(left, w_ffn[k])
            if r == 0:
                own[:, at] = value
            else:
                part[r - 1, k] = value.astype(BF16)

    sum_b = Scatter(cp, lambda r: part.at[r - 1], in_x, in_y, via_x, via_y, 33, place)
    cot_in.wait_d()
    feed(3)
    sum_b.start(3)
    cot_in.wait_x()
    feed(1)
    sum_b.start(1)
    cot_in.wait_y()
    feed(2)
    sum_b.start(2)
    sum_b.relay()
    feed(0)

    def ffn_grads(i, carry):
        at = pl.ds(pl.multiple_of(i * tile, tile), tile)
        for left, right, first in ((gp_g, b_g, 0), (act_g, cot_g, per_f)):
            turned = jnp.transpose(jnp.concatenate([left[p, :, at] for p in range(4)], axis=0))
            for k in range(per_f):
                cols = jnp.concatenate([right[p, :, k * slab_f : (k + 1) * slab_f] for p in range(4)], axis=0)
                g_ffn[first + k, at, :] = nn(turned, cols).astype(BF16)
        return carry

    f_tiles = w_ffn.shape[1] // tile
    if inside:
        sum_f = LineSum(cp_dp, g_ffn, cross_f, landed_f, 72 + 2 * chips, chip, core, chips)
        sum_g = LineSum(cp_dp, g_attn, cross_a, landed_a, 78 + 4 * chips, chip, core, chips)
        all_early = Everyone(cp_any, planes.at[0], lines.at[0], 84 + 6 * chips, s, chip, core, chips)
        all_late = Everyone(cp_any, planes.at[1], lines.at[1], 91 + 7 * chips, s, chip, core, chips)
        all_squares = Everyone(cp_any, planes_s, lines_s, 98 + 8 * chips, s, chip, core, chips)
    def ffn_grads_sent(i, carry):
        if inside:

            @pl.when(i == f_tiles // 2)
            def _():
                sum_f.start(0)

        return ffn_grads(i, carry)

    lax.fori_loop(0, f_tiles, ffn_grads_sent, 0)
    if inside:
        sum_f.start(1)
    if inside:
        sum_f.fold(0)
        sum_f.fold(1)
        sum_f.launch()

    def out_part(blk, k):
        return nn(act_g[blk], w_ffn[per_f + k])

    for j in range(4):
        att_x(j, s).wait_send()
        att_y(j, s).wait_send()
        att_relay(j, False)
    sum_o = Scatter(cp, lambda r: att.at[peer(r)], in_x2, in_y2, via_x2, via_y2, 48, place)
    for r in (3, 1, 2):
        for k in range(per_f):
            att[peer(r), k] = out_part(peer(r), k).astype(BF16)
    sum_b.wait()
    sum_o.start(3)

    def landed(from_x, from_y, at):
        tiles = range(from_x.shape[0])
        return jnp.concatenate([from_x[t, at, :].astype(F32) + from_y[t, at, :].astype(F32) for t in tiles], axis=1)

    def back_two(i, carry):
        at = pl.ds(pl.multiple_of(i * small, small), small)
        grad_b = own[at, :] + landed(in_x, in_y, at)
        normed, inv_std = normalise(resid[at, :])
        grad_y = cot_g[s, at, :].astype(F32)
        grad_resid = grad_y + norm_back(grad_b, normed, inv_std, vec[5:6, :])
        gres[at, :] = grad_resid
        low = grad_resid.astype(BF16)
        ga_g[s, at, :] = low
        early[0:1, :] += col_sum(low.astype(F32))
        early[1:2, :] += col_sum(grad_b * normed)
        early[2:3, :] += col_sum(grad_b)
        early[3:4, :] += col_sum(grad_y)
        return carry

    lax.fori_loop(0, rows // small, back_two, 0)

    for i, r in enumerate((3, 1, 2)):
        gsend[r] = nt(ga_g[s], wp[peer(r)]).astype(BF16)
        cp(gsend.at[r], gm.at[s], 39 + i, peer(r)).start()
    gm[s] = nt(ga_g[s], wp[s]).astype(BF16)
    ga_in = Gather(cp, ga_g, 42, place, 0, rows)
    ga_in.start()
    sum_b.sent()

    def spread(j):
        for pair in range(2):
            both = gm[j, :, pair * LANES : (pair + 1) * LANES].astype(F32)
            dom[2 * pair, j] = jnp.where(low_head, both, 0.0).astype(BF16)
            dom[2 * pair + 1, j] = jnp.where(low_head, 0.0, both).astype(BF16)

    def arrive(i, r):
        cp(gsend.at[r], gm.at[peer(r)], 39 + i, peer(r)).wait_recv()
        spread(peer(r))

    spread(s)

    def back_pair(pair, first, second):
        dk_acc[...] = jnp.zeros_like(dk_acc)
        dv_acc[...] = jnp.zeros_like(dv_acc)

        def back_block(r, carry):
            j = peer(r)
            for at_block, task in ((1, first), (3, second)):
                if task is not None:
                    pl.when(r == at_block)(task)
            sides = []
            for h in range(2):
                head = 2 * pair + h
                probs = jnp.exp(nt(ka[pair], qa[head, j]))
                grad_probs = nt(va[pair], dom[head, j])
                delta = jnp.sum(probs * grad_probs, axis=0, keepdims=True)
                grad_scores = (probs * (grad_probs - delta)).astype(BF16)
                dv_acc[...] += nn(probs.astype(BF16), dom[head, j])
                dk_acc[...] += nn(grad_scores, qa[head, j, :, :LANES])
                sides.append(nn(kt[pair], grad_scores))
            half_lane = LANES // 2
            turned = jnp.concatenate([sides[0][:half_lane], sides[1][half_lane:]], axis=0)
            dqkv[0, j, :, pair * LANES : (pair + 1) * LANES] = (jnp.transpose(turned) * 0.125).astype(BF16)
            return carry

        lax.fori_loop(0, 4, back_block, 0)
        for j in range(4):
            at = slice(j * rows, (j + 1) * rows)
            dqkv[1, j, :, pair * LANES : (pair + 1) * LANES] = dk_acc[at, :].astype(BF16)
            dqkv[2, j, :, pair * LANES : (pair + 1) * LANES] = dv_acc[at, :].astype(BF16)

    def after_own():
        arrive(1, 1)
        arrive(2, 2)

    def after_near():
        arrive(0, 3)
        if inside:
            sum_f.follow()
            all_early.start(early[...])

    back_pair(0, after_own, after_near)
    back_pair(1, None, ga_in.relay)

    sum_a = Scatter(cp, lambda r: part.at[r - 1], in_x, in_y, via_x, via_y, 54, place)

    def grad_in(r):
        blk = peer(r)
        left = jnp.concatenate([dqkv[c, blk] for c in range(3)], axis=1)
        for k in range(per_a):
            at = slice(k * slab_a, (k + 1) * slab_a)
            right = jnp.concatenate([w_attn[c * per_a + k] for c in range(3)], axis=0)
            value = nn(left, right)
            if r == 0:
                own[:, at] = value
            else:
                per_tile = slab_a // tile
                for t in range(per_tile):
                    part[r - 1, k * per_tile + t] = value[:, t * tile : (t + 1) * tile].astype(BF16)

    for r in (3, 1, 2):
        grad_in(r)
        sum_a.start(r)
    grad_in(0)

    my_cols = pl.ds(pl.multiple_of(s * local, local), local)
    for j in range(4):
        late[2:3, my_cols] += col_sum(dqkv[0, j].astype(F32))
        late[3:4, my_cols] += col_sum(dqkv[2, j].astype(F32))

    def attn_grads(c):
        turned = jnp.transpose(jnp.concatenate([dqkv[c, p] for p in range(4)], axis=0))
        for k in range(per_a):
            cols = jnp.concatenate([a_g[p, :, k * slab_a : (k + 1) * slab_a] for p in range(4)], axis=0)
            g_attn[c * per_a + k] = nn(turned, cols).astype(BF16)

    attn_grads(0)
    attn_grads(1)
    attn_grads(2)
    ga_in.wait_x()
    ga_in.wait_y()
    ga_in.wait_d()
    turned = jnp.transpose(jnp.concatenate([att[s, p] for p in range(4)], axis=0))
    for k in range(per_a):
        cols = jnp.concatenate([ga_g[p, :, k * slab_a : (k + 1) * slab_a] for p in range(4)], axis=0)
        g_attn[3 * per_a + k] = nn(turned, cols).astype(BF16)

    if inside:
        sum_g.start(0)
        sum_g.start(1)
    sum_a.relay()
    if inside:
        sum_g.fold(0)
        sum_g.fold(1)
        sum_g.launch()
    if inside:
        sum_f.finish(ffn_owned)
        ffn_squares = col_sum(ffn_owned[...] * ffn_owned[...])
        squares[...] = jnp.zeros_like(squares)
        sum_g.follow()
    sum_a.wait()
    sum_o.start(1)
    sum_o.start(2)
    sum_o.relay()

    def back_one(i, carry):
        at = pl.ds(pl.multiple_of(i * small, small), small)
        at_all = pl.ds(pl.multiple_of(s * rows + i * small, small), small)
        grad_a = own[at, :] + landed(in_x, in_y, at)
        masked = mask_col[at_all, :] > 0.0
        normed, inv_std = normalise(jnp.where(masked, vec[8:9, :], frames[at, :].astype(F32)))
        grad_x = gres[at, :] + norm_back(grad_a, normed, inv_std, vec[0:1, :])
        frames_grad[at, :] = jnp.where(masked, 0.0, grad_x)
        late[0:1, :] += col_sum(grad_a * normed)
        late[1:2, :] += col_sum(grad_a)
        late[4:5, :] += col_sum(jnp.where(masked, grad_x, 0.0))
        return carry

    lax.fori_loop(0, rows // small, back_one, 0)
    if inside:
        all_late.start(late[...])
        all_early.middle()
        sum_g.finish(attn_owned)
        attn_squares = col_sum(attn_owned[...] * attn_owned[...])
        owned_squares = sum(attn_squares[:, i * LANES : (i + 1) * LANES] for i in range(slab_a // LANES))
        owned_squares += sum(ffn_squares[:, i * LANES : (i + 1) * LANES] for i in range(slab_f // LANES))
        squares[0:1, :] = owned_squares
        all_squares.start(squares[...])
        all_late.middle()
        whole_early = all_early.end()
        all_squares.middle()
        whole_late = all_late.end()
        vec_out[0:4, :] = whole_late[0:4]
        vec_out[4:8, :] = whole_early[0:4]
        vec_out[8:9, :] = whole_late[4:5]
        vec_out[9:13, :] = whole_early[4:8]
        vec_square = col_sum(vec_out[...] * vec_out[...])

    sum_o.wait()
    for k in range(per_f):
        at = slice(k * slab_f, (k + 1) * slab_f)
        total = out_part(s, k) + resid[:, at] + in_x2[k].astype(F32) + in_y2[k].astype(F32) + vec[7:8, at]
        out[:, at] = total.astype(BF16)

    if inside:
        whole_squares = all_squares.end()
        total = jnp.sum(whole_squares[0:1], axis=1, keepdims=True) + jnp.sum(vec_square, axis=1, keepdims=True)
        norm_out[...] = jnp.broadcast_to(jnp.sqrt(total), norm_out.shape)
        line_a.sent()
        line_f.sent()
        sum_f.sent()
        sum_g.sent()
        all_early.sent()
        all_late.sent()
        all_squares.sent()

    wp_in.sent()
    for copy in wp_cross:
        copy.wait_send()
    cot_in.sent()

    for i, r in enumerate((3, 1, 2)):
        cp(gsend.at[r], gm.at[s], 39 + i, peer(r)).wait_send()
    ga_in.sent()
    sum_a.sent()
    sum_o.sent()


def run_layer(frames, segments, spans, cot, vec, attn_src, ffn_src, inside, chips):
    rows, width = frames.shape
    group = 4 * rows
    local = width // 4
    slab_count = 2 * chips if inside else SLABS
    hidden = ffn_src.shape[0] if inside else ffn_src.shape[1]
    attn_shape = (slab_count, local, attn_src.shape[-1])
    ffn_shape = (slab_count, hidden, ffn_src.shape[-1])
    vmem = pl.BlockSpec(memory_space=pltpu.VMEM)
    anywhere = pl.BlockSpec(memory_space=pl.ANY)
    source = anywhere if inside else vmem
    block = (4, rows, width)
    sums = (8, width)
    scratch = [
        pltpu.VMEM(block, BF16),
        pltpu.VMEM(block, BF16),
        pltpu.VMEM(block, BF16),
        pltpu.VMEM((4, local, width), BF16),
        pltpu.VMEM((4, 4, rows, 2 * LANES), BF16),
        pltpu.VMEM((2, group, 2 * LANES), BF16),
        pltpu.VMEM((2, group, LANES), BF16),
        pltpu.VMEM((2, LANES, group), BF16),
        pltpu.VMEM((4, 4, rows, local), BF16),
        pltpu.VMEM(block, BF16),
        pltpu.VMEM((4, rows, hidden), BF16),
        pltpu.VMEM((rows, width), F32),
        pltpu.VMEM((rows, width), F32),
        pltpu.VMEM((3, 4, rows, local), BF16),
        pltpu.VMEM((4, rows, local), BF16),
        pltpu.VMEM((4, rows, local), BF16),
        pltpu.VMEM((4, rows // 2, local), BF16),
        pltpu.VMEM((4, rows // 2, local), BF16),
        pltpu.VMEM((4, rows, local), BF16),
        pltpu.VMEM((4, rows, local), BF16),
        pltpu.VMEM((4, rows // 2, local), BF16),
        pltpu.VMEM((4, rows // 2, local), BF16),
        pltpu.VMEM((4, rows, local), BF16),
        pltpu.VMEM((4, rows, local), BF16),
        pltpu.VMEM((4, 4, rows, LANES), BF16),
        pltpu.VMEM(block, BF16),
        pltpu.VMEM((rows, width), F32),
        pltpu.VMEM((3, 4, rows, local), BF16),
        pltpu.VMEM((group, LANES), F32),
        pltpu.VMEM((group, LANES), F32),
        pltpu.VMEM((group, 1), F32),
        pltpu.VMEM((group, LANES), BF16),
        pltpu.VMEM((group, LANES), BF16),
    ]
    sem_count = 106 + 9 * chips if inside else 60
    scratch += [pltpu.SemaphoreType.DMA((sem_count,)), pltpu.SemaphoreType.DMA((sem_count,))]
    scratch.append(pltpu.SemaphoreType.DMA((4,)))
    if inside:
        scratch += [
            pltpu.VMEM(attn_shape, BF16),
            pltpu.VMEM(ffn_shape, BF16),
            pltpu.VMEM(attn_shape, BF16),
            pltpu.VMEM(ffn_shape, BF16),
            pltpu.VMEM((chips, *attn_shape[1:]), BF16),
            pltpu.VMEM((chips, *ffn_shape[1:]), BF16),
            pltpu.VMEM((chips, *attn_shape[1:]), BF16),
            pltpu.VMEM((chips, *ffn_shape[1:]), BF16),
            pltpu.VMEM(sums, F32),
            pltpu.VMEM(sums, F32),
            pltpu.VMEM((8, LANES), F32),
            pltpu.VMEM((2, 8, *sums), F32),
            pltpu.VMEM((2, chips, *sums), F32),
            pltpu.VMEM((8, 8, LANES), F32),
            pltpu.VMEM((chips, 8, LANES), F32),
        ]
        last = (
            jax.ShapeDtypeStruct(vec.shape, F32),
            jax.ShapeDtypeStruct((8, LANES), F32),
            jax.ShapeDtypeStruct(attn_shape[1:], F32),
            jax.ShapeDtypeStruct(ffn_shape[1:], F32),
        )
    else:
        last = (
            jax.ShapeDtypeStruct(sums, F32),
            jax.ShapeDtypeStruct(sums, F32),
            jax.ShapeDtypeStruct(attn_shape, BF16),
            jax.ShapeDtypeStruct(ffn_shape, BF16),
        )
    return pl.pallas_call(
        functools.partial(layer_kernel, inside, chips),
        out_shape=(jax.ShapeDtypeStruct((rows, width), BF16), jax.ShapeDtypeStruct((rows, width), F32), *last),
        in_specs=[vmem, vmem, vmem, anywhere, vmem, source, source],
        out_specs=(vmem,) * 6,
        scratch_shapes=scratch,
        compiler_params=pltpu.CompilerParams(
            collective_id=0, has_side_effects=True, vmem_limit_bytes=VMEM_LIMIT
        ),
    )(frames, segments, spans, cot, vec, attn_src, ffn_src)


def adam_kernel(norm, *refs):
    clip = jnp.minimum(1.0, MAX_NORM / (norm[0, 0] + 1e-06))
    attn, ffn, vec = refs[0:4], refs[4:8], refs[8:12]
    passed, refs = refs[12:14], refs[14:]
    attn_to, ffn_to, vec_to, norm_to, passed_to = refs[0:4], refs[4:8], refs[8:11], refs[11], refs[12:14]
    for source, target in zip(passed, passed_to):
        target[...] = source[...]

    def update(source, target, rate, decay):
        master, first, second, grad = (ref[...] for ref in source)
        for ref, value in zip(target, adam_step(master, first, second, grad * clip, rate, decay)):
            ref[...] = value
        if len(target) > 3:
            target[3][...] = target[0][...].astype(BF16)

    update(attn, attn_to, RATE_ATTN, DECAY_RATE)
    update(ffn, ffn_to, RATE_FFN, DECAY_RATE)

    @pl.when(pl.program_id(0) == 0)
    def _():
        update(vec, vec_to, RATE_VEC, 0.0)
        norm_to[0, 0] = norm[0, 0]


def run_adam(norm, attn, ffn, vec, passed):
    steps = 2

    def split(array):
        return pl.BlockSpec((array.shape[0] // steps, array.shape[1]), lambda i: (i, 0))

    whole = pl.BlockSpec(vec[0].shape, lambda i: (0, 0))
    scalar = pl.BlockSpec(memory_space=pltpu.SMEM)

    def shapes(array, copy):
        types = (F32, F32, F32, BF16) if copy else (F32, F32, F32)
        return tuple(jax.ShapeDtypeStruct(array.shape, t) for t in types)

    return pl.pallas_call(
        adam_kernel,
        grid=(steps,),
        out_shape=(
            *shapes(attn[0], True),
            *shapes(ffn[0], True),
            *shapes(vec[0], False),
            jax.ShapeDtypeStruct((1, 1), F32),
            *[jax.ShapeDtypeStruct(array.shape, array.dtype) for array in passed],
        ),
        in_specs=[scalar] + [split(attn[0])] * 4 + [split(ffn[0])] * 4 + [whole] * 4 + [split(array) for array in passed],
        out_specs=(*[split(attn[0])] * 4, *[split(ffn[0])] * 4, *[whole] * 3, scalar, *[split(array) for array in passed]),
        compiler_params=pltpu.CompilerParams(vmem_limit_bytes=VMEM_LIMIT),
    )(norm, *attn, *ffn, *vec, *passed)


def per_device(
    frames,
    segment_ids,
    span_starts,
    cotangent,
    attn_master,
    attn_first,
    attn_second,
    ffn_master,
    ffn_first,
    ffn_second,
    vec_master,
    vec_first,
    vec_second,
):
    dp_count = lax.axis_size("dp")

    def gather_slabs(master):
        shard = master.astype(BF16)
        whole = lax.all_gather(shard, "dp", axis=1, tiled=True)
        return whole.reshape(shard.shape[0], SLABS, -1).transpose(1, 0, 2)

    inside = attn_master.shape[1] % 256 == 0 and ffn_master.shape[1] % 256 == 0 and dp_count in (4, 8)
    head = (frames[0], segment_ids, span_starts, cotangent[0], vec_master)
    if inside:
        output, frames_grad, vec_grad, norm, attn_owned, ffn_owned = run_layer(
            *head, attn_master, ffn_master, True, dp_count // 2
        )
    else:
        output, frames_grad, early, late, g_attn, g_ffn = run_layer(
            *head, gather_slabs(attn_master), gather_slabs(ffn_master), False, dp_count // 2
        )
        vec_local = jnp.concatenate([late[0:4], early[0:4], late[4:5], early[4:8]], axis=0)

        def scatter_slabs(slabs):
            whole = slabs.astype(F32).transpose(1, 0, 2).reshape(slabs.shape[1], -1)
            return lax.psum_scatter(whole, "dp", scatter_dimension=1, tiled=True)

        attn_owned = scatter_slabs(g_attn)
        ffn_owned = scatter_slabs(g_ffn)
        owned_squares = jnp.sum(attn_owned * attn_owned) + jnp.sum(ffn_owned * ffn_owned)
        vec_grad, total_squares = lax.psum((vec_local, owned_squares), ("seq", "dp"))
        norm = jnp.broadcast_to(jnp.sqrt(total_squares + jnp.sum(vec_grad * vec_grad)), (8, LANES))
    updated = run_adam(
        norm,
        (attn_master, attn_first, attn_second, attn_owned),
        (ffn_master, ffn_first, ffn_second, ffn_owned),
        (vec_master, vec_first, vec_second, vec_grad),
        (output, frames_grad),
    )
    return (updated[-2][None], updated[-1][None], updated[-3].reshape(()), *updated[:-3])


def solution(mesh):
    return jax.shard_map(
        per_device,
        mesh=mesh,
        in_specs=(
            P("dp", "seq", None),
            P("dp", None),
            P("dp", None),
            P("dp", "seq", None),
            P("seq", "dp"),
            P("seq", "dp"),
            P("seq", "dp"),
            P("seq", "dp"),
            P("seq", "dp"),
            P("seq", "dp"),
            P(),
            P(),
            P(),
        ),
        out_specs=(
            P("dp", "seq", None),
            P("dp", "seq", None),
            P(),
            P("seq", "dp"),
            P("seq", "dp"),
            P("seq", "dp"),
            P("seq", "dp"),
            P("seq", "dp"),
            P("seq", "dp"),
            P("seq", "dp"),
            P("seq", "dp"),
            P(),
            P(),
            P(),
        ),
        check_vma=False,
    )
```
